256 devices in a mesh: outer: 8 (over z), inner: 32 (over x, y, core).
Axes of the slice: x: 4, y: 4, z: 8, core: 2. Of those that a mesh axis runs over, the one named last changes fastest.
Arguments:
- b_leaf: float32 [65536, 64], P(('outer', 'inner')), may hold values from -6 to 6
- b_sep: float32 [2048, 64], P(('outer', 'inner')), may hold values from -6 to 6
- b_root: float32 [2048, 64], P(('outer', 'inner')), may hold values from -6 to 6
- leaf_linv: float32 [65536, 256], P(('outer', 'inner')), as said below
- leaf_uinv: float32 [65536, 256], P(('outer', 'inner')), as said below
- leaf_lower: float32 [65536, 256], P(('outer', 'inner')), as said below
- leaf_upper: float32 [65536, 256], P(('outer', 'inner')), as said below
- sep_rows: int32 [256, 256], P(('outer', 'inner')), may hold values from 0 to 255, as said below
- sep_linv: float32 [2048, 256], P(('outer', 'inner')), as said below
- sep_uinv: float32 [2048, 256], P(('outer', 'inner')), as said below
- sep_lower: float32 [2048, 2048], P(None, ('outer', 'inner')), as said below
- sep_upper: float32 [2048, 2048], P(('outer', 'inner')), as said below
- root_linv: float32 [2048, 2048], P(('outer', 'inner')), as said below
- root_uinv: float32 [2048, 2048], P(('outer', 'inner')), as said below
- basis_leaf: float32 [65536, 512], P(('outer', 'inner')), as said below
- basis_sep: float32 [2048, 512], P(('outer', 'inner')), as said below
- basis_root: float32 [2048, 512], P(('outer', 'inner')), as said below
- g_blocks: float32 [262144, 128], P(('outer', 'inner')), may hold values from -0.25 to 0.25
- c_blocks: float32 [262144, 128], P(('outer', 'inner')), may hold values from -0.25 to 0.25
- block_cols: int32 [512, 4], P(('outer', 'inner')), may hold values from 0 to 1
Outputs:
- v_leaf: float32 [65536, 64], P(('outer', 'inner'))
- v_sep: float32 [2048, 64], P(('outer', 'inner'))
- v_root: float32 [2048, 64], P(('outer', 'inner'))
- coefficients: float32 [512, 64], replicated
- reduced_g: float32 [64, 64], replicated
- reduced_c: float32 [64, 64], replicated
The draws below stay inside these ranges and needn't reach their ends.
Inputs may be any that keep to these rules, and one draw needn't show every extreme that they name: `sep_rows`: each row holds 256 distinct numbers; every row names 0 and 255. `leaf_linv`: lower triangular in each diagonal block of the stack, nonzero diagonal. `leaf_uinv`: upper triangular in each diagonal block of the stack, nonzero diagonal. `sep_linv`: lower triangular in each block of 256 rows, nonzero diagonal. `sep_uinv`: upper triangular in each block of 256 rows, nonzero diagonal. `root_linv`: lower triangular, nonzero diagonal. `root_uinv`: upper triangular, nonzero diagonal. `leaf_lower`: entries of order one over the square root of 256. `leaf_upper`: entries of order one over the square root of 256. `sep_lower`: entries of order one over the square root of the number of its columns. `sep_upper`: entries of order one over the square root of 2048. basis_leaf, basis_sep and basis_root stacked by rows form Q with Q^T Q = 69632 I up to float32 rounding. `basis_sep`: part of the stacked Q described with basis_leaf. `basis_root`: part of the stacked Q described with basis_leaf.
All inputs are finite; a program needn't handle non-finite values.
Results may differ from the reference program's by a relative error of at most 0.0003.
Values sent between devices are 32-bit elements; how exact they have to be, the bound alone decides.
A program may use at most 64 MiB of HBM per device.

```python
import math
import jax
import jax.numpy as jnp
from jax import lax

P_SIZE = 64
BASIS = 512
NL = 256
SO_DEV = 8
SR_DEV = 8
KR = 256
BLK = 128
WID = 4
SO = 256
SR = 2048
NBR = 2
N_OUTER = 8
N_INNER = 32
DEVICES = 256


def triangle_stack(key, stack_count, extent, is_lower):
    key_off, key_diag = jax.random.split(key)
    off_diag = jax.random.normal(key_off, (stack_count, extent, extent)) * 0.7 / math.sqrt(extent)
    diagonal_vals = jax.random.uniform(key_diag, (stack_count, extent), minval=0.5, maxval=1.5)
    row_ids = jnp.arange(extent)[:, None]
    col_ids = jnp.arange(extent)[None, :]
    if is_lower:
        keep = row_ids > col_ids
    else:
        keep = row_ids < col_ids
    matrix = jnp.where(keep[None], off_diag, 0.0) + diagonal_vals[:, :, None] * (row_ids == col_ids)[None].astype(jnp.float32)
    return matrix.reshape(stack_count * extent, extent).astype(jnp.float32)


def dense_draw(key, row_total, col_total, fan_in):
    values = jnp.clip(jax.random.normal(key, (row_total, col_total)), -6.0, 6.0)
    return (values / math.sqrt(fan_in)).astype(jnp.float32)


def draw_leaf_linv(key, part):
    return triangle_stack(jax.random.fold_in(key, 11), DEVICES, NL, True)


def draw_leaf_uinv(key, part):
    return triangle_stack(jax.random.fold_in(key, 12), DEVICES, NL, False)


def draw_sep_linv(key, part):
    return triangle_stack(jax.random.fold_in(key, 13), N_OUTER, SO, True)


def draw_sep_uinv(key, part):
    return triangle_stack(jax.random.fold_in(key, 14), N_OUTER, SO, False)


def draw_root_linv(key, part):
    return triangle_stack(jax.random.fold_in(key, 15), 1, SR, True)


def draw_root_uinv(key, part):
    return triangle_stack(jax.random.fold_in(key, 16), 1, SR, False)


def draw_sep_rows(key, part):
    row_keys = jax.random.split(jax.random.fold_in(key, 17), DEVICES)

    def draw_row(row_key):
        shuffled = jax.random.permutation(row_key, SO - 2)[:KR - 2].astype(jnp.int32) + 1
        return jnp.concatenate([jnp.zeros((1,), jnp.int32), shuffled, jnp.full((1,), SO - 1, jnp.int32)])
    return jax.vmap(draw_row)(row_keys)


def draw_b_leaf(key, part):
    return dense_draw(jax.random.fold_in(key, 18), DEVICES * NL, P_SIZE, 1)


def draw_b_sep(key, part):
    return dense_draw(jax.random.fold_in(key, 19), N_OUTER * SO, P_SIZE, 1)


def draw_b_root(key, part):
    return dense_draw(jax.random.fold_in(key, 20), SR, P_SIZE, 1)


def draw_leaf_lower(key, part):
    return dense_draw(jax.random.fold_in(key, 21), DEVICES * KR, NL, NL)


def draw_leaf_upper(key, part):
    return dense_draw(jax.random.fold_in(key, 22), DEVICES * NL, KR, KR)


def draw_sep_upper(key, part):
    return dense_draw(jax.random.fold_in(key, 23), N_OUTER * SO, SR, SR)


def draw_sep_lower(key, part):
    base_key = jax.random.fold_in(key, 24)
    values = dense_draw(base_key, SR, N_OUTER * SO, N_OUTER * SO)
    pairing = jax.random.permutation(jax.random.fold_in(base_key, 1), DEVICES).astype(jnp.int32)
    row_block = jnp.arange(SR, dtype=jnp.int32) // SR_DEV
    col_block = jnp.arange(N_OUTER * SO, dtype=jnp.int32) // SO_DEV
    paired = pairing[col_block][None, :] == row_block[:, None]
    return jnp.where(paired, 6.0 * values, values).astype(jnp.float32)


def solve_ports(key, part):
    highest = lax.Precision.HIGHEST
    b_leaf = draw_b_leaf(key, part)
    b_sep = draw_b_sep(key, part)
    b_root = draw_b_root(key, part)
    leaf_linv = draw_leaf_linv(key, part)
    leaf_uinv = draw_leaf_uinv(key, part)
    leaf_lower = draw_leaf_lower(key, part)
    leaf_upper = draw_leaf_upper(key, part)
    sep_rows = draw_sep_rows(key, part)
    sep_linv = draw_sep_linv(key, part)
    sep_uinv = draw_sep_uinv(key, part)
    sep_lower = draw_sep_lower(key, part)
    sep_upper = draw_sep_upper(key, part)
    root_linv = draw_root_linv(key, part)
    root_uinv = draw_root_uinv(key, part)
    y_leaf = jnp.einsum('dij,djp->dip', leaf_linv.reshape(DEVICES, NL, NL), b_leaf.reshape(DEVICES, NL, P_SIZE), precision=highest)
    contrib = jnp.einsum('dkj,djp->dkp', leaf_lower.reshape(DEVICES, KR, NL), y_leaf, precision=highest)
    group_of = (jnp.arange(DEVICES, dtype=jnp.int32) // N_INNER)[:, None]
    target = (group_of * SO + sep_rows).reshape(-1).astype(jnp.int32)
    t_sep = jax.ops.segment_sum(contrib.reshape(DEVICES * KR, P_SIZE), target, num_segments=N_OUTER * SO)
    r_sep = (b_sep - t_sep).reshape(N_OUTER, SO, P_SIZE)
    y_sep = jnp.einsum('gij,gjp->gip', sep_linv.reshape(N_OUTER, SO, SO), r_sep, precision=highest).reshape(N_OUTER * SO, P_SIZE)
    y_root = jnp.dot(root_linv, b_root - jnp.dot(sep_lower, y_sep, precision=highest), precision=highest)
    x_root = jnp.dot(root_uinv, y_root, precision=highest)
    z_sep = (y_sep - jnp.dot(sep_upper, x_root, precision=highest)).reshape(N_OUTER, SO, P_SIZE)
    x_sep = jnp.einsum('gij,gjp->gip', sep_uinv.reshape(N_OUTER, SO, SO), z_sep, precision=highest)
    coupled = x_sep[group_of, sep_rows]
    z_leaf = y_leaf - jnp.einsum('dik,dkp->dip', leaf_upper.reshape(DEVICES, NL, KR), coupled, precision=highest)
    x_leaf = jnp.einsum('dij,djp->dip', leaf_uinv.reshape(DEVICES, NL, NL), z_leaf, precision=highest).reshape(DEVICES * NL, P_SIZE)
    return jnp.concatenate([x_leaf, x_sep.reshape(N_OUTER * SO, P_SIZE), x_root], axis=0)


def orthonormal_basis(key, part):
    highest = lax.Precision.HIGHEST
    stacked = solve_ports(key, part)
    spread = jnp.sqrt(jnp.mean(stacked * stacked))
    key_noise, key_mix = jax.random.split(jax.random.fold_in(key, 30))
    total_rows = DEVICES * (NL + SO_DEV + SR_DEV)
    noise = jax.random.normal(key_noise, (total_rows, BASIS))
    mixing = jax.random.normal(key_mix, (P_SIZE, BASIS)) * (3.3 / math.sqrt(BASIS))
    raw = noise + jnp.dot(stacked / spread, mixing, precision=highest)
    for sweep in range(2):
        gram_now = jnp.dot(raw.T, raw, precision=highest)
        lower_now = jnp.linalg.cholesky(gram_now)
        raw = lax.linalg.triangular_solve(lower_now, raw, left_side=False, lower=True, transpose_a=True)
    return (raw * math.sqrt(total_rows)).astype(jnp.float32)


def draw_basis_leaf(key, part):
    return orthonormal_basis(key, part)[:DEVICES * NL]


def draw_basis_sep(key, part):
    return orthonormal_basis(key, part)[DEVICES * NL:DEVICES * NL + N_OUTER * SO]


def draw_basis_root(key, part):
    return orthonormal_basis(key, part)[DEVICES * NL + N_OUTER * SO:]


def with_ends(values, key, low, largest):
    longest = values.shape.index(max(values.shape))
    spots = []
    for shift in (0, 1):
        where = [jax.random.randint(jax.random.fold_in(key, axis), (), 0, length) for axis, length in enumerate(values.shape)]
        where[longest] = (where[longest] + shift) % values.shape[longest]
        spots.append(tuple(where))
    return values.at[spots[0]].set(low).at[spots[1]].set(largest)


def level_of(key, shape, pieces, least, largest):
    gain, own = 1.0, jax.random.fold_in(key, 6)
    for position, blocks in pieces:
        heights = jnp.exp(jax.random.uniform(jax.random.fold_in(own, position), (blocks,), jnp.float32, least / len(pieces), largest / len(pieces)))
        gain = gain * jnp.repeat(heights, shape[position] // blocks).reshape([-1 if axis == position else 1 for axis in range(len(shape))])
    return gain


def normal_values(key, dims, deviation, bound, shards=(), kind=jnp.bfloat16):
    factor_of = level_of(key, dims, shards, -0.22, 0.18) if shards else 1.0
    entries = jax.random.normal(key, dims, jnp.float32) * deviation * factor_of
    return jnp.minimum(jnp.maximum(entries, -bound), bound).astype(kind)


def setup_inputs(seed: int = 0) -> dict:
    key_of = jax.random.split(jax.random.key(seed), 21)
    b_leaf = draw_b_leaf(jax.random.fold_in(key_of[20], 71), 0)
    b_sep = draw_b_sep(jax.random.fold_in(key_of[20], 71), 0)
    b_root = draw_b_root(jax.random.fold_in(key_of[20], 71), 0)
    leaf_linv = draw_leaf_linv(jax.random.fold_in(key_of[20], 71), 0)
    leaf_uinv = draw_leaf_uinv(jax.random.fold_in(key_of[20], 71), 0)
    leaf_lower = draw_leaf_lower(jax.random.fold_in(key_of[20], 71), 0)
    leaf_upper = draw_leaf_upper(jax.random.fold_in(key_of[20], 71), 0)
    sep_rows = draw_sep_rows(jax.random.fold_in(key_of[20], 71), 0)
    sep_linv = draw_sep_linv(jax.random.fold_in(key_of[20], 71), 0)
    sep_uinv = draw_sep_uinv(jax.random.fold_in(key_of[20], 71), 0)
    sep_lower = draw_sep_lower(jax.random.fold_in(key_of[20], 71), 0)
    sep_upper = draw_sep_upper(jax.random.fold_in(key_of[20], 71), 0)
    root_linv = draw_root_linv(jax.random.fold_in(key_of[20], 71), 0)
    root_uinv = draw_root_uinv(jax.random.fold_in(key_of[20], 71), 0)
    basis_leaf = draw_basis_leaf(jax.random.fold_in(key_of[20], 71), 0)
    basis_sep = draw_basis_sep(jax.random.fold_in(key_of[20], 71), 0)
    basis_root = draw_basis_root(jax.random.fold_in(key_of[20], 71), 0)
    g_blocks = normal_values(key_of[17], (DEVICES * NL * WID, BLK), (BLK * WID) ** -0.5, 0.25, ((0, 256),), jnp.float32)
    c_blocks = normal_values(key_of[18], (DEVICES * NL * WID, BLK), (BLK * WID) ** -0.5, 0.25, ((0, 256),), jnp.float32)
    block_cols = with_ends(jax.random.randint(key_of[19], (DEVICES * NBR, WID), 0, NBR), jax.random.fold_in(key_of[19], 1), 0, NBR - 1).astype(jnp.int32)
    return dict(b_leaf=b_leaf, b_sep=b_sep, b_root=b_root, leaf_linv=leaf_linv, leaf_uinv=leaf_uinv, leaf_lower=leaf_lower, leaf_upper=leaf_upper, sep_rows=sep_rows, sep_linv=sep_linv, sep_uinv=sep_uinv, sep_lower=sep_lower, sep_upper=sep_upper, root_linv=root_linv, root_uinv=root_uinv, basis_leaf=basis_leaf, basis_sep=basis_sep, basis_root=basis_root, g_blocks=g_blocks, c_blocks=c_blocks, block_cols=block_cols)


def product_exact(left, right):
    return jnp.dot(left.astype(jnp.float32), right.astype(jnp.float32), precision=lax.Precision.HIGHEST, preferred_element_type=jnp.float32)

def reference(b_leaf, b_sep, b_root, leaf_linv, leaf_uinv, leaf_lower, leaf_upper, sep_rows, sep_linv, sep_uinv, sep_lower, sep_upper, root_linv, root_uinv, basis_leaf, basis_sep, basis_root, g_blocks, c_blocks, block_cols):
    highest = lax.Precision.HIGHEST
    devices_all = N_OUTER * N_INNER
    y_leaf = jnp.einsum('dij,djp->dip', leaf_linv.reshape(devices_all, NL, NL), b_leaf.reshape(devices_all, NL, P_SIZE), precision=highest)
    contrib = jnp.einsum('dkj,djp->dkp', leaf_lower.reshape(devices_all, KR, NL), y_leaf, precision=highest)
    group_of = (jnp.arange(devices_all, dtype=jnp.int32) // N_INNER)[:, None]
    target = (group_of * SO + sep_rows).reshape(-1).astype(jnp.int32)
    t_sep = jax.ops.segment_sum(contrib.reshape(devices_all * KR, P_SIZE), target, num_segments=N_OUTER * SO)
    r_sep = (b_sep - t_sep).reshape(N_OUTER, SO, P_SIZE)
    y_sep = jnp.einsum('gij,gjp->gip', sep_linv.reshape(N_OUTER, SO, SO), r_sep, precision=highest).reshape(N_OUTER * SO, P_SIZE)
    y_root = product_exact(root_linv, b_root - product_exact(sep_lower, y_sep))
    x_root = product_exact(root_uinv, y_root)
    z_sep = (y_sep - product_exact(sep_upper, x_root)).reshape(N_OUTER, SO, P_SIZE)
    x_sep = jnp.einsum('gij,gjp->gip', sep_uinv.reshape(N_OUTER, SO, SO), z_sep, precision=highest)
    coupled = x_sep[group_of, sep_rows]
    z_leaf = y_leaf - jnp.einsum('dik,dkp->dip', leaf_upper.reshape(devices_all, NL, KR), coupled, precision=highest)
    x_leaf = jnp.einsum('dij,djp->dip', leaf_uinv.reshape(devices_all, NL, NL), z_leaf, precision=highest).reshape(devices_all * NL, P_SIZE)
    x_sep = x_sep.reshape(N_OUTER * SO, P_SIZE)
    node_count = float(devices_all * (NL + SO_DEV + SR_DEV))
    pieces_x = (x_leaf, x_sep, x_root)
    pieces_q = (basis_leaf, basis_sep, basis_root)
    projected = sum((product_exact(basis.T, values) for basis, values in zip(pieces_q, pieces_x)))
    coefficients = projected / node_count
    cleaned = [values - product_exact(basis, coefficients) for basis, values in zip(pieces_q, pieces_x)]
    gram_matrix = sum((product_exact(piece_now.T, piece_now) for piece_now in cleaned)) / node_count
    chol_lower = jnp.linalg.cholesky(gram_matrix)
    inverse_lower = lax.linalg.triangular_solve(chol_lower, jnp.eye(P_SIZE, dtype=jnp.float32), left_side=True, lower=True)
    v_leaf = product_exact(cleaned[0], inverse_lower.T)
    v_sep = product_exact(cleaned[1], inverse_lower.T)
    v_root = product_exact(cleaned[2], inverse_lower.T)
    blocked = v_leaf.reshape(devices_all, NBR, BLK, P_SIZE)
    device_ids = jnp.arange(devices_all, dtype=jnp.int32)[:, None, None]
    picked = blocked[device_ids, block_cols.reshape(devices_all, NBR, WID)]
    g_image = jnp.einsum('drwij,drwjp->drip', g_blocks.reshape(devices_all, NBR, WID, BLK, BLK), picked, precision=highest)
    c_image = jnp.einsum('drwij,drwjp->drip', c_blocks.reshape(devices_all, NBR, WID, BLK, BLK), picked, precision=highest)
    reduced_g = jnp.einsum('drip,driq->pq', blocked, g_image, precision=highest) / node_count
    reduced_c = jnp.einsum('drip,driq->pq', blocked, c_image, precision=highest) / node_count
    return (v_leaf, v_sep, v_root, coefficients, reduced_g, reduced_c)
```

```python
import functools

import jax
import jax.numpy as jnp
from jax import lax
from jax.experimental import pallas as pl
from jax.experimental.pallas import tpu as pltpu
from jax.sharding import PartitionSpec as P

MESH = pl.DeviceIdType.MESH
F32 = jnp.float32
NN = ((1,), (0,))
NT = ((1,), (1,))
TN = ((0,), (0,))
PIECES_P = 32
PIECES_K = 16


def mul(left, right, dims=NN):
    return lax.dot_general(
        left, right, (dims, ((), ())), precision=lax.Precision.HIGHEST, preferred_element_type=F32
    )


def wide(block):
    return jnp.concatenate([block, jnp.zeros_like(block)], axis=1)


def folded(block):
    half = block.shape[0] // 2
    return jnp.concatenate([block[:half], block[half:]], axis=1)


def unfolded_product(left, both):
    half = left.shape[1] // 2
    upper = mul(left[:, :half], both)
    lower = mul(left[:, half:], both)
    return upper[:, :64] + lower[:, 64:]


def inverse_factor(gram):
    row_ids = lax.broadcasted_iota(jnp.int32, (64, 64), 0)
    col_ids = lax.broadcasted_iota(jnp.int32, (64, 64), 1)
    start = jnp.concatenate([gram, (row_ids == col_ids).astype(F32)], axis=1)
    groups = tuple(start[8 * a : 8 * a + 8] for a in range(8))
    sub = lax.broadcasted_iota(jnp.int32, (8, 128), 0)

    def panel(p, groups):
        groups = list(groups)
        scale = jnp.zeros((8, 128), F32)
        for k in range(8):
            row = groups[0][k : k + 1, :]
            pivot = row[:, k : k + 1]
            scaled = row / pivot
            for a in range(8):
                factor = groups[a][:, k : k + 1]
                if a == 0:
                    factor = jnp.where(sub > k, jnp.broadcast_to(factor, (8, 128)), 0.0)
                else:
                    live = jnp.where(a + p < 8, 1.0, 0.0).astype(F32)
                    factor = jnp.broadcast_to(factor, (8, 128)) * live
                groups[a] = groups[a] - factor * scaled
            scale = jnp.where(sub == k, jnp.broadcast_to(lax.rsqrt(pivot), (8, 128)), scale)
        groups[0] = groups[0] * scale
        turned = [pltpu.roll(x, 120, 1) for x in groups]
        return tuple(turned[1:] + turned[:1])

    groups = lax.fori_loop(0, 8, panel, groups)
    return jnp.concatenate(groups, axis=0)[:, :64]


def by_owner(columns, n_outer, n_inner, out_ref):
    if n_inner * 8 != 256:
        moved = columns.reshape(8, n_outer, n_inner, 8).transpose(2, 0, 1, 3).reshape(n_inner, 8, n_outer * 8)
        out_ref[...] = jnp.concatenate(
            [moved, jnp.zeros((n_inner, 8, 128 - n_outer * 8), F32)], axis=2
        )
        return
    lane_group = lax.broadcasted_iota(jnp.int32, (8, 128), 1) // 8
    for m in range(2):
        shifted = []
        for o in range(n_outer):
            at = o * 256 + m * 128
            piece = columns[:, at : at + 128]
            shifted.append(pltpu.roll(piece, o * 8, 1) if o else piece)
        for ii in range(16):
            total = shifted[0]
            for o in range(1, n_outer):
                total = jnp.where(lane_group == (ii + o) % 16, shifted[o], total)
            out_ref[16 * m + ii] = pltpu.roll(total, 128 - ii * 8, 1) if ii else total


def kernel(
    n_outer,
    n_inner,
    b_t,
    b_sep,
    b_root,
    leaf_linv,
    leaf_uinv,
    leaf_lower,
    leaf_upper,
    sep_rows,
    sep_linv,
    sep_uinv,
    sep_lower_t,
    sep_upper,
    root_linv,
    root_uinv,
    basis_leaf,
    basis_sep,
    basis_root,
    g_blocks,
    c_blocks,
    block_cols,
    v_leaf_t,
    v_sep,
    v_root,
    coef_t,
    red_g,
    red_c,
    a_src,
    a_rcv,
    b_buf,
    sl_buf,
    su_buf,
    sp_src,
    sp_buf,
    l_buf,
    u_buf,
    rz_buf,
    d_buf,
    e_buf,
    f_buf,
    z_buf,
    p_src,
    p_rcv,
    pz_buf,
    pc_buf,
    k_src,
    k_rcv,
    kz_buf,
    kc_buf,
    q_all,
    hg,
    hc,
    send,
    recv,
):
    g = lax.axis_index("outer")
    i = lax.axis_index("inner")
    rb = n_outer * 8
    n_own = kc_buf.shape[0]
    stride = n_inner // n_own
    nodes = float(n_outer * n_inner * (basis_leaf.shape[0] + 16))
    A, B, SL, SU, SP, L, U, RZ, D, E_, F_, Z, PR, PZ, PC, KR, KZ, KC = range(18)

    def to_plane(phase, src, dst):
        def one(k, carry):
            peer = lax.rem(i + k, n_inner)
            pltpu.make_async_remote_copy(
                src_ref=src(peer, k),
                dst_ref=dst(peer, k),
                send_sem=send.at[phase],
                recv_sem=recv.at[phase],
                device_id=(g, peer),
                device_id_type=MESH,
            ).start()
            return carry

        lax.fori_loop(1, n_inner, one, 0)

    def to_column(phase, src, dst):
        def one(k, carry):
            peer = lax.rem(g + k, n_outer)
            pltpu.make_async_remote_copy(
                src_ref=src,
                dst_ref=dst,
                send_sem=send.at[phase],
                recv_sem=recv.at[phase],
                device_id=(peer, i),
                device_id_type=MESH,
            ).start()
            return carry

        lax.fori_loop(1, n_outer, one, 0)

    def arrived(phase, like):
        pltpu.make_async_copy(like, like, recv.at[phase]).wait()

    def sent(phase, like):
        pltpu.make_async_copy(like, like, send.at[phase]).wait()

    others = pl.ds(0, n_inner - 1)
    others_z = pl.ds(0, n_outer - 1)

    barrier = pltpu.get_barrier_semaphore()

    def greet_plane(k, carry):
        pl.semaphore_signal(
            barrier, inc=1, device_id=(g, lax.rem(i + k, n_inner)), device_id_type=MESH
        )
        return carry

    def greet_column(k, carry):
        pl.semaphore_signal(
            barrier, inc=1, device_id=(lax.rem(g + k, n_outer), i), device_id_type=MESH
        )
        return carry

    lax.fori_loop(1, n_inner, greet_plane, 0)
    lax.fori_loop(1, n_outer, greet_column, 0)

    width = n_inner * 8
    couples = sep_rows.shape[1]
    sel_t = (
        lax.broadcasted_iota(jnp.int32, (width, couples), 0)
        == jnp.broadcast_to(sep_rows[...], (width, couples))
    ).astype(F32)
    y_t = mul(b_t[...], leaf_linv[...], NT)
    contrib_t = mul(y_t, leaf_lower[...], NT)
    update = mul(sel_t, contrib_t, NT)
    a_src[...] = wide(update).reshape(n_inner, 8, 128)
    by_owner(sep_lower_t[...], n_outer, n_inner, sp_src)
    sp_buf[i] = sp_src[i]
    sl_buf[i] = sep_linv[...]
    su_buf[i] = sep_uinv[...]
    l_buf[g] = root_linv[...]
    u_buf[g] = root_uinv[...]

    pl.semaphore_wait(barrier, n_inner + n_outer - 2)

    to_plane(A, lambda peer, k: a_src.at[peer], lambda peer, k: a_rcv.at[k - 1])
    to_plane(SL, lambda peer, k: sep_linv, lambda peer, k: sl_buf.at[i])
    to_plane(SP, lambda peer, k: sp_src.at[peer], lambda peer, k: sp_buf.at[i])
    to_column(L, root_linv, l_buf.at[g])
    to_column(U, root_uinv, u_buf.at[g])

    arrived(A, a_rcv)
    b_buf[i] = wide(b_sep[...]) - (a_src[i] + jnp.sum(a_rcv[...], axis=0))
    to_plane(B, lambda peer, k: b_buf.at[i], lambda peer, k: b_buf.at[i])
    to_plane(SU, lambda peer, k: sep_uinv, lambda peer, k: su_buf.at[i])

    uy_t = mul(y_t, leaf_uinv[...], NT)
    coupling = mul(leaf_uinv[...], mul(leaf_upper[...], sel_t, NT))
    arrived(SL, sl_buf.at[others])
    arrived(SP, sp_buf.at[others])
    to_root = mul(sp_buf[...].reshape(width, 128)[:, :rb], sl_buf[...].reshape(width, width), TN)

    arrived(B, b_buf.at[others])
    rhs_sep = b_buf[...].reshape(width, 128)[:, :64]
    part = mul(to_root, rhs_sep)
    mine = lax.broadcasted_iota(jnp.int32, (rb, 64), 0) // 8 == g
    own = jnp.where(mine, jnp.concatenate([b_root[...]] * n_outer, axis=0), 0.0)
    rz_buf[g] = folded(own - part)
    to_column(RZ, rz_buf.at[g], rz_buf.at[g])
    y_own = mul(sep_linv[...], rhs_sep)
    arrived(RZ, rz_buf.at[others_z])

    def root_gather(phase, buf, block):
        buf[:, i] = block.reshape(n_outer // 2, 8, 128)
        to_plane(phase, lambda peer, k: buf.at[:, i], lambda peer, k: buf.at[:, i])

    def root_value(phase, buf):
        arrived(phase, buf.at[:, others])
        return buf[...].reshape(n_outer // 2 * n_inner * 8, 128)

    root_gather(D, d_buf, jnp.sum(rz_buf[...], axis=0))
    arrived(L, l_buf.at[others_z])
    lower_rows = l_buf[...].reshape(rb, l_buf.shape[2])
    y_root = unfolded_product(lower_rows, root_value(D, d_buf))
    root_gather(E_, e_buf, folded(y_root))

    size = g_blocks.shape[1]
    stored = block_cols.shape[1]
    for r in range(2):
        for c in range(2):
            for blocks, whole in ((g_blocks, hg), (c_blocks, hc)):
                total = jnp.zeros((size, size), F32)
                for w in range(stored):
                    at = (r * stored + w) * size
                    weight = jnp.where(block_cols[r, w] == c, 1.0, 0.0).astype(F32)
                    total = total + weight * blocks[at : at + size, :]
                whole[r * size : (r + 1) * size, c * size : (c + 1) * size] = total
    leaf_count = basis_leaf.shape[0]
    q_all[:leaf_count, :] = basis_leaf[...]
    q_all[leaf_count : leaf_count + 8, :] = basis_sep[...]
    q_all[leaf_count + 8 : leaf_count + 16, :] = basis_root[...]
    arrived(SU, su_buf.at[others])
    from_sep = mul(coupling, su_buf[...].reshape(width, width))

    arrived(U, u_buf.at[others_z])
    upper_rows = u_buf[...].reshape(rb, u_buf.shape[2])
    x_root = unfolded_product(upper_rows, root_value(E_, e_buf))
    root_gather(F_, f_buf, folded(x_root))
    row_ids = lax.broadcasted_iota(jnp.int32, (8, rb), 0)
    col_ids = lax.broadcasted_iota(jnp.int32, (8, rb), 1)
    pick = (col_ids == row_ids + 8 * g).astype(F32)
    x_root_t = mul(x_root, pick, ((0,), (1,)))

    z_own = y_own - unfolded_product(sep_upper[...], root_value(F_, f_buf))
    z_buf[i] = wide(z_own)
    to_plane(Z, lambda peer, k: z_buf.at[i], lambda peer, k: z_buf.at[i])
    arrived(Z, z_buf.at[others])
    z_t = jnp.transpose(z_buf[...].reshape(width, 128))[:64]
    x_leaf_t = uy_t - mul(z_t, from_sep, NT)
    x_sep_t = mul(z_t, sep_uinv[...], NT)
    x_t = jnp.concatenate([x_leaf_t, x_sep_t, x_root_t], axis=1)

    proj_t = mul(x_t, q_all[...])
    per = PIECES_P // n_inner
    for t in range(PIECES_P):
        r, c = t // 4, t % 4
        p_src[t // per, t % per] = proj_t[8 * r : 8 * r + 8, 128 * c : 128 * c + 128]
    to_plane(PR, lambda peer, k: p_src.at[peer], lambda peer, k: p_rcv.at[k - 1])
    arrived(PR, p_rcv)
    pz_buf[g] = p_src[i] + jnp.sum(p_rcv[...], axis=0)
    to_column(PZ, pz_buf.at[g], pz_buf.at[g])
    arrived(PZ, pz_buf.at[others_z])
    pc_buf[i] = jnp.sum(pz_buf[...], axis=0) / nodes
    to_plane(PC, lambda peer, k: pc_buf.at[i], lambda peer, k: pc_buf.at[i])
    arrived(PC, pc_buf.at[others])
    coefs = jnp.concatenate(
        [
            jnp.concatenate(
                [pc_buf[(4 * r + c) // per, (4 * r + c) % per] for c in range(4)], axis=1
            )
            for r in range(8)
        ],
        axis=0,
    )
    coef_t[...] = coefs
    clean_t = x_t - mul(coefs, q_all[...], NT)

    gram_part = mul(clean_t, clean_t, NT)
    clean_leaf_t = clean_t[:, :leaf_count]
    g_part = mul(mul(clean_leaf_t, hg[...]), clean_leaf_t, NT)
    c_part = mul(mul(clean_leaf_t, hc[...]), clean_leaf_t, NT)
    per_k = PIECES_K // n_own
    products = jnp.concatenate(
        [jnp.concatenate([g_part, c_part], axis=1), wide(gram_part)], axis=0
    )
    k_src[...] = products.reshape(n_own, per_k, 8, 128)
    owner = i // stride
    owns = lax.rem(i, stride) == 0

    def to_owner(k, carry):
        peer = lax.rem(i + k, n_inner)

        @pl.when(lax.rem(peer, stride) == 0)
        def _():
            pltpu.make_async_remote_copy(
                src_ref=k_src.at[peer // stride],
                dst_ref=k_rcv.at[k - 1],
                send_sem=send.at[KR],
                recv_sem=recv.at[KR],
                device_id=(g, peer),
                device_id_type=MESH,
            ).start()

        return carry

    lax.fori_loop(1, n_inner, to_owner, 0)

    @pl.when(owns)
    def _():
        arrived(KR, k_rcv)
        kz_buf[g] = k_src[owner] + jnp.sum(k_rcv[...], axis=0)
        to_column(KZ, kz_buf.at[g], kz_buf.at[g])
        arrived(KZ, kz_buf.at[others_z])
        kc_buf[owner] = jnp.sum(kz_buf[...], axis=0) / nodes
        to_plane(KC, lambda peer, k: kc_buf.at[owner], lambda peer, k: kc_buf.at[owner])
        arrived(KC, kc_buf.at[pl.ds(0, n_own - 1)])

    @pl.when(jnp.logical_not(owns))
    def _():
        arrived(KC, kc_buf)

    summed = kc_buf[...].reshape(128, 128)
    inverse = inverse_factor(summed[64:, :64])
    v_t = mul(inverse, clean_t)
    v_leaf_t[...] = v_t[:, :leaf_count]
    ends = jnp.concatenate([v_t[:, leaf_count:], jnp.zeros((64, 112), F32)], axis=1)
    ends = jnp.transpose(ends)
    v_sep[...] = ends[0:8]
    v_root[...] = ends[8:16]
    both = mul(inverse, summed[:64])
    red_g[...] = mul(both[:, :64], inverse, NT)
    red_c[...] = mul(both[:, 64:], inverse, NT)

    sent(A, a_rcv)
    sent(B, b_buf.at[others])
    sent(SL, sl_buf.at[others])
    sent(SU, su_buf.at[others])
    sent(SP, sp_buf.at[others])
    sent(L, l_buf.at[others_z])
    sent(U, u_buf.at[others_z])
    sent(RZ, rz_buf.at[others_z])
    sent(D, d_buf.at[:, others])
    sent(E_, e_buf.at[:, others])
    sent(F_, f_buf.at[:, others])
    sent(Z, z_buf.at[others])
    sent(PR, p_rcv)
    sent(PZ, pz_buf.at[others_z])
    sent(PC, pc_buf.at[others])

    @pl.when(owns)
    def _():
        sent(KR, k_src.at[pl.ds(0, n_own - 1)])
        sent(KZ, kz_buf.at[others_z])
        sent(KC, k_rcv)

    @pl.when(jnp.logical_not(owns))
    def _():
        sent(KR, k_src)


def shards(
    n_outer,
    n_inner,
    b_leaf,
    b_sep,
    b_root,
    leaf_linv,
    leaf_uinv,
    leaf_lower,
    leaf_upper,
    sep_rows,
    sep_linv,
    sep_uinv,
    sep_lower,
    sep_upper,
    root_linv,
    root_uinv,
    basis_leaf,
    basis_sep,
    basis_root,
    g_blocks,
    c_blocks,
    block_cols,
):
    nodes, ports = b_leaf.shape
    basis = basis_leaf.shape[1]
    root = root_linv.shape[1]
    width = n_inner * 8
    half = n_outer // 2
    per = PIECES_P // n_inner
    n_own = min(PIECES_K, n_inner)
    per_k = PIECES_K // n_own
    vmem = pl.BlockSpec(memory_space=pltpu.VMEM)
    smem = pl.BlockSpec(memory_space=pltpu.SMEM)
    scratch = [
        (n_inner, 8, 128),
        (n_inner - 1, 8, 128),
        (n_inner, 8, 128),
        (n_inner, 8, width),
        (n_inner, 8, width),
        (n_inner, 8, 128),
        (n_inner, 8, 128),
        (n_outer, 8, root),
        (n_outer, 8, root),
        (n_outer, n_outer * 4, 128),
        (half, n_inner, 8, 128),
        (half, n_inner, 8, 128),
        (half, n_inner, 8, 128),
        (n_inner, 8, 128),
        (n_inner, per, 8, 128),
        (n_inner - 1, per, 8, 128),
        (n_outer, per, 8, 128),
        (n_inner, per, 8, 128),
        (n_own, per_k, 8, 128),
        (n_inner - 1, per_k, 8, 128),
        (n_outer, per_k, 8, 128),
        (n_own, per_k, 8, 128),
        (nodes + 16, basis),
        (nodes, nodes),
        (nodes, nodes),
    ]
    outs = [(ports, nodes), (8, ports), (8, ports), (ports, basis), (ports, ports), (ports, ports)]
    v_leaf_t, v_sep, v_root, coef_t, red_g, red_c = pl.pallas_call(
        functools.partial(kernel, n_outer, n_inner),
        out_shape=[jax.ShapeDtypeStruct(s, F32) for s in outs],
        in_specs=[vmem] * 19 + [smem],
        out_specs=[vmem] * 6,
        scratch_shapes=[pltpu.VMEM(s, F32) for s in scratch]
        + [pltpu.SemaphoreType.DMA((18,)), pltpu.SemaphoreType.DMA((18,))],
        compiler_params=pltpu.CompilerParams(
            collective_id=0, has_side_effects=True, vmem_limit_bytes=48 * 2**20
        ),
    )(
        b_leaf.T,
        b_sep,
        b_root,
        leaf_linv,
        leaf_uinv,
        leaf_lower,
        leaf_upper,
        sep_rows,
        sep_linv,
        sep_uinv,
        sep_lower.T,
        sep_upper,
        root_linv,
        root_uinv,
        basis_leaf,
        basis_sep,
        basis_root,
        g_blocks,
        c_blocks,
        block_cols,
    )
    return v_leaf_t.T, v_sep, v_root, coef_t.T, red_g, red_c


def solution(mesh):
    rows = P(("outer", "inner"), None)
    return jax.shard_map(
        functools.partial(shards, mesh.shape["outer"], mesh.shape["inner"]),
        mesh=mesh,
        in_specs=(rows,) * 10 + (P(None, ("outer", "inner")),) + (rows,) * 9,
        out_specs=(rows, rows, rows, P(), P(), P()),
        check_vma=False,
    )
```

```python
import functools

import jax
import jax.numpy as jnp
from jax import lax
from jax.experimental import pallas as pl
from jax.experimental.pallas import tpu as pltpu
from jax.sharding import PartitionSpec as P

MESH = pl.DeviceIdType.MESH
F32 = jnp.float32
NN = ((1,), (0,))
NT = ((1,), (1,))
TN = ((0,), (0,))
PIECES_P = 32
PIECES_K = 16


def mul(left, right, dims=NN):
    return lax.dot_general(
        left, right, (dims, ((), ())), precision=lax.Precision.HIGHEST, preferred_element_type=F32
    )


def wide(block):
    return jnp.concatenate([block, jnp.zeros_like(block)], axis=1)


def folded(block):
    half = block.shape[0] // 2
    return jnp.concatenate([block[:half], block[half:]], axis=1)


def unfolded_product(left, both):
    half = left.shape[1] // 2
    upper = mul(left[:, :half], both)
    lower = mul(left[:, half:], both)
    return upper[:, :64] + lower[:, 64:]


def inverse_factor(gram):
    row_ids = lax.broadcasted_iota(jnp.int32, (64, 64), 0)
    col_ids = lax.broadcasted_iota(jnp.int32, (64, 64), 1)
    start = jnp.concatenate([gram, (row_ids == col_ids).astype(F32)], axis=1)
    groups = tuple(start[8 * a : 8 * a + 8] for a in range(8))
    sub = lax.broadcasted_iota(jnp.int32, (8, 128), 0)

    def panel(p, groups):
        groups = list(groups)
        scale = jnp.zeros((8, 128), F32)
        for k in range(8):
            row = groups[0][k : k + 1, :]
            pivot = row[:, k : k + 1]
            scaled = row / pivot
            for a in range(8):
                factor = groups[a][:, k : k + 1]
                if a == 0:
                    factor = jnp.where(sub > k, jnp.broadcast_to(factor, (8, 128)), 0.0)
                else:
                    live = jnp.where(a + p < 8, 1.0, 0.0).astype(F32)
                    factor = jnp.broadcast_to(factor, (8, 128)) * live
                groups[a] = groups[a] - factor * scaled
            scale = jnp.where(sub == k, jnp.broadcast_to(lax.rsqrt(pivot), (8, 128)), scale)
        groups[0] = groups[0] * scale
        turned = [pltpu.roll(x, 120, 1) for x in groups]
        return tuple(turned[1:] + turned[:1])

    groups = lax.fori_loop(0, 8, panel, groups)
    return jnp.concatenate(groups, axis=0)[:, :64]


def by_owner(columns, n_outer, n_inner, out_ref):
    if n_inner * 8 != 256:
        moved = columns.reshape(8, n_outer, n_inner, 8).transpose(2, 0, 1, 3).reshape(n_inner, 8, n_outer * 8)
        out_ref[...] = jnp.concatenate(
            [moved, jnp.zeros((n_inner, 8, 128 - n_outer * 8), F32)], axis=2
        )
        return
    lane_group = lax.broadcasted_iota(jnp.int32, (8, 128), 1) // 8
    for m in range(2):
        shifted = []
        for o in range(n_outer):
            at = o * 256 + m * 128
            piece = columns[:, at : at + 128]
            shifted.append(pltpu.roll(piece, o * 8, 1) if o else piece)
        for ii in range(16):
            total = shifted[0]
            for o in range(1, n_outer):
                total = jnp.where(lane_group == (ii + o) % 16, shifted[o], total)
            out_ref[16 * m + ii] = pltpu.roll(total, 128 - ii * 8, 1) if ii else total


def kernel(
    n_outer,
    n_inner,
    h_b_t,
    h_b_sep,
    h_b_root,
    h_leaf_linv,
    h_leaf_uinv,
    h_leaf_lower,
    h_leaf_upper,
    h_sep_rows,
    h_sep_linv,
    h_sep_uinv,
    h_sep_lower_t,
    h_sep_upper,
    h_root_linv,
    h_root_uinv,
    h_basis_leaf,
    h_basis_sep,
    h_basis_root,
    h_g_blocks,
    h_c_blocks,
    h_block_cols,
    v_leaf_t,
    v_sep,
    v_root,
    coef_t,
    red_g,
    red_c,
    a_src,
    a_rcv,
    b_buf,
    sl_buf,
    su_buf,
    sp_src,
    sp_buf,
    l_buf,
    u_buf,
    rz_buf,
    d_buf,
    e_buf,
    f_buf,
    z_buf,
    p_src,
    p_rcv,
    pz_buf,
    pc_buf,
    k_src,
    k_rcv,
    kz_buf,
    kc_buf,
    q_all,
    hg,
    hc,
    b_t,
    b_sep,
    b_root,
    leaf_linv,
    leaf_uinv,
    leaf_lower,
    leaf_upper,
    sep_rows,
    sep_lower_t,
    sep_upper,
    g_blocks,
    c_blocks,
    block_cols,
    send,
    recv,
    here,
):
    g = lax.axis_index("outer")
    i = lax.axis_index("inner")
    rb = n_outer * 8
    n_own = kc_buf.shape[0]
    stride = n_inner // n_own
    leaf_count = h_basis_leaf.shape[0]
    nodes = float(n_outer * n_inner * (leaf_count + 16))
    A, B, SL, SU, SP, L, U, RZ, D, E_, F_, Z, PR, PZ, PC, KR, KZ, KC = range(18)

    def to_plane(phase, src, dst):
        def one(k, carry):
            peer = lax.rem(i + k, n_inner)
            pltpu.make_async_remote_copy(
                src_ref=src(peer, k),
                dst_ref=dst(peer, k),
                send_sem=send.at[phase],
                recv_sem=recv.at[phase],
                device_id=(g, peer),
                device_id_type=MESH,
            ).start()
            return carry

        lax.fori_loop(1, n_inner, one, 0)

    def to_column(phase, src, dst):
        def one(k, carry):
            peer = lax.rem(g + k, n_outer)
            pltpu.make_async_remote_copy(
                src_ref=src,
                dst_ref=dst,
                send_sem=send.at[phase],
                recv_sem=recv.at[phase],
                device_id=(peer, i),
                device_id_type=MESH,
            ).start()
            return carry

        lax.fori_loop(1, n_outer, one, 0)

    def arrived(phase, like):
        pltpu.make_async_copy(like, like, recv.at[phase]).wait()

    def sent(phase, like):
        pltpu.make_async_copy(like, like, send.at[phase]).wait()

    others = pl.ds(0, n_inner - 1)
    others_z = pl.ds(0, n_outer - 1)

    own_slots = {
        "b_t": (h_b_t, b_t),
        "leaf_linv": (h_leaf_linv, leaf_linv),
        "leaf_lower": (h_leaf_lower, leaf_lower),
        "sep_rows": (h_sep_rows, sep_rows),
        "sep_lower_t": (h_sep_lower_t, sep_lower_t),
        "sep_linv": (h_sep_linv, sl_buf.at[i]),
        "root_linv": (h_root_linv, l_buf.at[g]),
        "root_uinv": (h_root_uinv, u_buf.at[g]),
        "sep_uinv": (h_sep_uinv, su_buf.at[i]),
        "b_sep": (h_b_sep, b_sep),
        "leaf_uinv": (h_leaf_uinv, leaf_uinv),
        "leaf_upper": (h_leaf_upper, leaf_upper),
        "b_root": (h_b_root, b_root),
        "sep_upper": (h_sep_upper, sep_upper),
        "g_blocks": (h_g_blocks, g_blocks),
        "c_blocks": (h_c_blocks, c_blocks),
        "block_cols": (h_block_cols, block_cols),
        "basis_leaf": (h_basis_leaf, q_all.at[pl.ds(0, leaf_count)]),
        "basis_sep": (h_basis_sep, q_all.at[pl.ds(leaf_count, 8)]),
        "basis_root": (h_basis_root, q_all.at[pl.ds(leaf_count + 8, 8)]),
    }
    loads = {
        name: pltpu.make_async_copy(src, dst, here.at[n])
        for n, (name, (src, dst)) in enumerate(own_slots.items())
    }
    for load in loads.values():
        load.start()

    def loaded(*names):
        for name in names:
            loads[name].wait()

    barrier = pltpu.get_barrier_semaphore()

    def greet_plane(k, carry):
        pl.semaphore_signal(
            barrier, inc=1, device_id=(g, lax.rem(i + k, n_inner)), device_id_type=MESH
        )
        return carry

    def greet_column(k, carry):
        pl.semaphore_signal(
            barrier, inc=1, device_id=(lax.rem(g + k, n_outer), i), device_id_type=MESH
        )
        return carry

    lax.fori_loop(1, n_inner, greet_plane, 0)
    lax.fori_loop(1, n_outer, greet_column, 0)

    loaded("b_t", "leaf_linv", "leaf_lower", "sep_rows", "sep_lower_t")
    width = n_inner * 8
    couples = sep_rows.shape[1]
    sel_t = (
        lax.broadcasted_iota(jnp.int32, (width, couples), 0)
        == jnp.broadcast_to(sep_rows[...], (width, couples))
    ).astype(F32)
    y_t = mul(b_t[...], leaf_linv[...], NT)
    contrib_t = mul(y_t, leaf_lower[...], NT)
    update = mul(sel_t, contrib_t, NT)
    a_src[...] = wide(update).reshape(n_inner, 8, 128)
    by_owner(sep_lower_t[...], n_outer, n_inner, sp_src)
    sp_buf[i] = sp_src[i]
    loaded("sep_linv", "root_linv", "root_uinv", "sep_uinv", "b_sep")

    pl.semaphore_wait(barrier, n_inner + n_outer - 2)

    to_plane(A, lambda peer, k: a_src.at[peer], lambda peer, k: a_rcv.at[k - 1])
    to_plane(SL, lambda peer, k: sl_buf.at[i], lambda peer, k: sl_buf.at[i])
    to_plane(SP, lambda peer, k: sp_src.at[peer], lambda peer, k: sp_buf.at[i])
    to_column(L, l_buf.at[g], l_buf.at[g])

    arrived(A, a_rcv)
    b_buf[i] = wide(b_sep[...]) - (a_src[i] + jnp.sum(a_rcv[...], axis=0))
    to_plane(B, lambda peer, k: b_buf.at[i], lambda peer, k: b_buf.at[i])

    loaded("leaf_uinv", "leaf_upper", "b_root")
    uy_t = mul(y_t, leaf_uinv[...], NT)
    coupling = mul(leaf_uinv[...], mul(leaf_upper[...], sel_t, NT))
    arrived(SL, sl_buf.at[others])
    arrived(SP, sp_buf.at[others])
    to_root = mul(sp_buf[...].reshape(width, 128)[:, :rb], sl_buf[...].reshape(width, width), TN)

    arrived(B, b_buf.at[others])
    rhs_sep = b_buf[...].reshape(width, 128)[:, :64]
    part = mul(to_root, rhs_sep)
    mine = lax.broadcasted_iota(jnp.int32, (rb, 64), 0) // 8 == g
    own = jnp.where(mine, jnp.concatenate([b_root[...]] * n_outer, axis=0), 0.0)
    rz_buf[g] = folded(own - part)
    to_column(RZ, rz_buf.at[g], rz_buf.at[g])
    to_plane(SU, lambda peer, k: su_buf.at[i], lambda peer, k: su_buf.at[i])
    y_own = mul(sl_buf[i], rhs_sep)
    arrived(RZ, rz_buf.at[others_z])

    def root_gather(phase, buf, block):
        buf[:, i] = block.reshape(n_outer // 2, 8, 128)
        to_plane(phase, lambda peer, k: buf.at[:, i], lambda peer, k: buf.at[:, i])

    def root_value(phase, buf):
        arrived(phase, buf.at[:, others])
        return buf[...].reshape(n_outer // 2 * n_inner * 8, 128)

    root_gather(D, d_buf, jnp.sum(rz_buf[...], axis=0))
    to_column(U, u_buf.at[g], u_buf.at[g])
    arrived(L, l_buf.at[others_z])
    lower_rows = l_buf[...].reshape(rb, l_buf.shape[2])
    y_root = unfolded_product(lower_rows, root_value(D, d_buf))
    root_gather(E_, e_buf, folded(y_root))

    loaded("g_blocks", "c_blocks", "block_cols", "basis_leaf", "basis_sep", "basis_root", "sep_upper")
    size = g_blocks.shape[1]
    stored = block_cols.shape[1]
    for r in range(2):
        for c in range(2):
            for blocks, whole in ((g_blocks, hg), (c_blocks, hc)):
                total = jnp.zeros((size, size), F32)
                for w in range(stored):
                    at = (r * stored + w) * size
                    weight = (block_cols[r : r + 1, w : w + 1] == c).astype(F32)
                    total = total + weight * blocks[at : at + size, :]
                whole[r * size : (r + 1) * size, c * size : (c + 1) * size] = total
    arrived(SU, su_buf.at[others])
    from_sep = mul(coupling, su_buf[...].reshape(width, width))

    arrived(U, u_buf.at[others_z])
    upper_rows = u_buf[...].reshape(rb, u_buf.shape[2])
    x_root = unfolded_product(upper_rows, root_value(E_, e_buf))
    root_gather(F_, f_buf, folded(x_root))
    row_ids = lax.broadcasted_iota(jnp.int32, (8, rb), 0)
    col_ids = lax.broadcasted_iota(jnp.int32, (8, rb), 1)
    pick = (col_ids == row_ids + 8 * g).astype(F32)
    x_root_t = mul(x_root, pick, ((0,), (1,)))

    z_own = y_own - unfolded_product(sep_upper[...], root_value(F_, f_buf))
    z_buf[i] = wide(z_own)
    to_plane(Z, lambda peer, k: z_buf.at[i], lambda peer, k: z_buf.at[i])
    arrived(Z, z_buf.at[others])
    z_t = jnp.transpose(z_buf[...].reshape(width, 128))[:64]
    x_leaf_t = uy_t - mul(z_t, from_sep, NT)
    x_sep_t = mul(z_t, su_buf[i], NT)
    x_t = jnp.concatenate([x_leaf_t, x_sep_t, x_root_t], axis=1)

    proj_t = mul(x_t, q_all[...])
    per = PIECES_P // n_inner
    for t in range(PIECES_P):
        r, c = t // 4, t % 4
        p_src[t // per, t % per] = proj_t[8 * r : 8 * r + 8, 128 * c : 128 * c + 128]
    to_plane(PR, lambda peer, k: p_src.at[peer], lambda peer, k: p_rcv.at[k - 1])
    arrived(PR, p_rcv)
    pz_buf[g] = p_src[i] + jnp.sum(p_rcv[...], axis=0)
    to_column(PZ, pz_buf.at[g], pz_buf.at[g])
    arrived(PZ, pz_buf.at[others_z])
    pc_buf[i] = jnp.sum(pz_buf[...], axis=0) / nodes
    to_plane(PC, lambda peer, k: pc_buf.at[i], lambda peer, k: pc_buf.at[i])
    arrived(PC, pc_buf.at[others])
    coefs = jnp.concatenate(
        [
            jnp.concatenate(
                [pc_buf[(4 * r + c) // per, (4 * r + c) % per] for c in range(4)], axis=1
            )
            for r in range(8)
        ],
        axis=0,
    )
    coef_t[...] = coefs
    clean_t = x_t - mul(coefs, q_all[...], NT)

    gram_part = mul(clean_t, clean_t, NT)
    clean_leaf_t = clean_t[:, :leaf_count]
    g_part = mul(mul(clean_leaf_t, hg[...]), clean_leaf_t, NT)
    c_part = mul(mul(clean_leaf_t, hc[...]), clean_leaf_t, NT)
    per_k = PIECES_K // n_own
    products = jnp.concatenate(
        [jnp.concatenate([g_part, c_part], axis=1), wide(gram_part)], axis=0
    )
    k_src[...] = products.reshape(n_own, per_k, 8, 128)
    owner = i // stride
    owns = lax.rem(i, stride) == 0

    def to_owner(k, carry):
        peer = lax.rem(i + k, n_inner)

        @pl.when(lax.rem(peer, stride) == 0)
        def _():
            pltpu.make_async_remote_copy(
                src_ref=k_src.at[peer // stride],
                dst_ref=k_rcv.at[k - 1],
                send_sem=send.at[KR],
                recv_sem=recv.at[KR],
                device_id=(g, peer),
                device_id_type=MESH,
            ).start()

        return carry

    lax.fori_loop(1, n_inner, to_owner, 0)

    @pl.when(owns)
    def _():
        arrived(KR, k_rcv)
        kz_buf[g] = k_src[owner] + jnp.sum(k_rcv[...], axis=0)
        to_column(KZ, kz_buf.at[g], kz_buf.at[g])
        arrived(KZ, kz_buf.at[others_z])
        kc_buf[owner] = jnp.sum(kz_buf[...], axis=0) / nodes
        to_plane(KC, lambda peer, k: kc_buf.at[owner], lambda peer, k: kc_buf.at[owner])
        arrived(KC, kc_buf.at[pl.ds(0, n_own - 1)])

    @pl.when(jnp.logical_not(owns))
    def _():
        arrived(KC, kc_buf)

    summed = kc_buf[...].reshape(128, 128)
    inverse = inverse_factor(summed[64:, :64])
    v_t = mul(inverse, clean_t)
    v_leaf_t[...] = v_t[:, :leaf_count]
    ends = jnp.concatenate([v_t[:, leaf_count:], jnp.zeros((64, 112), F32)], axis=1)
    ends = jnp.transpose(ends)
    v_sep[...] = ends[0:8]
    v_root[...] = ends[8:16]
    both = mul(inverse, summed[:64])
    red_g[...] = mul(both[:, :64], inverse, NT)
    red_c[...] = mul(both[:, 64:], inverse, NT)

    sent(A, a_rcv)
    sent(B, b_buf.at[others])
    sent(SL, sl_buf.at[others])
    sent(SU, su_buf.at[others])
    sent(SP, sp_buf.at[others])
    sent(L, l_buf.at[others_z])
    sent(U, u_buf.at[others_z])
    sent(RZ, rz_buf.at[others_z])
    sent(D, d_buf.at[:, others])
    sent(E_, e_buf.at[:, others])
    sent(F_, f_buf.at[:, others])
    sent(Z, z_buf.at[others])
    sent(PR, p_rcv)
    sent(PZ, pz_buf.at[others_z])
    sent(PC, pc_buf.at[others])

    @pl.when(owns)
    def _():
        sent(KR, k_src.at[pl.ds(0, n_own - 1)])
        sent(KZ, kz_buf.at[others_z])
        sent(KC, k_rcv)

    @pl.when(jnp.logical_not(owns))
    def _():
        sent(KR, k_src)


def shards(
    n_outer,
    n_inner,
    b_leaf,
    b_sep,
    b_root,
    leaf_linv,
    leaf_uinv,
    leaf_lower,
    leaf_upper,
    sep_rows,
    sep_linv,
    sep_uinv,
    sep_lower,
    sep_upper,
    root_linv,
    root_uinv,
    basis_leaf,
    basis_sep,
    basis_root,
    g_blocks,
    c_blocks,
    block_cols,
):
    nodes, ports = b_leaf.shape
    basis = basis_leaf.shape[1]
    root = root_linv.shape[1]
    width = n_inner * 8
    half = n_outer // 2
    per = PIECES_P // n_inner
    n_own = min(PIECES_K, n_inner)
    per_k = PIECES_K // n_own
    vmem = pl.BlockSpec(memory_space=pltpu.VMEM)
    hbm = pl.BlockSpec(memory_space=pltpu.HBM)
    scratch = [
        (n_inner, 8, 128),
        (n_inner - 1, 8, 128),
        (n_inner, 8, 128),
        (n_inner, 8, width),
        (n_inner, 8, width),
        (n_inner, 8, 128),
        (n_inner, 8, 128),
        (n_outer, 8, root),
        (n_outer, 8, root),
        (n_outer, n_outer * 4, 128),
        (half, n_inner, 8, 128),
        (half, n_inner, 8, 128),
        (half, n_inner, 8, 128),
        (n_inner, 8, 128),
        (n_inner, per, 8, 128),
        (n_inner - 1, per, 8, 128),
        (n_outer, per, 8, 128),
        (n_inner, per, 8, 128),
        (n_own, per_k, 8, 128),
        (n_inner - 1, per_k, 8, 128),
        (n_outer, per_k, 8, 128),
        (n_own, per_k, 8, 128),
        (nodes + 16, basis),
        (nodes, nodes),
        (nodes, nodes),
    ]
    b_leaf_t, sep_lower_t = b_leaf.T, sep_lower.T
    kept = (
        b_leaf_t,
        b_sep,
        b_root,
        leaf_linv,
        leaf_uinv,
        leaf_lower,
        leaf_upper,
        sep_rows,
        sep_lower_t,
        sep_upper,
        g_blocks,
        c_blocks,
        block_cols,
    )
    outs = [(ports, nodes), (8, ports), (8, ports), (ports, basis), (ports, ports), (ports, ports)]
    v_leaf_t, v_sep, v_root, coef_t, red_g, red_c = pl.pallas_call(
        functools.partial(kernel, n_outer, n_inner),
        out_shape=[jax.ShapeDtypeStruct(s, F32) for s in outs],
        in_specs=[hbm] * 20,
        out_specs=[vmem] * 6,
        scratch_shapes=[pltpu.VMEM(s, F32) for s in scratch]
        + [pltpu.VMEM(x.shape, x.dtype) for x in kept]
        + [pltpu.SemaphoreType.DMA((n,)) for n in (18, 18, 20)],
        compiler_params=pltpu.CompilerParams(
            collective_id=0, has_side_effects=True, vmem_limit_bytes=64 * 2**20
        ),
    )(
        b_leaf_t,
        b_sep,
        b_root,
        leaf_linv,
        leaf_uinv,
        leaf_lower,
        leaf_upper,
        sep_rows,
        sep_linv,
        sep_uinv,
        sep_lower_t,
        sep_upper,
        root_linv,
        root_uinv,
        basis_leaf,
        basis_sep,
        basis_root,
        g_blocks,
        c_blocks,
        block_cols,
    )
    return v_leaf_t.T, v_sep, v_root, coef_t.T, red_g, red_c


def solution(mesh):
    rows = P(("outer", "inner"), None)
    return jax.shard_map(
        functools.partial(shards, mesh.shape["outer"], mesh.shape["inner"]),
        mesh=mesh,
        in_specs=(rows,) * 10 + (P(None, ("outer", "inner")),) + (rows,) * 9,
        out_specs=(rows, rows, rows, P(), P(), P()),
        check_vma=False,
    )
```

```python
import functools

import jax
import jax.numpy as jnp
from jax import lax
from jax.experimental import pallas as pl
from jax.experimental.pallas import tpu as pltpu
from jax.sharding import PartitionSpec as P

MESH = pl.DeviceIdType.MESH
F32 = jnp.float32
NN = ((1,), (0,))
NT = ((1,), (1,))
TN = ((0,), (0,))
PIECES_P = 32
PIECES_K = 16


def mul(left, right, dims=NN):
    return lax.dot_general(
        left, right, (dims, ((), ())), precision=lax.Precision.HIGHEST, preferred_element_type=F32
    )


def wide(block):
    return jnp.concatenate([block, jnp.zeros_like(block)], axis=1)


def folded(block):
    half = block.shape[0] // 2
    return jnp.concatenate([block[:half], block[half:]], axis=1)


def unfolded_product(left, both):
    half = left.shape[1] // 2
    upper = mul(left[:, :half], both)
    lower = mul(left[:, half:], both)
    return upper[:, :64] + lower[:, 64:]


def inverse_factor(gram):
    row_ids = lax.broadcasted_iota(jnp.int32, (64, 64), 0)
    col_ids = lax.broadcasted_iota(jnp.int32, (64, 64), 1)
    start = jnp.concatenate([gram, (row_ids == col_ids).astype(F32)], axis=1)
    groups = tuple(start[8 * a : 8 * a + 8] for a in range(8))
    sub = lax.broadcasted_iota(jnp.int32, (8, 128), 0)

    def panel(p, groups):
        groups = list(groups)
        scale = jnp.zeros((8, 128), F32)
        for k in range(8):
            row = groups[0][k : k + 1, :]
            pivot = row[:, k : k + 1]
            scaled = row / pivot
            for a in range(8):
                factor = groups[a][:, k : k + 1]
                if a == 0:
                    factor = jnp.where(sub > k, jnp.broadcast_to(factor, (8, 128)), 0.0)
                else:
                    live = jnp.where(a + p < 8, 1.0, 0.0).astype(F32)
                    factor = jnp.broadcast_to(factor, (8, 128)) * live
                groups[a] = groups[a] - factor * scaled
            scale = jnp.where(sub == k, jnp.broadcast_to(lax.rsqrt(pivot), (8, 128)), scale)
        groups[0] = groups[0] * scale
        turned = [pltpu.roll(x, 120, 1) for x in groups]
        return tuple(turned[1:] + turned[:1])

    groups = lax.fori_loop(0, 8, panel, groups)
    return jnp.concatenate(groups, axis=0)[:, :64]


def by_owner(columns, n_outer, n_inner, out_ref):
    if n_inner * 8 != 256:
        moved = columns.reshape(8, n_outer, n_inner, 8).transpose(2, 0, 1, 3).reshape(n_inner, 8, n_outer * 8)
        out_ref[...] = jnp.concatenate(
            [moved, jnp.zeros((n_inner, 8, 128 - n_outer * 8), F32)], axis=2
        )
        return
    lane_group = lax.broadcasted_iota(jnp.int32, (8, 128), 1) // 8
    for m in range(2):
        shifted = []
        for o in range(n_outer):
            at = o * 256 + m * 128
            piece = columns[:, at : at + 128]
            shifted.append(pltpu.roll(piece, o * 8, 1) if o else piece)
        for ii in range(16):
            total = shifted[0]
            for o in range(1, n_outer):
                total = jnp.where(lane_group == (ii + o) % 16, shifted[o], total)
            out_ref[16 * m + ii] = pltpu.roll(total, 128 - ii * 8, 1) if ii else total


def kernel(
    n_outer,
    n_inner,
    h_b_t,
    h_b_sep,
    h_b_root,
    h_leaf_linv,
    h_leaf_uinv,
    h_leaf_lower,
    h_leaf_upper,
    h_sep_rows,
    h_sep_linv,
    h_sep_uinv,
    h_sep_lower_t,
    h_sep_upper,
    h_root_linv,
    h_root_uinv,
    h_basis_leaf,
    h_basis_sep,
    h_basis_root,
    h_g_blocks,
    h_c_blocks,
    h_block_cols,
    v_leaf_t,
    v_sep,
    v_root,
    coef_t,
    red_g,
    red_c,
    a_src,
    a_rcv,
    b_buf,
    sl_buf,
    su_buf,
    sp_src,
    sp_buf,
    ss_src,
    ss_buf,
    l_buf,
    u_buf,
    rz_buf,
    d_buf,
    e_buf,
    n_src,
    n_rcv,
    n_buf,
    m_src,
    m_rcv,
    m_buf,
    p_src,
    p_rcv,
    pz_buf,
    w_src,
    w_rcv,
    w_buf,
    k_src,
    k_rcv,
    kz_buf,
    kc_buf,
    q_all,
    hg,
    hc,
    b_t,
    b_sep,
    b_root,
    leaf_linv,
    leaf_uinv,
    leaf_lower,
    leaf_upper,
    sep_rows,
    sep_lower_t,
    sep_upper,
    g_blocks,
    c_blocks,
    block_cols,
    send,
    recv,
    here,
):
    g = lax.axis_index("outer")
    i = lax.axis_index("inner")
    rb = n_outer * 8
    n_own = kc_buf.shape[0]
    stride = n_inner // n_own
    leaf_count = h_basis_leaf.shape[0]
    nodes = float(n_outer * n_inner * (leaf_count + 16))
    A, B, SL, SU, SP, SS, L, U, RZ, D, E_, N1, N2, N3, N4, P1, P2, W1, W2, KR, KZ, KG, KC = range(23)

    def to_plane(phase, src, dst):
        def one(k, carry):
            peer = lax.rem(i + k, n_inner)
            pltpu.make_async_remote_copy(
                src_ref=src(peer, k),
                dst_ref=dst(peer, k),
                send_sem=send.at[phase],
                recv_sem=recv.at[phase],
                device_id=(g, peer),
                device_id_type=MESH,
            ).start()
            return carry

        lax.fori_loop(1, n_inner, one, 0)

    def to_column(phase, src, dst):
        def one(k, carry):
            peer = lax.rem(g + k, n_outer)
            pltpu.make_async_remote_copy(
                src_ref=src(peer),
                dst_ref=dst,
                send_sem=send.at[phase],
                recv_sem=recv.at[phase],
                device_id=(peer, i),
                device_id_type=MESH,
            ).start()
            return carry

        lax.fori_loop(1, n_outer, one, 0)

    def arrived(phase, like):
        pltpu.make_async_copy(like, like, recv.at[phase]).wait()

    def sent(phase, like):
        pltpu.make_async_copy(like, like, send.at[phase]).wait()

    others = pl.ds(0, n_inner - 1)
    others_z = pl.ds(0, n_outer - 1)

    own_slots = {
        "b_t": (h_b_t, b_t),
        "leaf_linv": (h_leaf_linv, leaf_linv),
        "leaf_lower": (h_leaf_lower, leaf_lower),
        "sep_rows": (h_sep_rows, sep_rows),
        "sep_lower_t": (h_sep_lower_t, sep_lower_t),
        "sep_linv": (h_sep_linv, sl_buf.at[i]),
        "root_linv": (h_root_linv, l_buf.at[g]),
        "root_uinv": (h_root_uinv, u_buf.at[g]),
        "sep_uinv": (h_sep_uinv, su_buf.at[i]),
        "b_sep": (h_b_sep, b_sep),
        "leaf_uinv": (h_leaf_uinv, leaf_uinv),
        "leaf_upper": (h_leaf_upper, leaf_upper),
        "b_root": (h_b_root, b_root),
        "sep_upper": (h_sep_upper, sep_upper),
        "g_blocks": (h_g_blocks, g_blocks),
        "c_blocks": (h_c_blocks, c_blocks),
        "block_cols": (h_block_cols, block_cols),
        "basis_leaf": (h_basis_leaf, q_all.at[pl.ds(0, leaf_count)]),
        "basis_sep": (h_basis_sep, q_all.at[pl.ds(leaf_count, 8)]),
        "basis_root": (h_basis_root, q_all.at[pl.ds(leaf_count + 8, 8)]),
    }
    loads = {
        name: pltpu.make_async_copy(src, dst, here.at[n])
        for n, (name, (src, dst)) in enumerate(own_slots.items())
    }
    for load in loads.values():
        load.start()

    def loaded(*names):
        for name in names:
            loads[name].wait()

    barrier = pltpu.get_barrier_semaphore()

    def greet_plane(k, carry):
        pl.semaphore_signal(
            barrier, inc=1, device_id=(g, lax.rem(i + k, n_inner)), device_id_type=MESH
        )
        return carry

    def greet_column(k, carry):
        pl.semaphore_signal(
            barrier, inc=1, device_id=(lax.rem(g + k, n_outer), i), device_id_type=MESH
        )
        return carry

    lax.fori_loop(1, n_inner, greet_plane, 0)
    lax.fori_loop(1, n_outer, greet_column, 0)

    loaded("b_t", "leaf_linv", "leaf_lower", "sep_rows")
    width = n_inner * 8
    couples = sep_rows.shape[1]
    sel_t = (
        lax.broadcasted_iota(jnp.int32, (width, couples), 0)
        == jnp.broadcast_to(sep_rows[...], (width, couples))
    ).astype(F32)
    y_t = mul(b_t[...], leaf_linv[...], NT)
    contrib_t = mul(y_t, leaf_lower[...], NT)
    update = mul(sel_t, contrib_t, NT)
    a_src[...] = wide(update).reshape(n_inner, 8, 128)
    loaded("sep_lower_t", "sep_upper")
    by_owner(sep_lower_t[...], n_outer, n_inner, sp_src)
    sp_buf[i] = sp_src[i]
    by_owner(sep_upper[...], n_outer, n_inner, ss_src)
    ss_buf[i] = ss_src[i]
    loaded("sep_linv", "root_linv", "root_uinv", "sep_uinv", "b_sep")

    pl.semaphore_wait(barrier, n_inner + n_outer - 2)

    to_plane(A, lambda peer, k: a_src.at[peer], lambda peer, k: a_rcv.at[k - 1])
    to_plane(SL, lambda peer, k: sl_buf.at[i], lambda peer, k: sl_buf.at[i])
    to_plane(SP, lambda peer, k: sp_src.at[peer], lambda peer, k: sp_buf.at[i])
    to_column(L, lambda peer: l_buf.at[g], l_buf.at[g])

    loaded("leaf_uinv", "leaf_upper", "b_root", "basis_leaf", "basis_sep", "basis_root")
    uy_t = mul(y_t, leaf_uinv[...], NT)
    coupling = mul(leaf_uinv[...], mul(leaf_upper[...], sel_t, NT))
    n_src[...] = mul(coupling, q_all[:leaf_count, :], TN).reshape(n_src.shape)

    arrived(A, a_rcv)
    b_buf[i] = wide(b_sep[...]) - (a_src[i] + jnp.sum(a_rcv[...], axis=0))
    to_plane(B, lambda peer, k: b_buf.at[i], lambda peer, k: b_buf.at[i])
    to_plane(N1, lambda peer, k: n_src.at[peer], lambda peer, k: n_rcv.at[k - 1])
    to_plane(SU, lambda peer, k: su_buf.at[i], lambda peer, k: su_buf.at[i])
    to_plane(SS, lambda peer, k: ss_src.at[peer], lambda peer, k: ss_buf.at[i])

    arrived(SL, sl_buf.at[others])
    arrived(SP, sp_buf.at[others])
    sep_inverse = sl_buf[...].reshape(width, width)
    to_root = mul(sp_buf[...].reshape(width, 128)[:, :rb], sep_inverse, TN)

    arrived(B, b_buf.at[others])
    rhs_sep = b_buf[...].reshape(width, 128)
    part = mul(to_root, rhs_sep[:, :64])
    mine = lax.broadcasted_iota(jnp.int32, (rb, 64), 0) // 8 == g
    own = jnp.where(mine, jnp.concatenate([b_root[...]] * n_outer, axis=0), 0.0)
    rz_buf[g] = folded(own - part)
    to_column(RZ, lambda peer: rz_buf.at[g], rz_buf.at[g])
    to_column(U, lambda peer: u_buf.at[g], u_buf.at[g])

    arrived(N1, n_rcv)
    n_buf[i] = q_all[leaf_count : leaf_count + 8, :] - (n_src[i] + jnp.sum(n_rcv[...], axis=0))
    to_plane(N2, lambda peer, k: n_buf.at[i], lambda peer, k: n_buf.at[i])

    def root_gather(phase, buf, block):
        buf[:, i] = block.reshape(n_outer // 2, 8, 128)
        to_plane(phase, lambda peer, k: buf.at[:, i], lambda peer, k: buf.at[:, i])

    def root_value(phase, buf):
        arrived(phase, buf.at[:, others])
        return buf[...].reshape(n_outer // 2 * n_inner * 8, 128)

    arrived(RZ, rz_buf.at[others_z])
    root_gather(D, d_buf, jnp.sum(rz_buf[...], axis=0))

    y_own = mul(sl_buf[i], rhs_sep[:, :64])
    sep_y_t = mul(jnp.transpose(rhs_sep)[:64], sep_inverse, NT)
    arrived(SU, su_buf.at[others])
    sep_upper_inverse = su_buf[...].reshape(width, width)
    from_sep = mul(coupling, sep_upper_inverse)
    start_t = jnp.concatenate(
        [uy_t - mul(sep_y_t, from_sep, NT), mul(sep_y_t, su_buf[i], NT)], axis=1
    )
    proj_t = mul(start_t, q_all[: leaf_count + 8, :])
    per = PIECES_P // n_inner
    for t in range(PIECES_P):
        r, c = t // 4, t % 4
        p_src[t // per, t % per] = proj_t[8 * r : 8 * r + 8, 128 * c : 128 * c + 128]
    to_plane(P1, lambda peer, k: p_src.at[peer], lambda peer, k: p_rcv.at[k - 1])

    arrived(SS, ss_buf.at[others])
    sep_by_root = ss_buf[...].reshape(width, 128)[:, :rb]
    arrived(N2, n_buf.at[others])
    m_src[...] = mul(
        mul(sep_upper_inverse, sep_by_root), n_buf[...].reshape(width, n_buf.shape[2]), TN
    ).reshape(m_src.shape)
    m_rcv[g] = m_src[g]
    to_column(N3, lambda peer: m_src.at[peer], m_rcv.at[g])

    arrived(L, l_buf.at[others_z])
    lower_rows = l_buf[...].reshape(rb, l_buf.shape[2])
    y_root = unfolded_product(lower_rows, root_value(D, d_buf))
    root_gather(E_, e_buf, folded(y_root))

    arrived(P1, p_rcv)
    pz_buf[g] = p_src[i] + jnp.sum(p_rcv[...], axis=0)
    to_column(P2, lambda peer: pz_buf.at[g], pz_buf.at[g])

    loaded("g_blocks", "c_blocks", "block_cols")
    size = g_blocks.shape[1]
    stored = block_cols.shape[1]
    for r in range(2):
        for c in range(2):
            for blocks, whole in ((g_blocks, hg), (c_blocks, hc)):
                total = jnp.zeros((size, size), F32)
                for w in range(stored):
                    at = (r * stored + w) * size
                    weight = (block_cols[r : r + 1, w : w + 1] == c).astype(F32)
                    total = total + weight * blocks[at : at + size, :]
                whole[r * size : (r + 1) * size, c * size : (c + 1) * size] = total

    arrived(N3, m_rcv.at[others_z])
    m_buf[g] = jnp.sum(m_rcv[...], axis=0) - q_all[leaf_count + 8 : leaf_count + 16, :]
    to_column(N4, lambda peer: m_buf.at[g], m_buf.at[g])
    arrived(P2, pz_buf.at[others_z])
    proj_start = jnp.sum(pz_buf[...], axis=0)

    arrived(U, u_buf.at[others_z])
    upper_rows = u_buf[...].reshape(rb, u_buf.shape[2])
    x_root = unfolded_product(upper_rows, root_value(E_, e_buf))

    sep_part = wide(mul(sep_by_root, x_root)).reshape(n_inner, 8, 128)
    arrived(N4, m_buf.at[others_z])
    proj_t = mul(x_root, m_buf[...].reshape(rb, m_buf.shape[2]), TN)
    w_src[:, 0] = sep_part
    for t in range(PIECES_P):
        r, c = t // 4, t % 4
        w_src[t // per, 1 + t % per] = proj_t[8 * r : 8 * r + 8, 128 * c : 128 * c + 128]
    to_plane(W1, lambda peer, k: w_src.at[peer], lambda peer, k: w_rcv.at[k - 1])
    row_ids = lax.broadcasted_iota(jnp.int32, (8, rb), 0)
    col_ids = lax.broadcasted_iota(jnp.int32, (8, rb), 1)
    pick = (col_ids == row_ids + 8 * g).astype(F32)
    x_root_t = mul(x_root, pick, ((0,), (1,)))
    arrived(W1, w_rcv)
    moved = w_src[i] + jnp.sum(w_rcv[...], axis=0)
    w_buf[i, 0] = wide(y_own) - moved[0]
    w_buf[i, pl.ds(1, per)] = (proj_start - moved[1:]) / nodes
    to_plane(W2, lambda peer, k: w_buf.at[i], lambda peer, k: w_buf.at[i])
    arrived(W2, w_buf.at[others])

    z_t = jnp.transpose(w_buf[:, 0].reshape(width, 128))[:64]
    x_leaf_t = uy_t - mul(z_t, from_sep, NT)
    x_sep_t = mul(z_t, su_buf[i], NT)
    x_t = jnp.concatenate([x_leaf_t, x_sep_t, x_root_t], axis=1)
    coefs = jnp.concatenate(
        [
            jnp.concatenate(
                [w_buf[(4 * r + c) // per, 1 + (4 * r + c) % per] for c in range(4)], axis=1
            )
            for r in range(8)
        ],
        axis=0,
    )
    clean_t = x_t - mul(coefs, q_all[...], NT)

    per_k = PIECES_K // n_own
    half = n_own // 2
    owner = i // stride
    owns = lax.rem(i, stride) == 0
    owns_gram = jnp.logical_and(owns, owner >= half)
    owns_rest = jnp.logical_and(owns, owner < half)

    def to_owners(first):
        def one(k, carry):
            peer = lax.rem(i + k, n_inner)
            at = peer // stride

            @pl.when(jnp.logical_and(lax.rem(peer, stride) == 0, at // half == first // half))
            def _():
                pltpu.make_async_remote_copy(
                    src_ref=k_src.at[at],
                    dst_ref=k_rcv.at[k - 1],
                    send_sem=send.at[KR],
                    recv_sem=recv.at[KR],
                    device_id=(g, peer),
                    device_id_type=MESH,
                ).start()

            return carry

        lax.fori_loop(1, n_inner, one, 0)

    k_src[half:] = wide(mul(clean_t, clean_t, NT)).reshape(half, per_k, 8, 128)
    to_owners(half)
    clean_leaf_t = clean_t[:, :leaf_count]
    coef_t[...] = coefs
    g_part = mul(mul(clean_leaf_t, hg[...]), clean_leaf_t, NT)
    c_part = mul(mul(clean_leaf_t, hc[...]), clean_leaf_t, NT)
    k_src[:half] = jnp.concatenate([g_part, c_part], axis=1).reshape(half, per_k, 8, 128)
    to_owners(0)

    @pl.when(owns)
    def _():
        arrived(KR, k_rcv)
        kz_buf[g] = k_src[owner] + jnp.sum(k_rcv[...], axis=0)
        to_column(KZ, lambda peer: kz_buf.at[g], kz_buf.at[g])
        arrived(KZ, kz_buf.at[others_z])
        kc_buf[owner] = jnp.sum(kz_buf[...], axis=0) / nodes

    @pl.when(owns_gram)
    def _():
        to_plane(KG, lambda peer, k: kc_buf.at[owner], lambda peer, k: kc_buf.at[owner])
        arrived(KG, kc_buf.at[pl.ds(0, half - 1)])

    @pl.when(owns_rest)
    def _():
        to_plane(KC, lambda peer, k: kc_buf.at[owner], lambda peer, k: kc_buf.at[owner])

    @pl.when(jnp.logical_not(owns_gram))
    def _():
        arrived(KG, kc_buf.at[pl.ds(0, half)])

    inverse = inverse_factor(kc_buf[half:].reshape(64, 128)[:, :64])
    v_t = mul(inverse, clean_t)
    v_leaf_t[...] = v_t[:, :leaf_count]
    ends = jnp.concatenate([v_t[:, leaf_count:], jnp.zeros((64, 112), F32)], axis=1)
    ends = jnp.transpose(ends)
    v_sep[...] = ends[0:8]
    v_root[...] = ends[8:16]

    @pl.when(owns_rest)
    def _():
        arrived(KC, kc_buf.at[pl.ds(0, half - 1)])

    @pl.when(jnp.logical_not(owns_rest))
    def _():
        arrived(KC, kc_buf.at[pl.ds(0, half)])

    both = mul(inverse, kc_buf[:half].reshape(64, 128))
    red_g[...] = mul(both[:, :64], inverse, NT)
    red_c[...] = mul(both[:, 64:], inverse, NT)

    sent(A, a_rcv)
    sent(B, b_buf.at[others])
    sent(SL, sl_buf.at[others])
    sent(SU, su_buf.at[others])
    sent(SP, sp_buf.at[others])
    sent(SS, ss_buf.at[others])
    sent(L, l_buf.at[others_z])
    sent(U, u_buf.at[others_z])
    sent(RZ, rz_buf.at[others_z])
    sent(D, d_buf.at[:, others])
    sent(E_, e_buf.at[:, others])
    sent(N1, n_rcv)
    sent(N2, n_buf.at[others])
    sent(N3, m_src.at[others_z])
    sent(N4, m_buf.at[others_z])
    sent(P1, p_rcv)
    sent(P2, pz_buf.at[others_z])
    sent(W1, w_rcv)
    sent(W2, w_buf.at[others])

    @pl.when(owns)
    def _():
        sent(KR, k_src.at[pl.ds(0, n_own - 1)])
        sent(KZ, kz_buf.at[others_z])

    @pl.when(jnp.logical_not(owns))
    def _():
        sent(KR, k_src)

    @pl.when(owns_gram)
    def _():
        sent(KG, k_rcv)

    @pl.when(owns_rest)
    def _():
        sent(KC, k_rcv)


def shards(
    n_outer,
    n_inner,
    b_leaf,
    b_sep,
    b_root,
    leaf_linv,
    leaf_uinv,
    leaf_lower,
    leaf_upper,
    sep_rows,
    sep_linv,
    sep_uinv,
    sep_lower,
    sep_upper,
    root_linv,
    root_uinv,
    basis_leaf,
    basis_sep,
    basis_root,
    g_blocks,
    c_blocks,
    block_cols,
):
    nodes, ports = b_leaf.shape
    basis = basis_leaf.shape[1]
    root = root_linv.shape[1]
    width = n_inner * 8
    half = n_outer // 2
    per = PIECES_P // n_inner
    n_own = min(PIECES_K, n_inner)
    per_k = PIECES_K // n_own
    vmem = pl.BlockSpec(memory_space=pltpu.VMEM)
    hbm = pl.BlockSpec(memory_space=pltpu.HBM)
    scratch = [
        (n_inner, 8, 128),
        (n_inner - 1, 8, 128),
        (n_inner, 8, 128),
        (n_inner, 8, width),
        (n_inner, 8, width),
        (n_inner, 8, 128),
        (n_inner, 8, 128),
        (n_inner, 8, 128),
        (n_inner, 8, 128),
        (n_outer, 8, root),
        (n_outer, 8, root),
        (n_outer, n_outer * 4, 128),
        (half, n_inner, 8, 128),
        (half, n_inner, 8, 128),
        (n_inner, 8, basis),
        (n_inner - 1, 8, basis),
        (n_inner, 8, basis),
        (n_outer, 8, basis),
        (n_outer, 8, basis),
        (n_outer, 8, basis),
        (n_inner, per, 8, 128),
        (n_inner - 1, per, 8, 128),
        (n_outer, per, 8, 128),
        (n_inner, 1 + per, 8, 128),
        (n_inner - 1, 1 + per, 8, 128),
        (n_inner, 1 + per, 8, 128),
        (n_own, per_k, 8, 128),
        (n_inner - 1, per_k, 8, 128),
        (n_outer, per_k, 8, 128),
        (n_own, per_k, 8, 128),
        (nodes + 16, basis),
        (nodes, nodes),
        (nodes, nodes),
    ]
    b_leaf_t, sep_lower_t = b_leaf.T, sep_lower.T
    kept = (
        b_leaf_t,
        b_sep,
        b_root,
        leaf_linv,
        leaf_uinv,
        leaf_lower,
        leaf_upper,
        sep_rows,
        sep_lower_t,
        sep_upper,
        g_blocks,
        c_blocks,
        block_cols,
    )
    outs = [(ports, nodes), (8, ports), (8, ports), (ports, basis), (ports, ports), (ports, ports)]
    v_leaf_t, v_sep, v_root, coef_t, red_g, red_c = pl.pallas_call(
        functools.partial(kernel, n_outer, n_inner),
        out_shape=[jax.ShapeDtypeStruct(s, F32) for s in outs],
        in_specs=[hbm] * 20,
        out_specs=[vmem] * 6,
        scratch_shapes=[pltpu.VMEM(s, F32) for s in scratch]
        + [pltpu.VMEM(x.shape, x.dtype) for x in kept]
        + [pltpu.SemaphoreType.DMA((n,)) for n in (23, 23, 20)],
        compiler_params=pltpu.CompilerParams(
            collective_id=0, has_side_effects=True, vmem_limit_bytes=64 * 2**20
        ),
    )(
        b_leaf_t,
        b_sep,
        b_root,
        leaf_linv,
        leaf_uinv,
        leaf_lower,
        leaf_upper,
        sep_rows,
        sep_linv,
        sep_uinv,
        sep_lower_t,
        sep_upper,
        root_linv,
        root_uinv,
        basis_leaf,
        basis_sep,
        basis_root,
        g_blocks,
        c_blocks,
        block_cols,
    )
    return v_leaf_t.T, v_sep, v_root, coef_t.T, red_g, red_c


def solution(mesh):
    rows = P(("outer", "inner"), None)
    return jax.shard_map(
        functools.partial(shards, mesh.shape["outer"], mesh.shape["inner"]),
        mesh=mesh,
        in_specs=(rows,) * 10 + (P(None, ("outer", "inner")),) + (rows,) * 9,
        out_specs=(rows, rows, rows, P(), P(), P()),
        check_vma=False,
    )
```

```python
import functools

import jax
import jax.numpy as jnp
from jax import lax
from jax.experimental import pallas as pl
from jax.experimental.pallas import tpu as pltpu
from jax.sharding import PartitionSpec as P

MESH = pl.DeviceIdType.MESH
F32 = jnp.float32
NN = ((1,), (0,))
NT = ((1,), (1,))
TN = ((0,), (0,))
PIECES_P = 32
PIECES_K = 16


def mul(left, right, dims=NN):
    return lax.dot_general(
        left, right, (dims, ((), ())), precision=lax.Precision.HIGHEST, preferred_element_type=F32
    )


def wide(block):
    return jnp.concatenate([block, jnp.zeros_like(block)], axis=1)


def folded(block):
    half = block.shape[0] // 2
    return jnp.concatenate([block[:half], block[half:]], axis=1)


def unfolded_product(left, both):
    half = left.shape[1] // 2
    upper = mul(left[:, :half], both)
    lower = mul(left[:, half:], both)
    return upper[:, :64] + lower[:, 64:]


def inverse_factor(gram):
    row_ids = lax.broadcasted_iota(jnp.int32, (64, 64), 0)
    col_ids = lax.broadcasted_iota(jnp.int32, (64, 64), 1)
    start = jnp.concatenate([gram, (row_ids == col_ids).astype(F32)], axis=1)
    groups = tuple(start[8 * a : 8 * a + 8] for a in range(8))

    def spread(block, k):
        return jnp.broadcast_to(block[:, k : k + 1], (block.shape[0], 128))

    def panel(p, groups):
        head = groups[0]
        rows = [head[j : j + 1] for j in range(8)]
        corner = [[spread(rows[j], k) if k >= j else None for k in range(8)] for j in range(8)]
        scaled, factors = [], []
        for j in range(8):
            inverse = 1.0 / corner[j][j]
            scaled.append(rows[j] * inverse)
            factors.append([corner[j][t] * inverse if t > j else None for t in range(8)])
            for t in range(j + 1, 8):
                rows[t] = rows[t] - factors[j][t] * rows[j]
                for k in range(t, 8):
                    corner[t][k] = corner[t][k] - factors[j][t] * corner[j][k]
        done = [rows[j] * lax.rsqrt(corner[j][j]) for j in range(8)]
        turned = []
        for a in range(1, 8):
            live = jnp.where(a + p < 8, 1.0, 0.0).astype(F32)
            columns = []
            total = jnp.zeros((8, 128), F32)
            for j in range(8):
                column = spread(groups[a], j)
                for t in range(j):
                    column = column - columns[t] * factors[t][j]
                columns.append(column)
                total = total + column * scaled[j]
            turned.append(groups[a] - live * total)
        turned.append(jnp.concatenate(done, axis=0))
        return tuple(pltpu.roll(x, 120, 1) for x in turned)

    groups = lax.fori_loop(0, 8, panel, groups)
    return jnp.concatenate(groups, axis=0)[:, :64]


def by_owner(columns, n_outer, n_inner, out_ref):
    if n_inner * 8 != 256:
        moved = columns.reshape(8, n_outer, n_inner, 8).transpose(2, 0, 1, 3).reshape(n_inner, 8, n_outer * 8)
        out_ref[...] = jnp.concatenate(
            [moved, jnp.zeros((n_inner, 8, 128 - n_outer * 8), F32)], axis=2
        )
        return
    lane_group = lax.broadcasted_iota(jnp.int32, (8, 128), 1) // 8
    for m in range(2):
        shifted = []
        for o in range(n_outer):
            at = o * 256 + m * 128
            piece = columns[:, at : at + 128]
            shifted.append(pltpu.roll(piece, o * 8, 1) if o else piece)
        for ii in range(16):
            total = shifted[0]
            for o in range(1, n_outer):
                total = jnp.where(lane_group == (ii + o) % 16, shifted[o], total)
            out_ref[16 * m + ii] = pltpu.roll(total, 128 - ii * 8, 1) if ii else total


def kernel(
    n_outer,
    n_inner,
    h_b_t,
    h_b_sep,
    h_b_root,
    h_leaf_linv,
    h_leaf_uinv,
    h_leaf_lower,
    h_leaf_upper,
    h_sep_rows,
    h_sep_linv,
    h_sep_uinv,
    h_sep_lower_t,
    h_sep_upper,
    h_root_linv,
    h_root_uinv,
    h_basis_leaf,
    h_basis_sep,
    h_basis_root,
    h_g_blocks,
    h_c_blocks,
    h_block_cols,
    o_v_leaf_t,
    o_v_sep,
    o_v_root,
    o_coef_t,
    o_red_g,
    o_red_c,
    a_src,
    a_rcv,
    b_buf,
    sl_buf,
    su_buf,
    sp_src,
    sp_buf,
    ss_src,
    ss_buf,
    l_buf,
    u_buf,
    rz_buf,
    d_buf,
    e_buf,
    n_src,
    n_sib,
    n_pair,
    n_rcv,
    n_buf,
    m_src,
    m_rcv,
    m_buf,
    p_src,
    p_rcv,
    pz_buf,
    w_src,
    w_rcv,
    w_buf,
    k_src,
    k_rcv,
    kz_buf,
    kc_buf,
    q_all,
    hg,
    hc,
    b_t,
    b_sep,
    b_root,
    leaf_linv,
    leaf_uinv,
    leaf_lower,
    leaf_upper,
    sep_rows,
    sep_lower_t,
    sep_upper,
    g_blocks,
    c_blocks,
    block_cols,
    v_leaf_t,
    v_sep,
    v_root,
    coef_t,
    red_g,
    red_c,
    send,
    recv,
    here,
    out,
):
    g = lax.axis_index("outer")
    i = lax.axis_index("inner")
    rb = n_outer * 8
    n_own = kc_buf.shape[0]
    stride = n_inner // n_own
    leaf_count = h_basis_leaf.shape[0]
    nodes = float(n_outer * n_inner * (leaf_count + 16))
    A, B, SL, SU, SP, SS, L, U, RZ, D, E_, N1, N2, N3, N4, P1, P2, W1, W2, KR, KZ, KG, KC, SLB, SUB, N1A, N2B = range(27)

    def to_plane(phase, src, dst):
        def one(k, carry):
            peer = lax.rem(i + k, n_inner)
            pltpu.make_async_remote_copy(
                src_ref=src(peer, k),
                dst_ref=dst(peer, k),
                send_sem=send.at[phase],
                recv_sem=recv.at[phase],
                device_id=(g, peer),
                device_id_type=MESH,
            ).start()
            return carry

        lax.fori_loop(1, n_inner, one, 0)

    pairs = n_inner // 2
    chip, core = i // 2, lax.rem(i, 2)
    sibling = i + 1 - 2 * core

    def to_same_core(phase, src, dst):
        def one(k, carry):
            peer = lax.rem(chip + k, pairs)
            pltpu.make_async_remote_copy(
                src_ref=src(peer),
                dst_ref=dst(k),
                send_sem=send.at[phase],
                recv_sem=recv.at[phase],
                device_id=(g, 2 * peer + core),
                device_id_type=MESH,
            ).start()
            return carry

        lax.fori_loop(1, pairs, one, 0)

    def to_sibling(phase, src, dst):
        pltpu.make_async_remote_copy(
            src_ref=src,
            dst_ref=dst,
            send_sem=send.at[phase],
            recv_sem=recv.at[phase],
            device_id=(g, sibling),
            device_id_type=MESH,
        ).start()

    def to_column(phase, src, dst):
        def one(k, carry):
            peer = lax.rem(g + k, n_outer)
            pltpu.make_async_remote_copy(
                src_ref=src(peer),
                dst_ref=dst,
                send_sem=send.at[phase],
                recv_sem=recv.at[phase],
                device_id=(peer, i),
                device_id_type=MESH,
            ).start()
            return carry

        lax.fori_loop(1, n_outer, one, 0)

    def arrived(phase, like):
        pltpu.make_async_copy(like, like, recv.at[phase]).wait()

    def sent(phase, like):
        pltpu.make_async_copy(like, like, send.at[phase]).wait()

    others = pl.ds(0, n_inner - 1)
    others_p = pl.ds(0, pairs - 1)
    others_z = pl.ds(0, n_outer - 1)

    own_slots = {
        "b_t": (h_b_t, b_t),
        "leaf_linv": (h_leaf_linv, leaf_linv),
        "leaf_lower": (h_leaf_lower, leaf_lower),
        "sep_rows": (h_sep_rows, sep_rows),
        "sep_lower_t": (h_sep_lower_t, sep_lower_t),
        "sep_linv": (h_sep_linv, sl_buf.at[chip, core]),
        "root_linv": (h_root_linv, l_buf.at[g]),
        "root_uinv": (h_root_uinv, u_buf.at[g]),
        "sep_uinv": (h_sep_uinv, su_buf.at[chip, core]),
        "b_sep": (h_b_sep, b_sep),
        "leaf_uinv": (h_leaf_uinv, leaf_uinv),
        "leaf_upper": (h_leaf_upper, leaf_upper),
        "b_root": (h_b_root, b_root),
        "sep_upper": (h_sep_upper, sep_upper),
        "g_blocks": (h_g_blocks, g_blocks),
        "c_blocks": (h_c_blocks, c_blocks),
        "block_cols": (h_block_cols, block_cols),
        "basis_leaf": (h_basis_leaf, q_all.at[pl.ds(0, leaf_count)]),
        "basis_sep": (h_basis_sep, q_all.at[pl.ds(leaf_count, 8)]),
        "basis_root": (h_basis_root, q_all.at[pl.ds(leaf_count + 8, 8)]),
    }
    loads = {
        name: pltpu.make_async_copy(src, dst, here.at[n])
        for n, (name, (src, dst)) in enumerate(own_slots.items())
    }
    stores = [
        pltpu.make_async_copy(src, dst, out.at[n])
        for n, (src, dst) in enumerate(
            (
                (v_leaf_t, o_v_leaf_t),
                (v_sep, o_v_sep),
                (v_root, o_v_root),
                (coef_t, o_coef_t),
                (red_g, o_red_g),
                (red_c, o_red_c),
            )
        )
    ]
    for load in loads.values():
        load.start()

    def loaded(*names):
        for name in names:
            loads[name].wait()

    barrier = pltpu.get_barrier_semaphore()

    def greet_plane(k, carry):
        pl.semaphore_signal(
            barrier, inc=1, device_id=(g, lax.rem(i + k, n_inner)), device_id_type=MESH
        )
        return carry

    def greet_column(k, carry):
        pl.semaphore_signal(
            barrier, inc=1, device_id=(lax.rem(g + k, n_outer), i), device_id_type=MESH
        )
        return carry

    lax.fori_loop(1, n_inner, greet_plane, 0)
    lax.fori_loop(1, n_outer, greet_column, 0)

    loaded("b_t", "leaf_linv", "leaf_lower", "sep_rows")
    width = n_inner * 8
    couples = sep_rows.shape[1]
    sel_t = (
        lax.broadcasted_iota(jnp.int32, (width, couples), 0)
        == jnp.broadcast_to(sep_rows[...], (width, couples))
    ).astype(F32)
    y_t = mul(b_t[...], leaf_linv[...], NT)
    contrib_t = mul(y_t, leaf_lower[...], NT)
    update = mul(sel_t, contrib_t, NT)
    a_src[...] = wide(update).reshape(n_inner, 8, 128)
    loaded("sep_linv", "root_linv", "root_uinv", "sep_uinv", "b_sep")

    pl.semaphore_wait(barrier, n_inner + n_outer - 2)

    to_plane(A, lambda peer, k: a_src.at[peer], lambda peer, k: a_rcv.at[k - 1])
    to_same_core(SL, lambda peer: sl_buf.at[chip, core], lambda k: sl_buf.at[chip, core])
    to_column(L, lambda peer: l_buf.at[g], l_buf.at[g])
    loaded("sep_lower_t", "sep_upper")
    by_owner(sep_lower_t[...], n_outer, n_inner, sp_src)
    sp_buf[i] = sp_src[i]
    to_plane(SP, lambda peer, k: sp_src.at[peer], lambda peer, k: sp_buf.at[i])
    by_owner(sep_upper[...], n_outer, n_inner, ss_src)
    ss_buf[i] = ss_src[i]

    loaded("leaf_uinv", "leaf_upper", "b_root", "basis_leaf", "basis_sep", "basis_root")
    uy_t = mul(y_t, leaf_uinv[...], NT)
    coupling = mul(leaf_uinv[...], mul(leaf_upper[...], sel_t, NT))
    n_src[...] = mul(coupling, q_all[:leaf_count, :], TN).reshape(n_src.shape)
    to_sibling(N1A, n_src.at[:, 1 - core], n_sib)

    arrived(A, a_rcv)
    b_buf[i] = wide(b_sep[...]) - (a_src[i] + jnp.sum(a_rcv[...], axis=0))
    to_plane(B, lambda peer, k: b_buf.at[i], lambda peer, k: b_buf.at[i])
    arrived(N1A, n_sib)
    n_pair[...] = n_src[:, core] + n_sib[...]
    to_same_core(N1, lambda peer: n_pair.at[peer], lambda k: n_rcv.at[k - 1])
    arrived(SL, sl_buf.at[others_p, 0])
    to_sibling(SLB, sl_buf.at[:, core], sl_buf.at[:, core])
    to_same_core(SU, lambda peer: su_buf.at[chip, core], lambda k: su_buf.at[chip, core])
    to_plane(SS, lambda peer, k: ss_src.at[peer], lambda peer, k: ss_buf.at[i])

    arrived(SLB, sl_buf.at[:, 0])
    arrived(SP, sp_buf.at[others])
    sep_inverse = sl_buf[...].reshape(width, width)
    to_root = mul(sp_buf[...].reshape(width, 128)[:, :rb], sep_inverse, TN)

    arrived(B, b_buf.at[others])
    rhs_sep = b_buf[...].reshape(width, 128)
    part = mul(to_root, rhs_sep[:, :64])
    mine = lax.broadcasted_iota(jnp.int32, (rb, 64), 0) // 8 == g
    own = jnp.where(mine, jnp.concatenate([b_root[...]] * n_outer, axis=0), 0.0)
    rz_buf[g] = folded(own - part)
    to_column(RZ, lambda peer: rz_buf.at[g], rz_buf.at[g])
    to_column(U, lambda peer: u_buf.at[g], u_buf.at[g])

    arrived(N1, n_rcv)
    mine_n = n_pair[chip] + jnp.sum(n_rcv[...], axis=0)
    n_buf[chip, core] = q_all[leaf_count : leaf_count + 8, :] - mine_n
    to_same_core(N2, lambda peer: n_buf.at[chip, core], lambda k: n_buf.at[chip, core])
    arrived(SU, su_buf.at[others_p, 0])
    to_sibling(SUB, su_buf.at[:, core], su_buf.at[:, core])

    def root_gather(phase, buf, block):
        buf[:, i] = block.reshape(n_outer // 2, 8, 128)
        to_plane(phase, lambda peer, k: buf.at[:, i], lambda peer, k: buf.at[:, i])

    def root_value(phase, buf):
        arrived(phase, buf.at[:, others])
        return buf[...].reshape(n_outer // 2 * n_inner * 8, 128)

    arrived(RZ, rz_buf.at[others_z])
    root_gather(D, d_buf, jnp.sum(rz_buf[...], axis=0))

    y_own = mul(sl_buf[chip, core], rhs_sep[:, :64])
    sep_y_t = mul(jnp.transpose(rhs_sep)[:64], sep_inverse, NT)
    arrived(SUB, su_buf.at[:, 0])
    sep_upper_inverse = su_buf[...].reshape(width, width)
    from_sep = mul(coupling, sep_upper_inverse)
    start_t = jnp.concatenate(
        [uy_t - mul(sep_y_t, from_sep, NT), mul(sep_y_t, su_buf[chip, core], NT)], axis=1
    )
    proj_t = mul(start_t, q_all[: leaf_count + 8, :])
    per = PIECES_P // n_inner
    for t in range(PIECES_P):
        r, c = t // 4, t % 4
        p_src[t // per, t % per] = proj_t[8 * r : 8 * r + 8, 128 * c : 128 * c + 128]
    to_plane(P1, lambda peer, k: p_src.at[peer], lambda peer, k: p_rcv.at[k - 1])

    arrived(N2, n_buf.at[others_p, 0])
    to_sibling(N2B, n_buf.at[:, core], n_buf.at[:, core])
    arrived(SS, ss_buf.at[others])
    sep_by_root = ss_buf[...].reshape(width, 128)[:, :rb]
    arrived(N2B, n_buf.at[:, 0])
    m_src[...] = mul(
        mul(sep_upper_inverse, sep_by_root), n_buf[...].reshape(width, n_buf.shape[3]), TN
    ).reshape(m_src.shape)
    m_rcv[g] = m_src[g]
    to_column(N3, lambda peer: m_src.at[peer], m_rcv.at[g])

    arrived(L, l_buf.at[others_z])
    lower_rows = l_buf[...].reshape(rb, l_buf.shape[2])
    y_root = unfolded_product(lower_rows, root_value(D, d_buf))
    root_gather(E_, e_buf, folded(y_root))

    arrived(P1, p_rcv)
    pz_buf[g] = p_src[i] + jnp.sum(p_rcv[...], axis=0)
    to_column(P2, lambda peer: pz_buf.at[g], pz_buf.at[g])

    loaded("g_blocks", "c_blocks", "block_cols")
    size = g_blocks.shape[1]
    stored = block_cols.shape[1]
    for r in range(2):
        for c in range(2):
            for blocks, whole in ((g_blocks, hg), (c_blocks, hc)):
                total = jnp.zeros((size, size), F32)
                for w in range(stored):
                    at = (r * stored + w) * size
                    weight = (block_cols[r : r + 1, w : w + 1] == c).astype(F32)
                    total = total + weight * blocks[at : at + size, :]
                whole[r * size : (r + 1) * size, c * size : (c + 1) * size] = total

    arrived(N3, m_rcv.at[others_z])
    m_buf[g] = jnp.sum(m_rcv[...], axis=0) - q_all[leaf_count + 8 : leaf_count + 16, :]
    to_column(N4, lambda peer: m_buf.at[g], m_buf.at[g])
    arrived(P2, pz_buf.at[others_z])
    proj_start = jnp.sum(pz_buf[...], axis=0)

    arrived(U, u_buf.at[others_z])
    upper_rows = u_buf[...].reshape(rb, u_buf.shape[2])
    x_root = unfolded_product(upper_rows, root_value(E_, e_buf))

    sep_part = wide(mul(sep_by_root, x_root)).reshape(n_inner, 8, 128)
    arrived(N4, m_buf.at[others_z])
    proj_t = mul(x_root, m_buf[...].reshape(rb, m_buf.shape[2]), TN)
    w_src[:, 0] = sep_part
    for t in range(PIECES_P):
        r, c = t // 4, t % 4
        w_src[t // per, 1 + t % per] = proj_t[8 * r : 8 * r + 8, 128 * c : 128 * c + 128]
    to_plane(W1, lambda peer, k: w_src.at[peer], lambda peer, k: w_rcv.at[k - 1])
    row_ids = lax.broadcasted_iota(jnp.int32, (8, rb), 0)
    col_ids = lax.broadcasted_iota(jnp.int32, (8, rb), 1)
    pick = (col_ids == row_ids + 8 * g).astype(F32)
    x_root_t = mul(x_root, pick, ((0,), (1,)))
    arrived(W1, w_rcv)
    moved = w_src[i] + jnp.sum(w_rcv[...], axis=0)
    w_buf[i, 0] = wide(y_own) - moved[0]
    w_buf[i, pl.ds(1, per)] = (proj_start - moved[1:]) / nodes
    to_plane(W2, lambda peer, k: w_buf.at[i], lambda peer, k: w_buf.at[i])
    arrived(W2, w_buf.at[others])

    z_t = jnp.transpose(w_buf[:, 0].reshape(width, 128))[:64]
    x_leaf_t = uy_t - mul(z_t, from_sep, NT)
    x_sep_t = mul(z_t, su_buf[chip, core], NT)
    x_t = jnp.concatenate([x_leaf_t, x_sep_t, x_root_t], axis=1)
    coefs = jnp.concatenate(
        [
            jnp.concatenate(
                [w_buf[(4 * r + c) // per, 1 + (4 * r + c) % per] for c in range(4)], axis=1
            )
            for r in range(8)
        ],
        axis=0,
    )
    clean_t = x_t - mul(coefs, q_all[...], NT)

    per_k = PIECES_K // n_own
    half = n_own // 2
    owner = i // stride
    owns = lax.rem(i, stride) == 0
    owns_gram = jnp.logical_and(owns, owner >= half)
    owns_rest = jnp.logical_and(owns, owner < half)

    def to_owners(first):
        def one(k, carry):
            peer = lax.rem(i + k, n_inner)
            at = peer // stride

            @pl.when(jnp.logical_and(lax.rem(peer, stride) == 0, at // half == first // half))
            def _():
                pltpu.make_async_remote_copy(
                    src_ref=k_src.at[at],
                    dst_ref=k_rcv.at[k - 1],
                    send_sem=send.at[KR],
                    recv_sem=recv.at[KR],
                    device_id=(g, peer),
                    device_id_type=MESH,
                ).start()

            return carry

        lax.fori_loop(1, n_inner, one, 0)

    k_src[half:] = wide(mul(clean_t, clean_t, NT)).reshape(half, per_k, 8, 128)
    to_owners(half)
    clean_leaf_t = clean_t[:, :leaf_count]
    coef_t[...] = coefs
    stores[3].start()
    g_part = mul(mul(clean_leaf_t, hg[...]), clean_leaf_t, NT)
    c_part = mul(mul(clean_leaf_t, hc[...]), clean_leaf_t, NT)
    k_src[:half] = jnp.concatenate([g_part, c_part], axis=1).reshape(half, per_k, 8, 128)
    to_owners(0)

    @pl.when(owns)
    def _():
        arrived(KR, k_rcv)
        kz_buf[g] = k_src[owner] + jnp.sum(k_rcv[...], axis=0)
        to_column(KZ, lambda peer: kz_buf.at[g], kz_buf.at[g])
        arrived(KZ, kz_buf.at[others_z])
        kc_buf[owner] = jnp.sum(kz_buf[...], axis=0) / nodes

    @pl.when(owns_gram)
    def _():
        to_plane(KG, lambda peer, k: kc_buf.at[owner], lambda peer, k: kc_buf.at[owner])
        arrived(KG, kc_buf.at[pl.ds(0, half - 1)])

    @pl.when(owns_rest)
    def _():
        to_plane(KC, lambda peer, k: kc_buf.at[owner], lambda peer, k: kc_buf.at[owner])

    @pl.when(jnp.logical_not(owns_gram))
    def _():
        arrived(KG, kc_buf.at[pl.ds(0, half)])

    inverse = inverse_factor(kc_buf[half:].reshape(64, 128)[:, :64])
    v_t = mul(inverse, clean_t)
    v_leaf_t[...] = v_t[:, :leaf_count]
    stores[0].start()
    ends = jnp.concatenate([v_t[:, leaf_count:], jnp.zeros((64, 112), F32)], axis=1)
    ends = jnp.transpose(ends)
    v_sep[...] = ends[0:8]
    v_root[...] = ends[8:16]
    stores[1].start()
    stores[2].start()

    @pl.when(owns_rest)
    def _():
        arrived(KC, kc_buf.at[pl.ds(0, half - 1)])

    @pl.when(jnp.logical_not(owns_rest))
    def _():
        arrived(KC, kc_buf.at[pl.ds(0, half)])

    both = mul(inverse, kc_buf[:half].reshape(64, 128))
    red_g[...] = mul(both[:, :64], inverse, NT)
    stores[4].start()
    red_c[...] = mul(both[:, 64:], inverse, NT)
    stores[5].start()

    sent(A, a_rcv)
    sent(B, b_buf.at[others])
    sent(SL, sl_buf.at[others_p, 0])
    sent(SU, su_buf.at[others_p, 0])
    sent(SLB, sl_buf.at[:, 0])
    sent(SUB, su_buf.at[:, 0])
    sent(SP, sp_buf.at[others])
    sent(SS, ss_buf.at[others])
    sent(L, l_buf.at[others_z])
    sent(U, u_buf.at[others_z])
    sent(RZ, rz_buf.at[others_z])
    sent(D, d_buf.at[:, others])
    sent(E_, e_buf.at[:, others])
    sent(N1A, n_sib)
    sent(N1, n_rcv)
    sent(N2, n_buf.at[others_p, 0])
    sent(N2B, n_buf.at[:, 0])
    sent(N3, m_src.at[others_z])
    sent(N4, m_buf.at[others_z])
    sent(P1, p_rcv)
    sent(P2, pz_buf.at[others_z])
    sent(W1, w_rcv)
    sent(W2, w_buf.at[others])

    @pl.when(owns)
    def _():
        sent(KR, k_src.at[pl.ds(0, n_own - 1)])
        sent(KZ, kz_buf.at[others_z])

    @pl.when(jnp.logical_not(owns))
    def _():
        sent(KR, k_src)

    @pl.when(owns_gram)
    def _():
        sent(KG, k_rcv)

    @pl.when(owns_rest)
    def _():
        sent(KC, k_rcv)

    for store in stores:
        store.wait()


def hand_over(count, *refs):
    src, dst, held = refs[:count], refs[count : 2 * count], refs[2 * count : 3 * count]
    come, go = refs[3 * count :]
    ins = [pltpu.make_async_copy(src[n], held[n], come.at[n]) for n in range(count)]
    outs = [pltpu.make_async_copy(held[n], dst[n], go.at[n]) for n in range(count)]
    for copy in ins:
        copy.start()
    for n in range(count):
        ins[n].wait()
        outs[n].start()
    for copy in outs:
        copy.wait()


def shards(
    n_outer,
    n_inner,
    b_leaf,
    b_sep,
    b_root,
    leaf_linv,
    leaf_uinv,
    leaf_lower,
    leaf_upper,
    sep_rows,
    sep_linv,
    sep_uinv,
    sep_lower,
    sep_upper,
    root_linv,
    root_uinv,
    basis_leaf,
    basis_sep,
    basis_root,
    g_blocks,
    c_blocks,
    block_cols,
):
    nodes, ports = b_leaf.shape
    basis = basis_leaf.shape[1]
    root = root_linv.shape[1]
    width = n_inner * 8
    half = n_outer // 2
    per = PIECES_P // n_inner
    n_own = min(PIECES_K, n_inner)
    per_k = PIECES_K // n_own
    hbm = pl.BlockSpec(memory_space=pltpu.HBM)
    scratch = [
        (n_inner, 8, 128),
        (n_inner - 1, 8, 128),
        (n_inner, 8, 128),
        (n_inner // 2, 2, 8, width),
        (n_inner // 2, 2, 8, width),
        (n_inner, 8, 128),
        (n_inner, 8, 128),
        (n_inner, 8, 128),
        (n_inner, 8, 128),
        (n_outer, 8, root),
        (n_outer, 8, root),
        (n_outer, n_outer * 4, 128),
        (half, n_inner, 8, 128),
        (half, n_inner, 8, 128),
        (n_inner // 2, 2, 8, basis),
        (n_inner // 2, 8, basis),
        (n_inner // 2, 8, basis),
        (n_inner // 2 - 1, 8, basis),
        (n_inner // 2, 2, 8, basis),
        (n_outer, 8, basis),
        (n_outer, 8, basis),
        (n_outer, 8, basis),
        (n_inner, per, 8, 128),
        (n_inner - 1, per, 8, 128),
        (n_outer, per, 8, 128),
        (n_inner, 1 + per, 8, 128),
        (n_inner - 1, 1 + per, 8, 128),
        (n_inner, 1 + per, 8, 128),
        (n_own, per_k, 8, 128),
        (n_inner - 1, per_k, 8, 128),
        (n_outer, per_k, 8, 128),
        (n_own, per_k, 8, 128),
        (nodes + 16, basis),
        (nodes, nodes),
        (nodes, nodes),
    ]
    b_leaf_t, sep_lower_t = b_leaf.T, sep_lower.T
    kept = (
        b_leaf_t,
        b_sep,
        b_root,
        leaf_linv,
        leaf_uinv,
        leaf_lower,
        leaf_upper,
        sep_rows,
        sep_lower_t,
        sep_upper,
        g_blocks,
        c_blocks,
        block_cols,
    )
    outs = [(ports, nodes), (8, ports), (8, ports), (ports, basis), (ports, ports), (ports, ports)]
    results = pl.pallas_call(
        functools.partial(kernel, n_outer, n_inner),
        out_shape=[jax.ShapeDtypeStruct(s, F32) for s in outs],
        in_specs=[hbm] * 20,
        out_specs=[hbm] * 6,
        scratch_shapes=[pltpu.VMEM(s, F32) for s in scratch]
        + [pltpu.VMEM(x.shape, x.dtype) for x in kept]
        + [pltpu.VMEM(s, F32) for s in outs]
        + [pltpu.SemaphoreType.DMA((n,)) for n in (27, 27, 20, 6)],
        compiler_params=pltpu.CompilerParams(
            collective_id=0, has_side_effects=True, vmem_limit_bytes=64 * 2**20
        ),
    )(
        b_leaf_t,
        b_sep,
        b_root,
        leaf_linv,
        leaf_uinv,
        leaf_lower,
        leaf_upper,
        sep_rows,
        sep_linv,
        sep_uinv,
        sep_lower_t,
        sep_upper,
        root_linv,
        root_uinv,
        basis_leaf,
        basis_sep,
        basis_root,
        g_blocks,
        c_blocks,
        block_cols,
    )
    v_leaf_t, v_sep, v_root, coef_t, red_g, red_c = pl.pallas_call(
        functools.partial(hand_over, len(outs)),
        out_shape=[jax.ShapeDtypeStruct(s, F32) for s in outs],
        in_specs=[hbm] * 6,
        out_specs=[hbm] * 6,
        scratch_shapes=[pltpu.VMEM(s, F32) for s in outs] + [pltpu.SemaphoreType.DMA((6,))] * 2,
    )(*results)
    return v_leaf_t.T, v_sep, v_root, coef_t.T, red_g, red_c


def solution(mesh):
    rows = P(("outer", "inner"), None)
    return jax.shard_map(
        functools.partial(shards, mesh.shape["outer"], mesh.shape["inner"]),
        mesh=mesh,
        in_specs=(rows,) * 10 + (P(None, ("outer", "inner")),) + (rows,) * 9,
        out_specs=(rows, rows, rows, P(), P(), P()),
        check_vma=False,
    )
```

```python
import functools

import jax
import jax.numpy as jnp
from jax import lax
from jax.experimental import pallas as pl
from jax.experimental.pallas import tpu as pltpu
from jax.sharding import PartitionSpec as P

MESH = pl.DeviceIdType.MESH
F32 = jnp.float32
NN = ((1,), (0,))
NT = ((1,), (1,))
TN = ((0,), (0,))
PIECES_P = 32
PIECES_K = 16


def mul(left, right, dims=NN):
    return lax.dot_general(
        left, right, (dims, ((), ())), precision=lax.Precision.HIGHEST, preferred_element_type=F32
    )


def wide(block):
    return jnp.concatenate([block, jnp.zeros_like(block)], axis=1)


def folded(block):
    half = block.shape[0] // 2
    return jnp.concatenate([block[:half], block[half:]], axis=1)


def unfolded_product(left, both):
    half = left.shape[1] // 2
    upper = mul(left[:, :half], both)
    lower = mul(left[:, half:], both)
    return upper[:, :64] + lower[:, 64:]


def inverse_factor(gram):
    row_ids = lax.broadcasted_iota(jnp.int32, (64, 64), 0)
    col_ids = lax.broadcasted_iota(jnp.int32, (64, 64), 1)
    start = jnp.concatenate([gram, (row_ids == col_ids).astype(F32)], axis=1)
    groups = tuple(start[8 * a : 8 * a + 8] for a in range(8))

    def spread(block, k):
        return jnp.broadcast_to(block[:, k : k + 1], (block.shape[0], 128))

    def panel(p, groups):
        head = groups[0]
        rows = [head[j : j + 1] for j in range(8)]
        corner = [[spread(rows[j], k) if k >= j else None for k in range(8)] for j in range(8)]
        scaled, factors = [], []
        for j in range(8):
            inverse = 1.0 / corner[j][j]
            scaled.append(rows[j] * inverse)
            factors.append([corner[j][t] * inverse if t > j else None for t in range(8)])
            for t in range(j + 1, 8):
                rows[t] = rows[t] - factors[j][t] * rows[j]
                for k in range(t, 8):
                    corner[t][k] = corner[t][k] - factors[j][t] * corner[j][k]
        done = [rows[j] * lax.rsqrt(corner[j][j]) for j in range(8)]
        turned = []
        for a in range(1, 8):
            live = jnp.where(a + p < 8, 1.0, 0.0).astype(F32)
            columns = []
            total = jnp.zeros((8, 128), F32)
            for j in range(8):
                column = spread(groups[a], j)
                for t in range(j):
                    column = column - columns[t] * factors[t][j]
                columns.append(column)
                total = total + column * scaled[j]
            turned.append(groups[a] - live * total)
        turned.append(jnp.concatenate(done, axis=0))
        return tuple(pltpu.roll(x, 120, 1) for x in turned)

    groups = lax.fori_loop(0, 8, panel, groups)
    return jnp.concatenate(groups, axis=0)[:, :64]


def by_owner(columns, n_outer, n_inner, out_ref):
    if n_inner * 8 != 256:
        moved = columns.reshape(8, n_outer, n_inner, 8).transpose(2, 0, 1, 3).reshape(n_inner, 8, n_outer * 8)
        out_ref[...] = jnp.concatenate(
            [moved, jnp.zeros((n_inner, 8, 128 - n_outer * 8), F32)], axis=2
        )
        return
    lane_group = lax.broadcasted_iota(jnp.int32, (8, 128), 1) // 8
    for m in range(2):
        shifted = []
        for o in range(n_outer):
            at = o * 256 + m * 128
            piece = columns[:, at : at + 128]
            shifted.append(pltpu.roll(piece, o * 8, 1) if o else piece)
        for ii in range(16):
            total = shifted[0]
            for o in range(1, n_outer):
                total = jnp.where(lane_group == (ii + o) % 16, shifted[o], total)
            out_ref[16 * m + ii] = pltpu.roll(total, 128 - ii * 8, 1) if ii else total


def kernel(
    n_outer,
    n_inner,
    h_b_t,
    h_b_sep,
    h_b_root,
    h_leaf_linv,
    h_leaf_uinv,
    h_leaf_lower,
    h_leaf_upper,
    h_sep_rows,
    h_sep_linv,
    h_sep_uinv,
    h_sep_lower_t,
    h_sep_upper,
    h_root_linv,
    h_root_uinv,
    h_basis_leaf,
    h_basis_sep,
    h_basis_root,
    h_g_blocks,
    h_c_blocks,
    h_block_cols,
    v_leaf_t,
    v_sep,
    v_root,
    coef_t,
    red_g,
    red_c,
    a_src,
    a_rcv,
    b_buf,
    sl_buf,
    su_buf,
    sp_src,
    sp_buf,
    ss_src,
    ss_buf,
    l_buf,
    u_buf,
    rz_buf,
    d_buf,
    e_buf,
    n_src,
    n_sib,
    n_pair,
    n_rcv,
    n_buf,
    m_src,
    m_rcv,
    m_buf,
    p_src,
    p_rcv,
    pz_buf,
    w_src,
    w_rcv,
    w_buf,
    k_src,
    k_rcv,
    kz_buf,
    kc_buf,
    q_all,
    hg,
    hc,
    b_t,
    b_sep,
    b_root,
    leaf_linv,
    leaf_uinv,
    leaf_lower,
    leaf_upper,
    sep_rows,
    sep_lower_t,
    sep_upper,
    g_blocks,
    c_blocks,
    block_cols,
    send,
    recv,
    here,
    tri_send,
    tri_recv,
):
    g = lax.axis_index("outer")
    i = lax.axis_index("inner")
    rb = n_outer * 8
    n_own = kc_buf.shape[0]
    stride = n_inner // n_own
    leaf_count = h_basis_leaf.shape[0]
    nodes = float(n_outer * n_inner * (leaf_count + 16))
    A, B, SL, SU, SP, SS, L, U, RZ, D, E_, N1, N2, N3, N4, P1, P2, W1, W2, KR, KZ, KG, KC, SLB, SUB, N1A, N2B = range(27)

    def to_plane(phase, src, dst):
        def one(k, carry):
            peer = lax.rem(i + k, n_inner)
            pltpu.make_async_remote_copy(
                src_ref=src(peer, k),
                dst_ref=dst(peer, k),
                send_sem=send.at[phase],
                recv_sem=recv.at[phase],
                device_id=(g, peer),
                device_id_type=MESH,
            ).start()
            return carry

        lax.fori_loop(1, n_inner, one, 0)

    pairs = n_inner // 2
    chip, core = i // 2, lax.rem(i, 2)
    sibling = i + 1 - 2 * core

    def to_same_core(phase, src, dst):
        def one(k, carry):
            peer = lax.rem(chip + k, pairs)
            pltpu.make_async_remote_copy(
                src_ref=src(peer),
                dst_ref=dst(k),
                send_sem=send.at[phase],
                recv_sem=recv.at[phase],
                device_id=(g, 2 * peer + core),
                device_id_type=MESH,
            ).start()
            return carry

        lax.fori_loop(1, pairs, one, 0)

    def to_sibling(phase, src, dst):
        pltpu.make_async_remote_copy(
            src_ref=src,
            dst_ref=dst,
            send_sem=send.at[phase],
            recv_sem=recv.at[phase],
            device_id=(g, sibling),
            device_id_type=MESH,
        ).start()

    def to_column(phase, src, dst):
        def one(k, carry):
            peer = lax.rem(g + k, n_outer)
            pltpu.make_async_remote_copy(
                src_ref=src(peer),
                dst_ref=dst,
                send_sem=send.at[phase],
                recv_sem=recv.at[phase],
                device_id=(peer, i),
                device_id_type=MESH,
            ).start()
            return carry

        lax.fori_loop(1, n_outer, one, 0)

    def arrived(phase, like):
        pltpu.make_async_copy(like, like, recv.at[phase]).wait()

    def sent(phase, like):
        pltpu.make_async_copy(like, like, send.at[phase]).wait()

    others = pl.ds(0, n_inner - 1)
    others_p = pl.ds(0, pairs - 1)
    others_z = pl.ds(0, n_outer - 1)

    own_slots = {
        "b_t": (h_b_t, b_t),
        "leaf_linv": (h_leaf_linv, leaf_linv),
        "leaf_lower": (h_leaf_lower, leaf_lower),
        "sep_rows": (h_sep_rows, sep_rows),
        "sep_lower_t": (h_sep_lower_t, sep_lower_t),
        "sep_linv": (h_sep_linv, sl_buf.at[chip, core]),
        "root_linv": (h_root_linv, l_buf.at[g]),
        "root_uinv": (h_root_uinv, u_buf.at[g]),
        "sep_uinv": (h_sep_uinv, su_buf.at[chip, core]),
        "b_sep": (h_b_sep, b_sep),
        "leaf_uinv": (h_leaf_uinv, leaf_uinv),
        "leaf_upper": (h_leaf_upper, leaf_upper),
        "b_root": (h_b_root, b_root),
        "sep_upper": (h_sep_upper, sep_upper),
        "g_blocks": (h_g_blocks, g_blocks),
        "c_blocks": (h_c_blocks, c_blocks),
        "block_cols": (h_block_cols, block_cols),
        "basis_leaf": (h_basis_leaf, q_all.at[pl.ds(0, leaf_count)]),
        "basis_sep": (h_basis_sep, q_all.at[pl.ds(leaf_count, 8)]),
        "basis_root": (h_basis_root, q_all.at[pl.ds(leaf_count + 8, 8)]),
    }
    loads = {
        name: pltpu.make_async_copy(src, dst, here.at[n])
        for n, (name, (src, dst)) in enumerate(own_slots.items())
    }
    span = n_inner * 8
    for o in range(n_outer):
        if o + 1 < n_outer:
            after = (n_outer - 1 - o) * span
            l_buf[o, :, (o + 1) * span :] = jnp.zeros((8, after), F32)
        if o:
            u_buf[o, :, : o * span] = jnp.zeros((8, o * span), F32)

    def part_of(which, o):
        if which == 0:
            return l_buf.at[o, :, pl.ds(0, (o + 1) * span)]
        return u_buf.at[o, :, pl.ds(o * span, (n_outer - o) * span)]

    def triangle_to_column(which):
        for o in range(n_outer):

            @pl.when(g == o)
            def _(o=o):
                def one(k, carry):
                    pltpu.make_async_remote_copy(
                        src_ref=part_of(which, o),
                        dst_ref=part_of(which, o),
                        send_sem=tri_send.at[which, k],
                        recv_sem=tri_recv.at[which, o],
                        device_id=(lax.rem(g + k, n_outer), i),
                        device_id_type=MESH,
                    ).start()
                    return carry

                lax.fori_loop(1, n_outer, one, 0)

    def triangle_arrived(which):
        for o in range(n_outer):

            @pl.when(g != o)
            def _(o=o):
                part = part_of(which, o)
                pltpu.make_async_copy(part, part, tri_recv.at[which, o]).wait()

    def triangle_sent(which):
        for o in range(n_outer):

            @pl.when(g == o)
            def _(o=o):
                part = part_of(which, o)

                def one(k, carry):
                    pltpu.make_async_copy(part, part, tri_send.at[which, k]).wait()
                    return carry

                lax.fori_loop(1, n_outer, one, 0)

    for load in loads.values():
        load.start()

    def loaded(*names):
        for name in names:
            loads[name].wait()

    barrier = pltpu.get_barrier_semaphore()

    def greet_plane(k, carry):
        pl.semaphore_signal(
            barrier, inc=1, device_id=(g, lax.rem(i + k, n_inner)), device_id_type=MESH
        )
        return carry

    def greet_column(k, carry):
        pl.semaphore_signal(
            barrier, inc=1, device_id=(lax.rem(g + k, n_outer), i), device_id_type=MESH
        )
        return carry

    lax.fori_loop(1, n_inner, greet_plane, 0)
    lax.fori_loop(1, n_outer, greet_column, 0)

    loaded("b_t", "leaf_linv", "leaf_lower", "sep_rows")
    width = n_inner * 8
    couples = sep_rows.shape[1]
    sel_t = (
        lax.broadcasted_iota(jnp.int32, (width, couples), 0)
        == jnp.broadcast_to(sep_rows[...], (width, couples))
    ).astype(F32)
    y_t = mul(b_t[...], leaf_linv[...], NT)
    contrib_t = mul(y_t, leaf_lower[...], NT)
    update = mul(sel_t, contrib_t, NT)
    a_src[...] = wide(update).reshape(n_inner, 8, 128)
    loaded("sep_linv", "root_linv", "root_uinv", "sep_uinv", "b_sep")

    pl.semaphore_wait(barrier, n_inner + n_outer - 2)

    to_plane(A, lambda peer, k: a_src.at[peer], lambda peer, k: a_rcv.at[k - 1])
    to_same_core(SL, lambda peer: sl_buf.at[chip, core], lambda k: sl_buf.at[chip, core])
    triangle_to_column(0)
    loaded("sep_lower_t", "sep_upper")
    by_owner(sep_lower_t[...], n_outer, n_inner, sp_src)
    sp_buf[i] = sp_src[i]
    to_plane(SP, lambda peer, k: sp_src.at[peer], lambda peer, k: sp_buf.at[i])
    by_owner(sep_upper[...], n_outer, n_inner, ss_src)
    ss_buf[i] = ss_src[i]

    loaded("leaf_uinv", "leaf_upper", "b_root", "basis_leaf", "basis_sep", "basis_root")
    uy_t = mul(y_t, leaf_uinv[...], NT)
    coupling = mul(leaf_uinv[...], mul(leaf_upper[...], sel_t, NT))
    n_src[...] = mul(coupling, q_all[:leaf_count, :], TN).reshape(n_src.shape)
    to_sibling(N1A, n_src.at[:, 1 - core], n_sib)

    arrived(A, a_rcv)
    b_buf[i] = wide(b_sep[...]) - (a_src[i] + jnp.sum(a_rcv[...], axis=0))
    to_plane(B, lambda peer, k: b_buf.at[i], lambda peer, k: b_buf.at[i])
    arrived(N1A, n_sib)
    n_pair[...] = n_src[:, core] + n_sib[...]
    to_same_core(N1, lambda peer: n_pair.at[peer], lambda k: n_rcv.at[k - 1])
    arrived(SL, sl_buf.at[others_p, 0])
    to_sibling(SLB, sl_buf.at[:, core], sl_buf.at[:, core])
    to_same_core(SU, lambda peer: su_buf.at[chip, core], lambda k: su_buf.at[chip, core])
    to_plane(SS, lambda peer, k: ss_src.at[peer], lambda peer, k: ss_buf.at[i])

    arrived(SLB, sl_buf.at[:, 0])
    arrived(SP, sp_buf.at[others])
    sep_inverse = sl_buf[...].reshape(width, width)
    to_root = mul(sp_buf[...].reshape(width, 128)[:, :rb], sep_inverse, TN)

    arrived(B, b_buf.at[others])
    rhs_sep = b_buf[...].reshape(width, 128)
    part = mul(to_root, rhs_sep[:, :64])
    mine = lax.broadcasted_iota(jnp.int32, (rb, 64), 0) // 8 == g
    own = jnp.where(mine, jnp.concatenate([b_root[...]] * n_outer, axis=0), 0.0)
    rz_buf[g] = folded(own - part)
    to_column(RZ, lambda peer: rz_buf.at[g], rz_buf.at[g])
    triangle_to_column(1)

    arrived(N1, n_rcv)
    mine_n = n_pair[chip] + jnp.sum(n_rcv[...], axis=0)
    n_buf[chip, core] = q_all[leaf_count : leaf_count + 8, :] - mine_n
    to_same_core(N2, lambda peer: n_buf.at[chip, core], lambda k: n_buf.at[chip, core])
    arrived(SU, su_buf.at[others_p, 0])
    to_sibling(SUB, su_buf.at[:, core], su_buf.at[:, core])

    def root_gather(phase, buf, block):
        buf[:, i] = block.reshape(n_outer // 2, 8, 128)
        to_plane(phase, lambda peer, k: buf.at[:, i], lambda peer, k: buf.at[:, i])

    def root_value(phase, buf):
        arrived(phase, buf.at[:, others])
        return buf[...].reshape(n_outer // 2 * n_inner * 8, 128)

    arrived(RZ, rz_buf.at[others_z])
    root_gather(D, d_buf, jnp.sum(rz_buf[...], axis=0))

    y_own = mul(sl_buf[chip, core], rhs_sep[:, :64])
    sep_y_t = mul(jnp.transpose(rhs_sep)[:64], sep_inverse, NT)
    arrived(SUB, su_buf.at[:, 0])
    sep_upper_inverse = su_buf[...].reshape(width, width)
    from_sep = mul(coupling, sep_upper_inverse)
    start_t = jnp.concatenate(
        [uy_t - mul(sep_y_t, from_sep, NT), mul(sep_y_t, su_buf[chip, core], NT)], axis=1
    )
    proj_t = mul(start_t, q_all[: leaf_count + 8, :])
    per = PIECES_P // n_inner
    for t in range(PIECES_P):
        r, c = t // 4, t % 4
        p_src[t // per, t % per] = proj_t[8 * r : 8 * r + 8, 128 * c : 128 * c + 128]
    to_plane(P1, lambda peer, k: p_src.at[peer], lambda peer, k: p_rcv.at[k - 1])

    arrived(N2, n_buf.at[others_p, 0])
    to_sibling(N2B, n_buf.at[:, core], n_buf.at[:, core])
    arrived(SS, ss_buf.at[others])
    sep_by_root = ss_buf[...].reshape(width, 128)[:, :rb]
    arrived(N2B, n_buf.at[:, 0])
    m_src[...] = mul(
        mul(sep_upper_inverse, sep_by_root), n_buf[...].reshape(width, n_buf.shape[3]), TN
    ).reshape(m_src.shape)
    m_rcv[g] = m_src[g]
    to_column(N3, lambda peer: m_src.at[peer], m_rcv.at[g])

    triangle_arrived(0)
    lower_rows = l_buf[...].reshape(rb, l_buf.shape[2])
    y_root = unfolded_product(lower_rows, root_value(D, d_buf))
    root_gather(E_, e_buf, folded(y_root))

    arrived(P1, p_rcv)
    pz_buf[g] = p_src[i] + jnp.sum(p_rcv[...], axis=0)
    to_column(P2, lambda peer: pz_buf.at[g], pz_buf.at[g])

    loaded("g_blocks", "c_blocks", "block_cols")
    size = g_blocks.shape[1]
    stored = block_cols.shape[1]
    for r in range(2):
        for c in range(2):
            for blocks, whole in ((g_blocks, hg), (c_blocks, hc)):
                total = jnp.zeros((size, size), F32)
                for w in range(stored):
                    at = (r * stored + w) * size
                    weight = (block_cols[r : r + 1, w : w + 1] == c).astype(F32)
                    total = total + weight * blocks[at : at + size, :]
                whole[r * size : (r + 1) * size, c * size : (c + 1) * size] = total

    arrived(N3, m_rcv.at[others_z])
    m_buf[g] = jnp.sum(m_rcv[...], axis=0) - q_all[leaf_count + 8 : leaf_count + 16, :]
    to_column(N4, lambda peer: m_buf.at[g], m_buf.at[g])
    arrived(P2, pz_buf.at[others_z])
    proj_start = jnp.sum(pz_buf[...], axis=0)

    triangle_arrived(1)
    upper_rows = u_buf[...].reshape(rb, u_buf.shape[2])
    x_root = unfolded_product(upper_rows, root_value(E_, e_buf))

    sep_part = wide(mul(sep_by_root, x_root)).reshape(n_inner, 8, 128)
    arrived(N4, m_buf.at[others_z])
    proj_t = mul(x_root, m_buf[...].reshape(rb, m_buf.shape[2]), TN)
    w_src[:, 0] = sep_part
    for t in range(PIECES_P):
        r, c = t // 4, t % 4
        w_src[t // per, 1 + t % per] = proj_t[8 * r : 8 * r + 8, 128 * c : 128 * c + 128]
    to_plane(W1, lambda peer, k: w_src.at[peer], lambda peer, k: w_rcv.at[k - 1])
    row_ids = lax.broadcasted_iota(jnp.int32, (8, rb), 0)
    col_ids = lax.broadcasted_iota(jnp.int32, (8, rb), 1)
    pick = (col_ids == row_ids + 8 * g).astype(F32)
    x_root_t = mul(x_root, pick, ((0,), (1,)))
    arrived(W1, w_rcv)
    moved = w_src[i] + jnp.sum(w_rcv[...], axis=0)
    w_buf[i, 0] = wide(y_own) - moved[0]
    w_buf[i, pl.ds(1, per)] = (proj_start - moved[1:]) / nodes
    to_plane(W2, lambda peer, k: w_buf.at[i], lambda peer, k: w_buf.at[i])
    arrived(W2, w_buf.at[others])

    z_t = jnp.transpose(w_buf[:, 0].reshape(width, 128))[:64]
    x_leaf_t = uy_t - mul(z_t, from_sep, NT)
    x_sep_t = mul(z_t, su_buf[chip, core], NT)
    x_t = jnp.concatenate([x_leaf_t, x_sep_t, x_root_t], axis=1)
    coefs = jnp.concatenate(
        [
            jnp.concatenate(
                [w_buf[(4 * r + c) // per, 1 + (4 * r + c) % per] for c in range(4)], axis=1
            )
            for r in range(8)
        ],
        axis=0,
    )
    clean_t = x_t - mul(coefs, q_all[...], NT)

    per_k = PIECES_K // n_own
    half = n_own // 2
    owner = i // stride
    owns = lax.rem(i, stride) == 0
    owns_gram = jnp.logical_and(owns, owner >= half)
    owns_rest = jnp.logical_and(owns, owner < half)

    def to_owners(first):
        def one(k, carry):
            peer = lax.rem(i + k, n_inner)
            at = peer // stride

            @pl.when(jnp.logical_and(lax.rem(peer, stride) == 0, at // half == first // half))
            def _():
                pltpu.make_async_remote_copy(
                    src_ref=k_src.at[at],
                    dst_ref=k_rcv.at[k - 1],
                    send_sem=send.at[KR],
                    recv_sem=recv.at[KR],
                    device_id=(g, peer),
                    device_id_type=MESH,
                ).start()

            return carry

        lax.fori_loop(1, n_inner, one, 0)

    k_src[half:] = wide(mul(clean_t, clean_t, NT)).reshape(half, per_k, 8, 128)
    to_owners(half)
    clean_leaf_t = clean_t[:, :leaf_count]
    coef_t[...] = coefs
    g_part = mul(mul(clean_leaf_t, hg[...]), clean_leaf_t, NT)
    c_part = mul(mul(clean_leaf_t, hc[...]), clean_leaf_t, NT)
    k_src[:half] = jnp.concatenate([g_part, c_part], axis=1).reshape(half, per_k, 8, 128)
    to_owners(0)

    @pl.when(owns)
    def _():
        arrived(KR, k_rcv)
        kz_buf[g] = k_src[owner] + jnp.sum(k_rcv[...], axis=0)
        to_column(KZ, lambda peer: kz_buf.at[g], kz_buf.at[g])
        arrived(KZ, kz_buf.at[others_z])
        kc_buf[owner] = jnp.sum(kz_buf[...], axis=0) / nodes

    @pl.when(owns_gram)
    def _():
        to_plane(KG, lambda peer, k: kc_buf.at[owner], lambda peer, k: kc_buf.at[owner])
        arrived(KG, kc_buf.at[pl.ds(0, half - 1)])

    @pl.when(owns_rest)
    def _():
        to_plane(KC, lambda peer, k: kc_buf.at[owner], lambda peer, k: kc_buf.at[owner])

    @pl.when(jnp.logical_not(owns_gram))
    def _():
        arrived(KG, kc_buf.at[pl.ds(0, half)])

    inverse = inverse_factor(kc_buf[half:].reshape(64, 128)[:, :64])
    v_t = mul(inverse, clean_t)
    v_leaf_t[...] = v_t[:, :leaf_count]
    ends = jnp.concatenate([v_t[:, leaf_count:], jnp.zeros((64, 112), F32)], axis=1)
    ends = jnp.transpose(ends)
    v_sep[...] = ends[0:8]
    v_root[...] = ends[8:16]

    @pl.when(owns_rest)
    def _():
        arrived(KC, kc_buf.at[pl.ds(0, half - 1)])

    @pl.when(jnp.logical_not(owns_rest))
    def _():
        arrived(KC, kc_buf.at[pl.ds(0, half)])

    both = mul(inverse, kc_buf[:half].reshape(64, 128))
    red_g[...] = mul(both[:, :64], inverse, NT)
    red_c[...] = mul(both[:, 64:], inverse, NT)

    sent(A, a_rcv)
    sent(B, b_buf.at[others])
    sent(SL, sl_buf.at[others_p, 0])
    sent(SU, su_buf.at[others_p, 0])
    sent(SLB, sl_buf.at[:, 0])
    sent(SUB, su_buf.at[:, 0])
    sent(SP, sp_buf.at[others])
    sent(SS, ss_buf.at[others])
    triangle_sent(0)
    triangle_sent(1)
    sent(RZ, rz_buf.at[others_z])
    sent(D, d_buf.at[:, others])
    sent(E_, e_buf.at[:, others])
    sent(N1A, n_sib)
    sent(N1, n_rcv)
    sent(N2, n_buf.at[others_p, 0])
    sent(N2B, n_buf.at[:, 0])
    sent(N3, m_src.at[others_z])
    sent(N4, m_buf.at[others_z])
    sent(P1, p_rcv)
    sent(P2, pz_buf.at[others_z])
    sent(W1, w_rcv)
    sent(W2, w_buf.at[others])

    @pl.when(owns)
    def _():
        sent(KR, k_src.at[pl.ds(0, n_own - 1)])
        sent(KZ, kz_buf.at[others_z])

    @pl.when(jnp.logical_not(owns))
    def _():
        sent(KR, k_src)

    @pl.when(owns_gram)
    def _():
        sent(KG, k_rcv)

    @pl.when(owns_rest)
    def _():
        sent(KC, k_rcv)


def hand_over(count, *refs):
    done = refs[-1]
    copies = [
        pltpu.make_async_copy(refs[n], refs[count + n], done.at[n]) for n in range(count)
    ]
    for copy in copies:
        copy.start()
    for copy in copies:
        copy.wait()


def shards(
    n_outer,
    n_inner,
    b_leaf,
    b_sep,
    b_root,
    leaf_linv,
    leaf_uinv,
    leaf_lower,
    leaf_upper,
    sep_rows,
    sep_linv,
    sep_uinv,
    sep_lower,
    sep_upper,
    root_linv,
    root_uinv,
    basis_leaf,
    basis_sep,
    basis_root,
    g_blocks,
    c_blocks,
    block_cols,
):
    nodes, ports = b_leaf.shape
    basis = basis_leaf.shape[1]
    root = root_linv.shape[1]
    width = n_inner * 8
    half = n_outer // 2
    per = PIECES_P // n_inner
    n_own = min(PIECES_K, n_inner)
    per_k = PIECES_K // n_own
    hbm = pl.BlockSpec(memory_space=pltpu.HBM)
    scratch = [
        (n_inner, 8, 128),
        (n_inner - 1, 8, 128),
        (n_inner, 8, 128),
        (n_inner // 2, 2, 8, width),
        (n_inner // 2, 2, 8, width),
        (n_inner, 8, 128),
        (n_inner, 8, 128),
        (n_inner, 8, 128),
        (n_inner, 8, 128),
        (n_outer, 8, root),
        (n_outer, 8, root),
        (n_outer, n_outer * 4, 128),
        (half, n_inner, 8, 128),
        (half, n_inner, 8, 128),
        (n_inner // 2, 2, 8, basis),
        (n_inner // 2, 8, basis),
        (n_inner // 2, 8, basis),
        (n_inner // 2 - 1, 8, basis),
        (n_inner // 2, 2, 8, basis),
        (n_outer, 8, basis),
        (n_outer, 8, basis),
        (n_outer, 8, basis),
        (n_inner, per, 8, 128),
        (n_inner - 1, per, 8, 128),
        (n_outer, per, 8, 128),
        (n_inner, 1 + per, 8, 128),
        (n_inner - 1, 1 + per, 8, 128),
        (n_inner, 1 + per, 8, 128),
        (n_own, per_k, 8, 128),
        (n_inner - 1, per_k, 8, 128),
        (n_outer, per_k, 8, 128),
        (n_own, per_k, 8, 128),
        (nodes + 16, basis),
        (nodes, nodes),
        (nodes, nodes),
    ]
    b_leaf_t, sep_lower_t = b_leaf.T, sep_lower.T
    kept = (
        b_leaf_t,
        b_sep,
        b_root,
        leaf_linv,
        leaf_uinv,
        leaf_lower,
        leaf_upper,
        sep_rows,
        sep_lower_t,
        sep_upper,
        g_blocks,
        c_blocks,
        block_cols,
    )
    outs = [(ports, nodes), (8, ports), (8, ports), (ports, basis), (ports, ports), (ports, ports)]
    vmem = pl.BlockSpec(memory_space=pltpu.VMEM)
    results = pl.pallas_call(
        functools.partial(kernel, n_outer, n_inner),
        out_shape=[pltpu.VMEM(s, F32) for s in outs],
        in_specs=[hbm] * 20,
        out_specs=[vmem] * 6,
        scratch_shapes=[pltpu.VMEM(s, F32) for s in scratch]
        + [pltpu.VMEM(x.shape, x.dtype) for x in kept]
        + [pltpu.SemaphoreType.DMA((n,)) for n in (27, 27, 20)]
        + [pltpu.SemaphoreType.DMA((2, n_outer))] * 2,
        compiler_params=pltpu.CompilerParams(
            collective_id=0, has_side_effects=True, vmem_limit_bytes=58 * 2**20
        ),
    )(*(pltpu.with_memory_space_constraint(x, pltpu.HBM) for x in (
        b_leaf_t,
        b_sep,
        b_root,
        leaf_linv,
        leaf_uinv,
        leaf_lower,
        leaf_upper,
        sep_rows,
        sep_linv,
        sep_uinv,
        sep_lower_t,
        sep_upper,
        root_linv,
        root_uinv,
        basis_leaf,
        basis_sep,
        basis_root,
        g_blocks,
        c_blocks,
        block_cols,
    )))
    v_leaf_t, v_sep, v_root, coef_t, red_g, red_c = pl.pallas_call(
        functools.partial(hand_over, len(outs)),
        out_shape=[jax.ShapeDtypeStruct(s, F32) for s in outs],
        in_specs=[vmem] * 6,
        out_specs=[hbm] * 6,
        scratch_shapes=[pltpu.SemaphoreType.DMA((6,))],
        compiler_params=pltpu.CompilerParams(vmem_limit_bytes=8 * 2**20),
    )(*results)
    return v_leaf_t.T, v_sep, v_root, coef_t.T, red_g, red_c


def solution(mesh):
    rows = P(("outer", "inner"), None)
    return jax.shard_map(
        functools.partial(shards, mesh.shape["outer"], mesh.shape["inner"]),
        mesh=mesh,
        in_specs=(rows,) * 10 + (P(None, ("outer", "inner")),) + (rows,) * 9,
        out_specs=(rows, rows, rows, P(), P(), P()),
        check_vma=False,
    )
```

```python
import functools

import jax
import jax.numpy as jnp
from jax import lax
from jax.experimental import pallas as pl
from jax.experimental.pallas import tpu as pltpu
from jax.sharding import PartitionSpec as P

MESH = pl.DeviceIdType.MESH
F32 = jnp.float32
NN = ((1,), (0,))
NT = ((1,), (1,))
TN = ((0,), (0,))
PIECES_P = 32
PIECES_K = 16


def mul(left, right, dims=NN):
    return lax.dot_general(
        left, right, (dims, ((), ())), precision=lax.Precision.HIGHEST, preferred_element_type=F32
    )


def wide(block):
    return jnp.concatenate([block, jnp.zeros_like(block)], axis=1)


def folded(block):
    half = block.shape[0] // 2
    return jnp.concatenate([block[:half], block[half:]], axis=1)


def unfolded_product(left, both):
    half = left.shape[1] // 2
    upper = mul(left[:, :half], both)
    lower = mul(left[:, half:], both)
    return upper[:, :64] + lower[:, 64:]


def inverse_factor(gram):
    row_ids = lax.broadcasted_iota(jnp.int32, (64, 64), 0)
    col_ids = lax.broadcasted_iota(jnp.int32, (64, 64), 1)
    start = jnp.concatenate([gram, (row_ids == col_ids).astype(F32)], axis=1)
    groups = tuple(start[8 * a : 8 * a + 8] for a in range(8))

    def spread(block, k):
        return jnp.broadcast_to(block[:, k : k + 1], (block.shape[0], 128))

    def panel(p, groups):
        head = groups[0]
        rows = [head[j : j + 1] for j in range(8)]
        corner = [[spread(rows[j], k) if k >= j else None for k in range(8)] for j in range(8)]
        scaled, factors = [], []
        for j in range(8):
            inverse = 1.0 / corner[j][j]
            scaled.append(rows[j] * inverse)
            factors.append([corner[j][t] * inverse if t > j else None for t in range(8)])
            for t in range(j + 1, 8):
                rows[t] = rows[t] - factors[j][t] * rows[j]
                for k in range(t, 8):
                    corner[t][k] = corner[t][k] - factors[j][t] * corner[j][k]
        done = [rows[j] * lax.rsqrt(corner[j][j]) for j in range(8)]
        turned = []
        for a in range(1, 8):
            live = jnp.where(a + p < 8, 1.0, 0.0).astype(F32)
            columns = []
            total = jnp.zeros((8, 128), F32)
            for j in range(8):
                column = spread(groups[a], j)
                for t in range(j):
                    column = column - columns[t] * factors[t][j]
                columns.append(column)
                total = total + column * scaled[j]
            turned.append(groups[a] - live * total)
        turned.append(jnp.concatenate(done, axis=0))
        return tuple(pltpu.roll(x, 120, 1) for x in turned)

    groups = lax.fori_loop(0, 8, panel, groups)
    return jnp.concatenate(groups, axis=0)[:, :64]


def by_owner(columns, n_outer, n_inner, out_ref):
    if n_inner * 8 != 256:
        moved = columns.reshape(8, n_outer, n_inner, 8).transpose(2, 0, 1, 3).reshape(n_inner, 8, n_outer * 8)
        out_ref[...] = jnp.concatenate(
            [moved, jnp.zeros((n_inner, 8, 128 - n_outer * 8), F32)], axis=2
        )
        return
    lane_group = lax.broadcasted_iota(jnp.int32, (8, 128), 1) // 8
    for m in range(2):
        shifted = []
        for o in range(n_outer):
            at = o * 256 + m * 128
            piece = columns[:, at : at + 128]
            shifted.append(pltpu.roll(piece, o * 8, 1) if o else piece)
        for ii in range(16):
            total = shifted[0]
            for o in range(1, n_outer):
                total = jnp.where(lane_group == (ii + o) % 16, shifted[o], total)
            out_ref[16 * m + ii] = pltpu.roll(total, 128 - ii * 8, 1) if ii else total


def around(count, far, body):
    lax.fori_loop(far, count, body, 0)
    lax.fori_loop(1, far, body, 0)


def kernel(
    n_outer,
    n_inner,
    h_b_t,
    h_b_sep,
    h_b_root,
    h_leaf_linv,
    h_leaf_uinv,
    h_leaf_lower,
    h_leaf_upper,
    h_sep_rows,
    h_sep_linv,
    h_sep_uinv,
    h_sep_lower_t,
    h_sep_upper,
    h_root_linv,
    h_root_uinv,
    h_basis_leaf,
    h_basis_sep,
    h_basis_root,
    h_g_blocks,
    h_c_blocks,
    h_block_cols,
    v_leaf_t,
    v_sep,
    v_root,
    coef_t,
    red_g,
    red_c,
    a_src,
    a_rcv,
    b_buf,
    sl_buf,
    su_buf,
    sp_src,
    sp_buf,
    ss_src,
    ss_buf,
    l_buf,
    u_buf,
    rz_buf,
    d_buf,
    e_buf,
    n_src,
    n_sib,
    n_pair,
    n_rcv,
    n_buf,
    m_src,
    m_rcv,
    m_buf,
    p_src,
    p_rcv,
    pz_buf,
    w_src,
    w_rcv,
    w_buf,
    k_src,
    k_rcv,
    kz_buf,
    kc_buf,
    q_all,
    hg,
    hc,
    b_t,
    b_sep,
    b_root,
    leaf_linv,
    leaf_uinv,
    leaf_lower,
    leaf_upper,
    sep_rows,
    sep_lower_t,
    sep_upper,
    g_blocks,
    c_blocks,
    block_cols,
    send,
    recv,
    here,
    tri_send,
    tri_recv,
):
    g = lax.axis_index("outer")
    i = lax.axis_index("inner")
    rb = n_outer * 8
    n_own = kc_buf.shape[0]
    stride = n_inner // n_own
    leaf_count = h_basis_leaf.shape[0]
    nodes = float(n_outer * n_inner * (leaf_count + 16))
    A, B, SL, SU, SP, SS, L, U, RZ, D, E_, N1, N2, N3, N4, P1, P2, W1, W2, KR, KZ, KG, KC, SLB, SUB, N1A, N2B = range(27)

    far_plane, far_chip, far_column = n_inner * 5 // 8, max(n_inner * 5 // 16, 1), max(n_outer * 3 // 8, 1)

    def to_plane(phase, src, dst):
        def one(k, carry):
            peer = lax.rem(i + k, n_inner)
            pltpu.make_async_remote_copy(
                src_ref=src(peer, k),
                dst_ref=dst(peer, k),
                send_sem=send.at[phase],
                recv_sem=recv.at[phase],
                device_id=(g, peer),
                device_id_type=MESH,
            ).start()
            return carry

        around(n_inner, far_plane, one)

    pairs = n_inner // 2
    chip, core = i // 2, lax.rem(i, 2)
    sibling = i + 1 - 2 * core

    def to_same_core(phase, src, dst):
        def one(k, carry):
            peer = lax.rem(chip + k, pairs)
            pltpu.make_async_remote_copy(
                src_ref=src(peer),
                dst_ref=dst(k),
                send_sem=send.at[phase],
                recv_sem=recv.at[phase],
                device_id=(g, 2 * peer + core),
                device_id_type=MESH,
            ).start()
            return carry

        around(pairs, far_chip, one)

    def to_sibling(phase, src, dst):
        pltpu.make_async_remote_copy(
            src_ref=src,
            dst_ref=dst,
            send_sem=send.at[phase],
            recv_sem=recv.at[phase],
            device_id=(g, sibling),
            device_id_type=MESH,
        ).start()

    def to_column(phase, src, dst):
        def one(k, carry):
            peer = lax.rem(g + k, n_outer)
            pltpu.make_async_remote_copy(
                src_ref=src(peer),
                dst_ref=dst,
                send_sem=send.at[phase],
                recv_sem=recv.at[phase],
                device_id=(peer, i),
                device_id_type=MESH,
            ).start()
            return carry

        around(n_outer, far_column, one)

    def arrived(phase, like):
        pltpu.make_async_copy(like, like, recv.at[phase]).wait()

    def sent(phase, like):
        pltpu.make_async_copy(like, like, send.at[phase]).wait()

    others = pl.ds(0, n_inner - 1)
    others_p = pl.ds(0, pairs - 1)
    others_z = pl.ds(0, n_outer - 1)

    own_slots = {
        "b_t": (h_b_t, b_t),
        "leaf_linv": (h_leaf_linv, leaf_linv),
        "leaf_lower": (h_leaf_lower, leaf_lower),
        "sep_rows": (h_sep_rows, sep_rows),
        "sep_lower_t": (h_sep_lower_t, sep_lower_t),
        "sep_linv": (h_sep_linv, sl_buf.at[chip, core]),
        "root_linv": (h_root_linv, l_buf.at[g]),
        "root_uinv": (h_root_uinv, u_buf.at[g]),
        "sep_uinv": (h_sep_uinv, su_buf.at[chip, core]),
        "b_sep": (h_b_sep, b_sep),
        "leaf_uinv": (h_leaf_uinv, leaf_uinv),
        "leaf_upper": (h_leaf_upper, leaf_upper),
        "b_root": (h_b_root, b_root),
        "sep_upper": (h_sep_upper, sep_upper),
        "g_blocks": (h_g_blocks, g_blocks),
        "c_blocks": (h_c_blocks, c_blocks),
        "block_cols": (h_block_cols, block_cols),
        "basis_leaf": (h_basis_leaf, q_all.at[pl.ds(0, leaf_count)]),
        "basis_sep": (h_basis_sep, q_all.at[pl.ds(leaf_count, 8)]),
        "basis_root": (h_basis_root, q_all.at[pl.ds(leaf_count + 8, 8)]),
    }
    loads = {
        name: pltpu.make_async_copy(src, dst, here.at[n])
        for n, (name, (src, dst)) in enumerate(own_slots.items())
    }
    span = n_inner * 8
    for o in range(n_outer):
        if o + 1 < n_outer:
            after = (n_outer - 1 - o) * span
            l_buf[o, :, (o + 1) * span :] = jnp.zeros((8, after), F32)
        if o:
            u_buf[o, :, : o * span] = jnp.zeros((8, o * span), F32)

    def part_of(which, o):
        if which == 0:
            return l_buf.at[o, :, pl.ds(0, (o + 1) * span)]
        return u_buf.at[o, :, pl.ds(o * span, (n_outer - o) * span)]

    def triangle_to_column(which):
        for o in range(n_outer):

            @pl.when(g == o)
            def _(o=o):
                def one(k, carry):
                    pltpu.make_async_remote_copy(
                        src_ref=part_of(which, o),
                        dst_ref=part_of(which, o),
                        send_sem=tri_send.at[which, k],
                        recv_sem=tri_recv.at[which, o],
                        device_id=(lax.rem(g + k, n_outer), i),
                        device_id_type=MESH,
                    ).start()
                    return carry

                lax.fori_loop(1, n_outer, one, 0)

    def triangle_arrived(which):
        for o in range(n_outer):

            @pl.when(g != o)
            def _(o=o):
                part = part_of(which, o)
                pltpu.make_async_copy(part, part, tri_recv.at[which, o]).wait()

    def triangle_sent(which):
        for o in range(n_outer):

            @pl.when(g == o)
            def _(o=o):
                part = part_of(which, o)

                def one(k, carry):
                    pltpu.make_async_copy(part, part, tri_send.at[which, k]).wait()
                    return carry

                lax.fori_loop(1, n_outer, one, 0)

    for load in loads.values():
        load.start()

    def loaded(*names):
        for name in names:
            loads[name].wait()

    barrier = pltpu.get_barrier_semaphore()

    def greet_plane(k, carry):
        pl.semaphore_signal(
            barrier, inc=1, device_id=(g, lax.rem(i + k, n_inner)), device_id_type=MESH
        )
        return carry

    def greet_column(k, carry):
        pl.semaphore_signal(
            barrier, inc=1, device_id=(lax.rem(g + k, n_outer), i), device_id_type=MESH
        )
        return carry

    around(n_inner, far_plane, greet_plane)
    lax.fori_loop(1, n_outer, greet_column, 0)

    loaded("b_t", "leaf_linv", "leaf_lower", "sep_rows")
    width = n_inner * 8
    couples = sep_rows.shape[1]
    sel_t = (
        lax.broadcasted_iota(jnp.int32, (width, couples), 0)
        == jnp.broadcast_to(sep_rows[...], (width, couples))
    ).astype(F32)
    y_t = mul(b_t[...], leaf_linv[...], NT)
    contrib_t = mul(y_t, leaf_lower[...], NT)
    update = mul(sel_t, contrib_t, NT)
    a_src[...] = wide(update).reshape(n_inner, 8, 128)
    loaded("sep_linv", "root_linv", "root_uinv", "sep_uinv", "b_sep")

    pl.semaphore_wait(barrier, n_inner + n_outer - 2)

    to_plane(A, lambda peer, k: a_src.at[peer], lambda peer, k: a_rcv.at[k - 1])
    to_same_core(SL, lambda peer: sl_buf.at[chip, core], lambda k: sl_buf.at[chip, core])
    triangle_to_column(0)
    loaded("sep_lower_t", "sep_upper")
    by_owner(sep_lower_t[...], n_outer, n_inner, sp_src)
    sp_buf[i] = sp_src[i]
    to_plane(SP, lambda peer, k: sp_src.at[peer], lambda peer, k: sp_buf.at[i])
    by_owner(sep_upper[...], n_outer, n_inner, ss_src)
    ss_buf[i] = ss_src[i]

    loaded("leaf_uinv", "leaf_upper", "b_root", "basis_leaf", "basis_sep", "basis_root")
    uy_t = mul(y_t, leaf_uinv[...], NT)
    coupling = mul(leaf_uinv[...], mul(leaf_upper[...], sel_t, NT))
    n_src[...] = mul(coupling, q_all[:leaf_count, :], TN).reshape(n_src.shape)
    to_sibling(N1A, n_src.at[:, 1 - core], n_sib)

    arrived(A, a_rcv)
    b_buf[i] = wide(b_sep[...]) - (a_src[i] + jnp.sum(a_rcv[...], axis=0))
    to_plane(B, lambda peer, k: b_buf.at[i], lambda peer, k: b_buf.at[i])
    arrived(N1A, n_sib)
    n_pair[...] = n_src[:, core] + n_sib[...]
    to_same_core(N1, lambda peer: n_pair.at[peer], lambda k: n_rcv.at[k - 1])
    arrived(SL, sl_buf.at[others_p, 0])
    to_sibling(SLB, sl_buf.at[:, core], sl_buf.at[:, core])
    to_same_core(SU, lambda peer: su_buf.at[chip, core], lambda k: su_buf.at[chip, core])
    to_plane(SS, lambda peer, k: ss_src.at[peer], lambda peer, k: ss_buf.at[i])

    arrived(SLB, sl_buf.at[:, 0])
    arrived(SP, sp_buf.at[others])
    sep_inverse = sl_buf[...].reshape(width, width)
    to_root = mul(sp_buf[...].reshape(width, 128)[:, :rb], sep_inverse, TN)

    arrived(B, b_buf.at[others])
    rhs_sep = b_buf[...].reshape(width, 128)
    part = mul(to_root, rhs_sep[:, :64])
    mine = lax.broadcasted_iota(jnp.int32, (rb, 64), 0) // 8 == g
    own = jnp.where(mine, jnp.concatenate([b_root[...]] * n_outer, axis=0), 0.0)
    rz_buf[g] = folded(own - part)
    to_column(RZ, lambda peer: rz_buf.at[g], rz_buf.at[g])
    triangle_to_column(1)

    y_own = mul(sl_buf[chip, core], rhs_sep[:, :64])
    sep_y_t = mul(jnp.transpose(rhs_sep)[:64], sep_inverse, NT)
    arrived(N1, n_rcv)
    mine_n = n_pair[chip] + jnp.sum(n_rcv[...], axis=0)
    n_buf[chip, core] = q_all[leaf_count : leaf_count + 8, :] - mine_n
    to_same_core(N2, lambda peer: n_buf.at[chip, core], lambda k: n_buf.at[chip, core])
    arrived(SU, su_buf.at[others_p, 0])
    to_sibling(SUB, su_buf.at[:, core], su_buf.at[:, core])

    def root_gather(phase, buf, block):
        buf[:, i] = block.reshape(n_outer // 2, 8, 128)
        to_plane(phase, lambda peer, k: buf.at[:, i], lambda peer, k: buf.at[:, i])

    def root_value(phase, buf):
        arrived(phase, buf.at[:, others])
        return buf[...].reshape(n_outer // 2 * n_inner * 8, 128)

    arrived(RZ, rz_buf.at[others_z])
    root_gather(D, d_buf, jnp.sum(rz_buf[...], axis=0))

    arrived(SUB, su_buf.at[:, 0])
    sep_upper_inverse = su_buf[...].reshape(width, width)
    from_sep = mul(coupling, sep_upper_inverse)
    start_t = jnp.concatenate(
        [uy_t - mul(sep_y_t, from_sep, NT), mul(sep_y_t, su_buf[chip, core], NT)], axis=1
    )
    proj_t = mul(start_t, q_all[: leaf_count + 8, :])
    per = PIECES_P // n_inner
    for t in range(PIECES_P):
        r, c = t // 4, t % 4
        p_src[t // per, t % per] = proj_t[8 * r : 8 * r + 8, 128 * c : 128 * c + 128]
    to_plane(P1, lambda peer, k: p_src.at[peer], lambda peer, k: p_rcv.at[k - 1])

    arrived(N2, n_buf.at[others_p, 0])
    to_sibling(N2B, n_buf.at[:, core], n_buf.at[:, core])
    arrived(SS, ss_buf.at[others])
    sep_by_root = ss_buf[...].reshape(width, 128)[:, :rb]
    arrived(N2B, n_buf.at[:, 0])
    m_src[...] = mul(
        mul(sep_upper_inverse, sep_by_root), n_buf[...].reshape(width, n_buf.shape[3]), TN
    ).reshape(m_src.shape)
    m_rcv[g] = m_src[g]
    to_column(N3, lambda peer: m_src.at[peer], m_rcv.at[g])

    triangle_arrived(0)
    lower_rows = l_buf[...].reshape(rb, l_buf.shape[2])
    y_root = unfolded_product(lower_rows, root_value(D, d_buf))
    root_gather(E_, e_buf, folded(y_root))

    arrived(P1, p_rcv)
    pz_buf[g] = p_src[i] + jnp.sum(p_rcv[...], axis=0)
    to_column(P2, lambda peer: pz_buf.at[g], pz_buf.at[g])

    loaded("g_blocks", "c_blocks", "block_cols")
    size = g_blocks.shape[1]
    stored = block_cols.shape[1]
    for r in range(2):
        for c in range(2):
            for blocks, whole in ((g_blocks, hg), (c_blocks, hc)):
                total = jnp.zeros((size, size), F32)
                for w in range(stored):
                    at = (r * stored + w) * size
                    weight = (block_cols[r : r + 1, w : w + 1] == c).astype(F32)
                    total = total + weight * blocks[at : at + size, :]
                whole[r * size : (r + 1) * size, c * size : (c + 1) * size] = total

    arrived(N3, m_rcv.at[others_z])
    m_buf[g] = jnp.sum(m_rcv[...], axis=0) - q_all[leaf_count + 8 : leaf_count + 16, :]
    to_column(N4, lambda peer: m_buf.at[g], m_buf.at[g])
    arrived(P2, pz_buf.at[others_z])
    proj_start = jnp.sum(pz_buf[...], axis=0)

    triangle_arrived(1)
    upper_rows = u_buf[...].reshape(rb, u_buf.shape[2])
    x_root = unfolded_product(upper_rows, root_value(E_, e_buf))

    sep_part = wide(mul(sep_by_root, x_root)).reshape(n_inner, 8, 128)
    arrived(N4, m_buf.at[others_z])
    proj_t = mul(x_root, m_buf[...].reshape(rb, m_buf.shape[2]), TN)
    w_src[:, 0] = sep_part
    for t in range(PIECES_P):
        r, c = t // 4, t % 4
        w_src[t // per, 1 + t % per] = proj_t[8 * r : 8 * r + 8, 128 * c : 128 * c + 128]
    to_plane(W1, lambda peer, k: w_src.at[peer], lambda peer, k: w_rcv.at[k - 1])
    row_ids = lax.broadcasted_iota(jnp.int32, (8, rb), 0)
    col_ids = lax.broadcasted_iota(jnp.int32, (8, rb), 1)
    pick = (col_ids == row_ids + 8 * g).astype(F32)
    x_root_t = mul(x_root, pick, ((0,), (1,)))
    arrived(W1, w_rcv)
    moved = w_src[i] + jnp.sum(w_rcv[...], axis=0)
    w_buf[i, 0] = wide(y_own) - moved[0]
    w_buf[i, pl.ds(1, per)] = (proj_start - moved[1:]) / nodes
    to_plane(W2, lambda peer, k: w_buf.at[i], lambda peer, k: w_buf.at[i])
    arrived(W2, w_buf.at[others])

    z_t = jnp.transpose(w_buf[:, 0].reshape(width, 128))[:64]
    x_leaf_t = uy_t - mul(z_t, from_sep, NT)
    x_sep_t = mul(z_t, su_buf[chip, core], NT)
    x_t = jnp.concatenate([x_leaf_t, x_sep_t, x_root_t], axis=1)
    coefs = jnp.concatenate(
        [
            jnp.concatenate(
                [w_buf[(4 * r + c) // per, 1 + (4 * r + c) % per] for c in range(4)], axis=1
            )
            for r in range(8)
        ],
        axis=0,
    )
    clean_t = x_t - mul(coefs, q_all[...], NT)

    per_k = PIECES_K // n_own
    half = n_own // 2
    owner = i // stride
    owns = lax.rem(i, stride) == 0
    owns_gram = jnp.logical_and(owns, owner >= half)
    owns_rest = jnp.logical_and(owns, owner < half)

    def to_owners(first):
        def one(n, carry):
            at = first + n
            peer = at * stride

            @pl.when(peer != i)
            def _():
                pltpu.make_async_remote_copy(
                    src_ref=k_src.at[at],
                    dst_ref=k_rcv.at[lax.rem(peer + n_inner - i, n_inner) - 1],
                    send_sem=send.at[KR],
                    recv_sem=recv.at[KR],
                    device_id=(g, peer),
                    device_id_type=MESH,
                ).start()

            return carry

        lax.fori_loop(0, half, one, 0)

    k_src[half:] = wide(mul(clean_t, clean_t, NT)).reshape(half, per_k, 8, 128)
    to_owners(half)
    clean_leaf_t = clean_t[:, :leaf_count]
    coef_t[...] = coefs
    g_part = mul(mul(clean_leaf_t, hg[...]), clean_leaf_t, NT)
    c_part = mul(mul(clean_leaf_t, hc[...]), clean_leaf_t, NT)
    k_src[:half] = jnp.concatenate([g_part, c_part], axis=1).reshape(half, per_k, 8, 128)
    to_owners(0)

    @pl.when(owns)
    def _():
        arrived(KR, k_rcv)
        kz_buf[g] = k_src[owner] + jnp.sum(k_rcv[...], axis=0)
        to_column(KZ, lambda peer: kz_buf.at[g], kz_buf.at[g])
        arrived(KZ, kz_buf.at[others_z])
        kc_buf[owner] = jnp.sum(kz_buf[...], axis=0) / nodes

    @pl.when(owns_gram)
    def _():
        to_plane(KG, lambda peer, k: kc_buf.at[owner], lambda peer, k: kc_buf.at[owner])
        arrived(KG, kc_buf.at[pl.ds(0, half - 1)])

    @pl.when(owns_rest)
    def _():
        to_plane(KC, lambda peer, k: kc_buf.at[owner], lambda peer, k: kc_buf.at[owner])

    @pl.when(jnp.logical_not(owns_gram))
    def _():
        arrived(KG, kc_buf.at[pl.ds(0, half)])

    inverse = inverse_factor(kc_buf[half:].reshape(64, 128)[:, :64])
    v_t = mul(inverse, clean_t)
    v_leaf_t[...] = v_t[:, :leaf_count]
    ends = jnp.concatenate([v_t[:, leaf_count:], jnp.zeros((64, 112), F32)], axis=1)
    ends = jnp.transpose(ends)
    v_sep[...] = ends[0:8]
    v_root[...] = ends[8:16]

    @pl.when(owns_rest)
    def _():
        arrived(KC, kc_buf.at[pl.ds(0, half - 1)])

    @pl.when(jnp.logical_not(owns_rest))
    def _():
        arrived(KC, kc_buf.at[pl.ds(0, half)])

    both = mul(inverse, kc_buf[:half].reshape(64, 128))
    red_g[...] = mul(both[:, :64], inverse, NT)
    red_c[...] = mul(both[:, 64:], inverse, NT)

    sent(A, a_rcv)
    sent(B, b_buf.at[others])
    sent(SL, sl_buf.at[others_p, 0])
    sent(SU, su_buf.at[others_p, 0])
    sent(SLB, sl_buf.at[:, 0])
    sent(SUB, su_buf.at[:, 0])
    sent(SP, sp_buf.at[others])
    sent(SS, ss_buf.at[others])
    triangle_sent(0)
    triangle_sent(1)
    sent(RZ, rz_buf.at[others_z])
    sent(D, d_buf.at[:, others])
    sent(E_, e_buf.at[:, others])
    sent(N1A, n_sib)
    sent(N1, n_rcv)
    sent(N2, n_buf.at[others_p, 0])
    sent(N2B, n_buf.at[:, 0])
    sent(N3, m_src.at[others_z])
    sent(N4, m_buf.at[others_z])
    sent(P1, p_rcv)
    sent(P2, pz_buf.at[others_z])
    sent(W1, w_rcv)
    sent(W2, w_buf.at[others])

    @pl.when(owns)
    def _():
        sent(KR, k_src.at[pl.ds(0, n_own - 1)])
        sent(KZ, kz_buf.at[others_z])

    @pl.when(jnp.logical_not(owns))
    def _():
        sent(KR, k_src)

    @pl.when(owns_gram)
    def _():
        sent(KG, k_rcv)

    @pl.when(owns_rest)
    def _():
        sent(KC, k_rcv)


def hand_over(count, *refs):
    done = refs[-1]
    copies = [
        pltpu.make_async_copy(refs[n], refs[count + n], done.at[n]) for n in range(count)
    ]
    for copy in copies:
        copy.start()
    for copy in copies:
        copy.wait()


def shards(
    n_outer,
    n_inner,
    b_leaf,
    b_sep,
    b_root,
    leaf_linv,
    leaf_uinv,
    leaf_lower,
    leaf_upper,
    sep_rows,
    sep_linv,
    sep_uinv,
    sep_lower,
    sep_upper,
    root_linv,
    root_uinv,
    basis_leaf,
    basis_sep,
    basis_root,
    g_blocks,
    c_blocks,
    block_cols,
):
    nodes, ports = b_leaf.shape
    basis = basis_leaf.shape[1]
    root = root_linv.shape[1]
    width = n_inner * 8
    half = n_outer // 2
    per = PIECES_P // n_inner
    n_own = min(PIECES_K, n_inner)
    per_k = PIECES_K // n_own
    hbm = pl.BlockSpec(memory_space=pltpu.HBM)
    scratch = [
        (n_inner, 8, 128),
        (n_inner - 1, 8, 128),
        (n_inner, 8, 128),
        (n_inner // 2, 2, 8, width),
        (n_inner // 2, 2, 8, width),
        (n_inner, 8, 128),
        (n_inner, 8, 128),
        (n_inner, 8, 128),
        (n_inner, 8, 128),
        (n_outer, 8, root),
        (n_outer, 8, root),
        (n_outer, n_outer * 4, 128),
        (half, n_inner, 8, 128),
        (half, n_inner, 8, 128),
        (n_inner // 2, 2, 8, basis),
        (n_inner // 2, 8, basis),
        (n_inner // 2, 8, basis),
        (n_inner // 2 - 1, 8, basis),
        (n_inner // 2, 2, 8, basis),
        (n_outer, 8, basis),
        (n_outer, 8, basis),
        (n_outer, 8, basis),
        (n_inner, per, 8, 128),
        (n_inner - 1, per, 8, 128),
        (n_outer, per, 8, 128),
        (n_inner, 1 + per, 8, 128),
        (n_inner - 1, 1 + per, 8, 128),
        (n_inner, 1 + per, 8, 128),
        (n_own, per_k, 8, 128),
        (n_inner - 1, per_k, 8, 128),
        (n_outer, per_k, 8, 128),
        (n_own, per_k, 8, 128),
        (nodes + 16, basis),
        (nodes, nodes),
        (nodes, nodes),
    ]
    b_leaf_t, sep_lower_t = b_leaf.T, sep_lower.T
    kept = (
        b_leaf_t,
        b_sep,
        b_root,
        leaf_linv,
        leaf_uinv,
        leaf_lower,
        leaf_upper,
        sep_rows,
        sep_lower_t,
        sep_upper,
        g_blocks,
        c_blocks,
        block_cols,
    )
    outs = [(ports, nodes), (8, ports), (8, ports), (ports, basis), (ports, ports), (ports, ports)]
    vmem = pl.BlockSpec(memory_space=pltpu.VMEM)
    results = pl.pallas_call(
        functools.partial(kernel, n_outer, n_inner),
        out_shape=[pltpu.VMEM(s, F32) for s in outs],
        in_specs=[hbm] * 20,
        out_specs=[vmem] * 6,
        scratch_shapes=[pltpu.VMEM(s, F32) for s in scratch]
        + [pltpu.VMEM(x.shape, x.dtype) for x in kept]
        + [pltpu.SemaphoreType.DMA((n,)) for n in (27, 27, 20)]
        + [pltpu.SemaphoreType.DMA((2, n_outer))] * 2,
        compiler_params=pltpu.CompilerParams(
            collective_id=0, has_side_effects=True, vmem_limit_bytes=58 * 2**20
        ),
    )(*(pltpu.with_memory_space_constraint(x, pltpu.HBM) for x in (
        b_leaf_t,
        b_sep,
        b_root,
        leaf_linv,
        leaf_uinv,
        leaf_lower,
        leaf_upper,
        sep_rows,
        sep_linv,
        sep_uinv,
        sep_lower_t,
        sep_upper,
        root_linv,
        root_uinv,
        basis_leaf,
        basis_sep,
        basis_root,
        g_blocks,
        c_blocks,
        block_cols,
    )))
    v_leaf_t, v_sep, v_root, coef_t, red_g, red_c = pl.pallas_call(
        functools.partial(hand_over, len(outs)),
        out_shape=[jax.ShapeDtypeStruct(s, F32) for s in outs],
        in_specs=[vmem] * 6,
        out_specs=[hbm] * 6,
        scratch_shapes=[pltpu.SemaphoreType.DMA((6,))],
        compiler_params=pltpu.CompilerParams(vmem_limit_bytes=8 * 2**20),
    )(*results)
    return v_leaf_t.T, v_sep, v_root, coef_t.T, red_g, red_c


def solution(mesh):
    rows = P(("outer", "inner"), None)
    return jax.shard_map(
        functools.partial(shards, mesh.shape["outer"], mesh.shape["inner"]),
        mesh=mesh,
        in_specs=(rows,) * 10 + (P(None, ("outer", "inner")),) + (rows,) * 9,
        out_specs=(rows, rows, rows, P(), P(), P()),
        check_vma=False,
    )
```

```python
import functools

import jax
import jax.numpy as jnp
from jax import lax
from jax.experimental import pallas as pl
from jax.experimental.pallas import tpu as pltpu
from jax.sharding import PartitionSpec as P

MESH = pl.DeviceIdType.MESH
F32 = jnp.float32
NN = ((1,), (0,))
NT = ((1,), (1,))
TN = ((0,), (0,))
PIECES_P = 32
PIECES_K = 16


def mul(left, right, dims=NN):
    return lax.dot_general(
        left, right, (dims, ((), ())), precision=lax.Precision.HIGHEST, preferred_element_type=F32
    )


def wide(block):
    return jnp.concatenate([block, jnp.zeros_like(block)], axis=1)


def folded(block):
    half = block.shape[0] // 2
    return jnp.concatenate([block[:half], block[half:]], axis=1)


def unfolded_product(left, both):
    half = left.shape[1] // 2
    upper = mul(left[:, :half], both)
    lower = mul(left[:, half:], both)
    return upper[:, :64] + lower[:, 64:]


def inverse_factor(gram):
    row_ids = lax.broadcasted_iota(jnp.int32, (64, 64), 0)
    col_ids = lax.broadcasted_iota(jnp.int32, (64, 64), 1)
    start = jnp.concatenate([gram, (row_ids == col_ids).astype(F32)], axis=1)
    groups = tuple(start[8 * a : 8 * a + 8] for a in range(8))

    def spread(block, k):
        return jnp.broadcast_to(block[:, k : k + 1], (block.shape[0], 128))

    def panel(p, groups):
        head = groups[0]
        rows = [head[j : j + 1] for j in range(8)]
        corner = [[spread(rows[j], k) if k >= j else None for k in range(8)] for j in range(8)]
        scaled, factors = [], []
        for j in range(8):
            inverse = 1.0 / corner[j][j]
            scaled.append(rows[j] * inverse)
            factors.append([corner[j][t] * inverse if t > j else None for t in range(8)])
            for t in range(j + 1, 8):
                rows[t] = rows[t] - factors[j][t] * rows[j]
                for k in range(t, 8):
                    corner[t][k] = corner[t][k] - factors[j][t] * corner[j][k]
        done = [rows[j] * lax.rsqrt(corner[j][j]) for j in range(8)]
        turned = []
        for a in range(1, 8):
            live = jnp.where(a + p < 8, 1.0, 0.0).astype(F32)
            columns = []
            total = jnp.zeros((8, 128), F32)
            for j in range(8):
                column = spread(groups[a], j)
                for t in range(j):
                    column = column - columns[t] * factors[t][j]
                columns.append(column)
                total = total + column * scaled[j]
            turned.append(groups[a] - live * total)
        turned.append(jnp.concatenate(done, axis=0))
        return tuple(pltpu.roll(x, 120, 1) for x in turned)

    groups = lax.fori_loop(0, 8, panel, groups)
    return jnp.concatenate(groups, axis=0)[:, :64]


def by_owner(columns, n_outer, n_inner, out_ref):
    if n_inner * 8 != 256:
        moved = columns.reshape(8, n_outer, n_inner, 8).transpose(2, 0, 1, 3).reshape(n_inner, 8, n_outer * 8)
        out_ref[...] = jnp.concatenate(
            [moved, jnp.zeros((n_inner, 8, 128 - n_outer * 8), F32)], axis=2
        )
        return
    lane_group = lax.broadcasted_iota(jnp.int32, (8, 128), 1) // 8
    for m in range(2):
        shifted = []
        for o in range(n_outer):
            at = o * 256 + m * 128
            piece = columns[:, at : at + 128]
            shifted.append(pltpu.roll(piece, o * 8, 1) if o else piece)
        for ii in range(16):
            total = shifted[0]
            for o in range(1, n_outer):
                total = jnp.where(lane_group == (ii + o) % 16, shifted[o], total)
            out_ref[16 * m + ii] = pltpu.roll(total, 128 - ii * 8, 1) if ii else total


def around(count, far, body):
    lax.fori_loop(far, count, body, 0)
    lax.fori_loop(1, far, body, 0)


def kernel(
    n_outer,
    n_inner,
    h_b_t,
    h_b_sep,
    h_b_root,
    h_leaf_linv,
    h_leaf_uinv,
    h_leaf_lower,
    h_leaf_upper,
    h_sep_rows,
    h_sep_linv,
    h_sep_uinv,
    h_sep_lower_t,
    h_sep_upper,
    h_root_linv,
    h_root_uinv,
    h_basis_leaf,
    h_basis_sep,
    h_basis_root,
    h_g_blocks,
    h_c_blocks,
    h_block_cols,
    v_leaf_t,
    v_sep,
    v_root,
    coef_t,
    red_g,
    red_c,
    a_src,
    a_rcv,
    b_buf,
    sl_buf,
    su_buf,
    sp_src,
    sp_buf,
    ss_src,
    ss_buf,
    l_buf,
    u_buf,
    rz_buf,
    d_buf,
    e_buf,
    n_src,
    n_sib,
    n_pair,
    n_rcv,
    n_buf,
    m_src,
    m_rcv,
    m_buf,
    p_src,
    p_rcv,
    pz_buf,
    w_src,
    w_rcv,
    w_buf,
    k_src,
    k_rcv,
    kz_buf,
    kc_buf,
    q_all,
    hg,
    hc,
    b_t,
    b_sep,
    b_root,
    leaf_linv,
    leaf_uinv,
    leaf_lower,
    leaf_upper,
    sep_rows,
    sep_lower_t,
    sep_upper,
    g_blocks,
    c_blocks,
    block_cols,
    send,
    recv,
    here,
    tri_send,
    tri_recv,
):
    g = lax.axis_index("outer")
    i = lax.axis_index("inner")
    rb = n_outer * 8
    n_own = kc_buf.shape[0]
    stride = n_inner // n_own
    leaf_count = h_basis_leaf.shape[0]
    nodes = float(n_outer * n_inner * (leaf_count + 16))
    A, B, SL, SU, SP, SS, L, U, RZ, D, E_, N1, N2, N3, N4, P1, P2, W1, W2, KR, KZ, KG, KC, SLB, SUB, N1A, N2B = range(27)

    far_plane, far_chip, far_column = n_inner * 5 // 8, max(n_inner * 5 // 16, 1), max(n_outer * 3 // 8, 1)

    def to_plane(phase, src, dst):
        def one(k, carry):
            peer = lax.rem(i + k, n_inner)
            pltpu.make_async_remote_copy(
                src_ref=src(peer, k),
                dst_ref=dst(peer, k),
                send_sem=send.at[phase],
                recv_sem=recv.at[phase],
                device_id=(g, peer),
                device_id_type=MESH,
            ).start()
            return carry

        around(n_inner, far_plane, one)

    pairs = n_inner // 2
    chip, core = i // 2, lax.rem(i, 2)
    sibling = i + 1 - 2 * core

    def to_same_core(phase, src, dst):
        def one(k, carry):
            peer = lax.rem(chip + k, pairs)
            pltpu.make_async_remote_copy(
                src_ref=src(peer),
                dst_ref=dst(k),
                send_sem=send.at[phase],
                recv_sem=recv.at[phase],
                device_id=(g, 2 * peer + core),
                device_id_type=MESH,
            ).start()
            return carry

        around(pairs, far_chip, one)

    def to_sibling(phase, src, dst):
        pltpu.make_async_remote_copy(
            src_ref=src,
            dst_ref=dst,
            send_sem=send.at[phase],
            recv_sem=recv.at[phase],
            device_id=(g, sibling),
            device_id_type=MESH,
        ).start()

    def to_column(phase, src, dst):
        def one(k, carry):
            peer = lax.rem(g + k, n_outer)
            pltpu.make_async_remote_copy(
                src_ref=src(peer),
                dst_ref=dst,
                send_sem=send.at[phase],
                recv_sem=recv.at[phase],
                device_id=(peer, i),
                device_id_type=MESH,
            ).start()
            return carry

        around(n_outer, far_column, one)

    def arrived(phase, like):
        pltpu.make_async_copy(like, like, recv.at[phase]).wait()

    def sent(phase, like):
        pltpu.make_async_copy(like, like, send.at[phase]).wait()

    others = pl.ds(0, n_inner - 1)
    others_p = pl.ds(0, pairs - 1)
    others_z = pl.ds(0, n_outer - 1)

    own_slots = {
        "b_t": (h_b_t, b_t),
        "leaf_linv": (h_leaf_linv, leaf_linv),
        "leaf_lower": (h_leaf_lower, leaf_lower),
        "sep_rows": (h_sep_rows, sep_rows),
        "sep_lower_t": (h_sep_lower_t, sep_lower_t),
        "sep_linv": (h_sep_linv, sl_buf.at[chip, core]),
        "root_linv": (h_root_linv, l_buf.at[g]),
        "root_uinv": (h_root_uinv, u_buf.at[g]),
        "sep_uinv": (h_sep_uinv, su_buf.at[chip, core]),
        "b_sep": (h_b_sep, b_sep),
        "leaf_uinv": (h_leaf_uinv, leaf_uinv),
        "leaf_upper": (h_leaf_upper, leaf_upper),
        "b_root": (h_b_root, b_root),
        "sep_upper": (h_sep_upper, sep_upper),
        "g_blocks": (h_g_blocks, g_blocks),
        "c_blocks": (h_c_blocks, c_blocks),
        "block_cols": (h_block_cols, block_cols),
        "basis_leaf": (h_basis_leaf, q_all.at[pl.ds(0, leaf_count)]),
        "basis_sep": (h_basis_sep, q_all.at[pl.ds(leaf_count, 8)]),
        "basis_root": (h_basis_root, q_all.at[pl.ds(leaf_count + 8, 8)]),
    }
    loads = {
        name: pltpu.make_async_copy(src, dst, here.at[n])
        for n, (name, (src, dst)) in enumerate(own_slots.items())
    }
    first = ("b_t", "leaf_linv", "leaf_lower", "sep_rows")
    for name in first:
        loads[name].start()

    barrier = pltpu.get_barrier_semaphore()

    def greet_plane(k, carry):
        pl.semaphore_signal(
            barrier, inc=1, device_id=(g, lax.rem(i + k, n_inner)), device_id_type=MESH
        )
        return carry

    def greet_column(k, carry):
        pl.semaphore_signal(
            barrier, inc=1, device_id=(lax.rem(g + k, n_outer), i), device_id_type=MESH
        )
        return carry

    around(n_inner, far_plane, greet_plane)
    lax.fori_loop(1, n_outer, greet_column, 0)

    span = n_inner * 8
    for o in range(n_outer):
        if o + 1 < n_outer:
            after = (n_outer - 1 - o) * span
            l_buf[o, :, (o + 1) * span :] = jnp.zeros((8, after), F32)
        if o:
            u_buf[o, :, : o * span] = jnp.zeros((8, o * span), F32)

    def part_of(which, o):
        if which == 0:
            return l_buf.at[o, :, pl.ds(0, (o + 1) * span)]
        return u_buf.at[o, :, pl.ds(o * span, (n_outer - o) * span)]

    def triangle_to_column(which):
        for o in range(n_outer):

            @pl.when(g == o)
            def _(o=o):
                def one(k, carry):
                    pltpu.make_async_remote_copy(
                        src_ref=part_of(which, o),
                        dst_ref=part_of(which, o),
                        send_sem=tri_send.at[which, k],
                        recv_sem=tri_recv.at[which, o],
                        device_id=(lax.rem(g + k, n_outer), i),
                        device_id_type=MESH,
                    ).start()
                    return carry

                lax.fori_loop(1, n_outer, one, 0)

    def triangle_arrived(which):
        for o in range(n_outer):

            @pl.when(g != o)
            def _(o=o):
                part = part_of(which, o)
                pltpu.make_async_copy(part, part, tri_recv.at[which, o]).wait()

    def triangle_sent(which):
        for o in range(n_outer):

            @pl.when(g == o)
            def _(o=o):
                part = part_of(which, o)

                def one(k, carry):
                    pltpu.make_async_copy(part, part, tri_send.at[which, k]).wait()
                    return carry

                lax.fori_loop(1, n_outer, one, 0)

    for name, load in loads.items():
        if name not in first:
            load.start()

    def loaded(*names):
        for name in names:
            loads[name].wait()

    loaded(*first)
    width = n_inner * 8
    couples = sep_rows.shape[1]
    sel_t = (
        lax.broadcasted_iota(jnp.int32, (width, couples), 0)
        == jnp.broadcast_to(sep_rows[...], (width, couples))
    ).astype(F32)
    y_t = mul(b_t[...], leaf_linv[...], NT)
    contrib_t = mul(y_t, leaf_lower[...], NT)
    update = mul(sel_t, contrib_t, NT)
    a_src[...] = wide(update).reshape(n_inner, 8, 128)
    loaded("sep_linv", "root_linv", "root_uinv", "sep_uinv", "b_sep")

    pl.semaphore_wait(barrier, n_inner + n_outer - 2)

    to_plane(A, lambda peer, k: a_src.at[peer], lambda peer, k: a_rcv.at[k - 1])
    to_same_core(SL, lambda peer: sl_buf.at[chip, core], lambda k: sl_buf.at[chip, core])
    triangle_to_column(0)
    loaded("sep_lower_t", "sep_upper")
    by_owner(sep_lower_t[...], n_outer, n_inner, sp_src)
    sp_buf[i] = sp_src[i]
    to_plane(SP, lambda peer, k: sp_src.at[peer], lambda peer, k: sp_buf.at[i])
    by_owner(sep_upper[...], n_outer, n_inner, ss_src)
    ss_buf[i] = ss_src[i]

    loaded("leaf_uinv", "leaf_upper", "b_root", "basis_leaf", "basis_sep", "basis_root")
    uy_t = mul(y_t, leaf_uinv[...], NT)
    coupling = mul(leaf_uinv[...], mul(leaf_upper[...], sel_t, NT))
    n_src[...] = mul(coupling, q_all[:leaf_count, :], TN).reshape(n_src.shape)
    to_sibling(N1A, n_src.at[:, 1 - core], n_sib)

    arrived(A, a_rcv)
    b_buf[i] = wide(b_sep[...]) - (a_src[i] + jnp.sum(a_rcv[...], axis=0))
    to_plane(B, lambda peer, k: b_buf.at[i], lambda peer, k: b_buf.at[i])
    arrived(N1A, n_sib)
    n_pair[...] = n_src[:, core] + n_sib[...]
    to_same_core(N1, lambda peer: n_pair.at[peer], lambda k: n_rcv.at[k - 1])
    arrived(SL, sl_buf.at[others_p, 0])
    to_sibling(SLB, sl_buf.at[:, core], sl_buf.at[:, core])
    to_same_core(SU, lambda peer: su_buf.at[chip, core], lambda k: su_buf.at[chip, core])
    to_plane(SS, lambda peer, k: ss_src.at[peer], lambda peer, k: ss_buf.at[i])

    arrived(SLB, sl_buf.at[:, 0])
    arrived(SP, sp_buf.at[others])
    sep_inverse = sl_buf[...].reshape(width, width)
    to_root = mul(sp_buf[...].reshape(width, 128)[:, :rb], sep_inverse, TN)

    arrived(B, b_buf.at[others])
    rhs_sep = b_buf[...].reshape(width, 128)
    part = mul(to_root, rhs_sep[:, :64])
    mine = lax.broadcasted_iota(jnp.int32, (rb, 64), 0) // 8 == g
    own = jnp.where(mine, jnp.concatenate([b_root[...]] * n_outer, axis=0), 0.0)
    rz_buf[g] = folded(own - part)
    to_column(RZ, lambda peer: rz_buf.at[g], rz_buf.at[g])
    triangle_to_column(1)

    y_own = mul(sl_buf[chip, core], rhs_sep[:, :64])
    sep_y_t = mul(jnp.transpose(rhs_sep)[:64], sep_inverse, NT)
    arrived(N1, n_rcv)
    mine_n = n_pair[chip] + jnp.sum(n_rcv[...], axis=0)
    n_buf[chip, core] = q_all[leaf_count : leaf_count + 8, :] - mine_n
    to_same_core(N2, lambda peer: n_buf.at[chip, core], lambda k: n_buf.at[chip, core])
    arrived(SU, su_buf.at[others_p, 0])
    to_sibling(SUB, su_buf.at[:, core], su_buf.at[:, core])

    def root_gather(phase, buf, block):
        buf[:, i] = block.reshape(n_outer // 2, 8, 128)
        to_plane(phase, lambda peer, k: buf.at[:, i], lambda peer, k: buf.at[:, i])

    def root_value(phase, buf):
        arrived(phase, buf.at[:, others])
        return buf[...].reshape(n_outer // 2 * n_inner * 8, 128)

    arrived(RZ, rz_buf.at[others_z])
    root_gather(D, d_buf, jnp.sum(rz_buf[...], axis=0))

    arrived(SUB, su_buf.at[:, 0])
    sep_upper_inverse = su_buf[...].reshape(width, width)
    from_sep = mul(coupling, sep_upper_inverse)
    arrived(N2, n_buf.at[others_p, 0])
    to_sibling(N2B, n_buf.at[:, core], n_buf.at[:, core])
    arrived(SS, ss_buf.at[others])
    sep_by_root = ss_buf[...].reshape(width, 128)[:, :rb]
    arrived(N2B, n_buf.at[:, 0])
    m_src[...] = mul(
        mul(sep_upper_inverse, sep_by_root), n_buf[...].reshape(width, n_buf.shape[3]), TN
    ).reshape(m_src.shape)
    m_rcv[g] = m_src[g]
    to_column(N3, lambda peer: m_src.at[peer], m_rcv.at[g])

    start_t = jnp.concatenate(
        [uy_t - mul(sep_y_t, from_sep, NT), mul(sep_y_t, su_buf[chip, core], NT)], axis=1
    )
    proj_t = mul(start_t, q_all[: leaf_count + 8, :])
    per = PIECES_P // n_inner
    for t in range(PIECES_P):
        r, c = t // 4, t % 4
        p_src[t // per, t % per] = proj_t[8 * r : 8 * r + 8, 128 * c : 128 * c + 128]
    to_plane(P1, lambda peer, k: p_src.at[peer], lambda peer, k: p_rcv.at[k - 1])

    triangle_arrived(0)
    lower_rows = l_buf[...].reshape(rb, l_buf.shape[2])
    y_root = unfolded_product(lower_rows, root_value(D, d_buf))
    root_gather(E_, e_buf, folded(y_root))

    arrived(P1, p_rcv)
    pz_buf[g] = p_src[i] + jnp.sum(p_rcv[...], axis=0)
    to_column(P2, lambda peer: pz_buf.at[g], pz_buf.at[g])

    loaded("g_blocks", "c_blocks", "block_cols")
    size = g_blocks.shape[1]
    stored = block_cols.shape[1]
    for r in range(2):
        for c in range(2):
            for blocks, whole in ((g_blocks, hg), (c_blocks, hc)):
                total = jnp.zeros((size, size), F32)
                for w in range(stored):
                    at = (r * stored + w) * size
                    weight = (block_cols[r : r + 1, w : w + 1] == c).astype(F32)
                    total = total + weight * blocks[at : at + size, :]
                whole[r * size : (r + 1) * size, c * size : (c + 1) * size] = total

    arrived(N3, m_rcv.at[others_z])
    m_buf[g] = jnp.sum(m_rcv[...], axis=0) - q_all[leaf_count + 8 : leaf_count + 16, :]
    to_column(N4, lambda peer: m_buf.at[g], m_buf.at[g])
    arrived(P2, pz_buf.at[others_z])
    proj_start = jnp.sum(pz_buf[...], axis=0)

    triangle_arrived(1)
    upper_rows = u_buf[...].reshape(rb, u_buf.shape[2])
    x_root = unfolded_product(upper_rows, root_value(E_, e_buf))

    sep_part = wide(mul(sep_by_root, x_root)).reshape(n_inner, 8, 128)
    arrived(N4, m_buf.at[others_z])
    proj_t = mul(x_root, m_buf[...].reshape(rb, m_buf.shape[2]), TN)
    w_src[:, 0] = sep_part
    for t in range(PIECES_P):
        r, c = t // 4, t % 4
        w_src[t // per, 1 + t % per] = proj_t[8 * r : 8 * r + 8, 128 * c : 128 * c + 128]
    to_plane(W1, lambda peer, k: w_src.at[peer], lambda peer, k: w_rcv.at[k - 1])
    row_ids = lax.broadcasted_iota(jnp.int32, (8, rb), 0)
    col_ids = lax.broadcasted_iota(jnp.int32, (8, rb), 1)
    pick = (col_ids == row_ids + 8 * g).astype(F32)
    x_root_t = mul(x_root, pick, ((0,), (1,)))
    arrived(W1, w_rcv)
    moved = w_src[i] + jnp.sum(w_rcv[...], axis=0)
    w_buf[i, 0] = wide(y_own) - moved[0]
    w_buf[i, pl.ds(1, per)] = (proj_start - moved[1:]) / nodes
    to_plane(W2, lambda peer, k: w_buf.at[i], lambda peer, k: w_buf.at[i])
    arrived(W2, w_buf.at[others])

    z_t = jnp.transpose(w_buf[:, 0].reshape(width, 128))[:64]
    x_leaf_t = uy_t - mul(z_t, from_sep, NT)
    x_sep_t = mul(z_t, su_buf[chip, core], NT)
    x_t = jnp.concatenate([x_leaf_t, x_sep_t, x_root_t], axis=1)
    coefs = jnp.concatenate(
        [
            jnp.concatenate(
                [w_buf[(4 * r + c) // per, 1 + (4 * r + c) % per] for c in range(4)], axis=1
            )
            for r in range(8)
        ],
        axis=0,
    )
    clean_t = x_t - mul(coefs, q_all[...], NT)

    per_k = PIECES_K // n_own
    half = n_own // 2
    owner = i // stride
    owns = lax.rem(i, stride) == 0
    owns_gram = jnp.logical_and(owns, owner >= half)
    owns_rest = jnp.logical_and(owns, owner < half)

    def to_owners(first):
        def one(n, carry):
            at = first + n
            peer = at * stride

            @pl.when(peer != i)
            def _():
                pltpu.make_async_remote_copy(
                    src_ref=k_src.at[at],
                    dst_ref=k_rcv.at[lax.rem(peer + n_inner - i, n_inner) - 1],
                    send_sem=send.at[KR],
                    recv_sem=recv.at[KR],
                    device_id=(g, peer),
                    device_id_type=MESH,
                ).start()

            return carry

        lax.fori_loop(0, half, one, 0)

    k_src[half:] = wide(mul(clean_t, clean_t, NT)).reshape(half, per_k, 8, 128)
    to_owners(half)
    clean_leaf_t = clean_t[:, :leaf_count]
    coef_t[...] = coefs
    g_part = mul(mul(clean_leaf_t, hg[...]), clean_leaf_t, NT)
    c_part = mul(mul(clean_leaf_t, hc[...]), clean_leaf_t, NT)
    k_src[:half] = jnp.concatenate([g_part, c_part], axis=1).reshape(half, per_k, 8, 128)
    to_owners(0)

    @pl.when(owns)
    def _():
        arrived(KR, k_rcv)
        kz_buf[g] = k_src[owner] + jnp.sum(k_rcv[...], axis=0)
        to_column(KZ, lambda peer: kz_buf.at[g], kz_buf.at[g])
        arrived(KZ, kz_buf.at[others_z])
        kc_buf[owner] = jnp.sum(kz_buf[...], axis=0) / nodes

    @pl.when(owns_gram)
    def _():
        to_plane(KG, lambda peer, k: kc_buf.at[owner], lambda peer, k: kc_buf.at[owner])
        arrived(KG, kc_buf.at[pl.ds(0, half - 1)])

    @pl.when(owns_rest)
    def _():
        to_plane(KC, lambda peer, k: kc_buf.at[owner], lambda peer, k: kc_buf.at[owner])

    @pl.when(jnp.logical_not(owns_gram))
    def _():
        arrived(KG, kc_buf.at[pl.ds(0, half)])

    inverse = inverse_factor(kc_buf[half:].reshape(64, 128)[:, :64])
    v_t = mul(inverse, clean_t)
    v_leaf_t[...] = v_t[:, :leaf_count]
    ends = jnp.concatenate([v_t[:, leaf_count:], jnp.zeros((64, 112), F32)], axis=1)
    ends = jnp.transpose(ends)
    v_sep[...] = ends[0:8]
    v_root[...] = ends[8:16]

    @pl.when(owns_rest)
    def _():
        arrived(KC, kc_buf.at[pl.ds(0, half - 1)])

    @pl.when(jnp.logical_not(owns_rest))
    def _():
        arrived(KC, kc_buf.at[pl.ds(0, half)])

    both = mul(inverse, kc_buf[:half].reshape(64, 128))
    red_g[...] = mul(both[:, :64], inverse, NT)
    red_c[...] = mul(both[:, 64:], inverse, NT)

    sent(A, a_rcv)
    sent(B, b_buf.at[others])
    sent(SL, sl_buf.at[others_p, 0])
    sent(SU, su_buf.at[others_p, 0])
    sent(SLB, sl_buf.at[:, 0])
    sent(SUB, su_buf.at[:, 0])
    sent(SP, sp_buf.at[others])
    sent(SS, ss_buf.at[others])
    triangle_sent(0)
    triangle_sent(1)
    sent(RZ, rz_buf.at[others_z])
    sent(D, d_buf.at[:, others])
    sent(E_, e_buf.at[:, others])
    sent(N1A, n_sib)
    sent(N1, n_rcv)
    sent(N2, n_buf.at[others_p, 0])
    sent(N2B, n_buf.at[:, 0])
    sent(N3, m_src.at[others_z])
    sent(N4, m_buf.at[others_z])
    sent(P1, p_rcv)
    sent(P2, pz_buf.at[others_z])
    sent(W1, w_rcv)
    sent(W2, w_buf.at[others])

    @pl.when(owns)
    def _():
        sent(KR, k_src.at[pl.ds(0, n_own - 1)])
        sent(KZ, kz_buf.at[others_z])

    @pl.when(jnp.logical_not(owns))
    def _():
        sent(KR, k_src)

    @pl.when(owns_gram)
    def _():
        sent(KG, k_rcv)

    @pl.when(owns_rest)
    def _():
        sent(KC, k_rcv)


def hand_over(count, *refs):
    done = refs[-1]
    copies = [
        pltpu.make_async_copy(refs[n], refs[count + n], done.at[n]) for n in range(count)
    ]
    for copy in copies:
        copy.start()
    for copy in copies:
        copy.wait()


def shards(
    n_outer,
    n_inner,
    b_leaf,
    b_sep,
    b_root,
    leaf_linv,
    leaf_uinv,
    leaf_lower,
    leaf_upper,
    sep_rows,
    sep_linv,
    sep_uinv,
    sep_lower,
    sep_upper,
    root_linv,
    root_uinv,
    basis_leaf,
    basis_sep,
    basis_root,
    g_blocks,
    c_blocks,
    block_cols,
):
    nodes, ports = b_leaf.shape
    basis = basis_leaf.shape[1]
    root = root_linv.shape[1]
    width = n_inner * 8
    half = n_outer // 2
    per = PIECES_P // n_inner
    n_own = min(PIECES_K, n_inner)
    per_k = PIECES_K // n_own
    hbm = pl.BlockSpec(memory_space=pltpu.HBM)
    scratch = [
        (n_inner, 8, 128),
        (n_inner - 1, 8, 128),
        (n_inner, 8, 128),
        (n_inner // 2, 2, 8, width),
        (n_inner // 2, 2, 8, width),
        (n_inner, 8, 128),
        (n_inner, 8, 128),
        (n_inner, 8, 128),
        (n_inner, 8, 128),
        (n_outer, 8, root),
        (n_outer, 8, root),
        (n_outer, n_outer * 4, 128),
        (half, n_inner, 8, 128),
        (half, n_inner, 8, 128),
        (n_inner // 2, 2, 8, basis),
        (n_inner // 2, 8, basis),
        (n_inner // 2, 8, basis),
        (n_inner // 2 - 1, 8, basis),
        (n_inner // 2, 2, 8, basis),
        (n_outer, 8, basis),
        (n_outer, 8, basis),
        (n_outer, 8, basis),
        (n_inner, per, 8, 128),
        (n_inner - 1, per, 8, 128),
        (n_outer, per, 8, 128),
        (n_inner, 1 + per, 8, 128),
        (n_inner - 1, 1 + per, 8, 128),
        (n_inner, 1 + per, 8, 128),
        (n_own, per_k, 8, 128),
        (n_inner - 1, per_k, 8, 128),
        (n_outer, per_k, 8, 128),
        (n_own, per_k, 8, 128),
        (nodes + 16, basis),
        (nodes, nodes),
        (nodes, nodes),
    ]
    b_leaf_t, sep_lower_t = b_leaf.T, sep_lower.T
    kept = (
        b_leaf_t,
        b_sep,
        b_root,
        leaf_linv,
        leaf_uinv,
        leaf_lower,
        leaf_upper,
        sep_rows,
        sep_lower_t,
        sep_upper,
        g_blocks,
        c_blocks,
        block_cols,
    )
    outs = [(ports, nodes), (8, ports), (8, ports), (ports, basis), (ports, ports), (ports, ports)]
    vmem = pl.BlockSpec(memory_space=pltpu.VMEM)
    results = pl.pallas_call(
        functools.partial(kernel, n_outer, n_inner),
        out_shape=[pltpu.VMEM(s, F32) for s in outs],
        in_specs=[hbm] * 20,
        out_specs=[vmem] * 6,
        scratch_shapes=[pltpu.VMEM(s, F32) for s in scratch]
        + [pltpu.VMEM(x.shape, x.dtype) for x in kept]
        + [pltpu.SemaphoreType.DMA((n,)) for n in (27, 27, 20)]
        + [pltpu.SemaphoreType.DMA((2, n_outer))] * 2,
        compiler_params=pltpu.CompilerParams(
            collective_id=0, has_side_effects=True, vmem_limit_bytes=58 * 2**20
        ),
    )(*(pltpu.with_memory_space_constraint(x, pltpu.HBM) for x in (
        b_leaf_t,
        b_sep,
        b_root,
        leaf_linv,
        leaf_uinv,
        leaf_lower,
        leaf_upper,
        sep_rows,
        sep_linv,
        sep_uinv,
        sep_lower_t,
        sep_upper,
        root_linv,
        root_uinv,
        basis_leaf,
        basis_sep,
        basis_root,
        g_blocks,
        c_blocks,
        block_cols,
    )))
    v_leaf_t, v_sep, v_root, coef_t, red_g, red_c = pl.pallas_call(
        functools.partial(hand_over, len(outs)),
        out_shape=[jax.ShapeDtypeStruct(s, F32) for s in outs],
        in_specs=[vmem] * 6,
        out_specs=[hbm] * 6,
        scratch_shapes=[pltpu.SemaphoreType.DMA((6,))],
        compiler_params=pltpu.CompilerParams(vmem_limit_bytes=8 * 2**20),
    )(*results)
    return v_leaf_t.T, v_sep, v_root, coef_t.T, red_g, red_c


def solution(mesh):
    rows = P(("outer", "inner"), None)
    return jax.shard_map(
        functools.partial(shards, mesh.shape["outer"], mesh.shape["inner"]),
        mesh=mesh,
        in_specs=(rows,) * 10 + (P(None, ("outer", "inner")),) + (rows,) * 9,
        out_specs=(rows, rows, rows, P(), P(), P()),
        check_vma=False,
    )
```
